256 devices in a mesh: row: 8 (over y_hi, x), col: 32 (over y_lo, z, core).
Axes of the slice: x: 4, y: 4 (y_hi: 2, y_lo: 2; y = y_hi * 2 + y_lo), z: 8, core: 2. Of those that a mesh axis runs over, the one named last changes fastest.
Arguments:
- pair_codes: bfloat16 [24, 4096, 128], P('row', 'col'), may hold values from -448 to 448
- exponents: int32 [24, 32], P('row', 'col'), may hold values from -8 to -5
- token_length: int32 [1], replicated, may hold values from 2048 to 4096
- norm_gain: float32 [128], replicated, may hold values from 0.5 to 1.5
- proj_weight: bfloat16 [128, 512], replicated, may hold values from -0.5 to 0.5
- out_weight: bfloat16 [128, 128], replicated, may hold values from -2 to 2
- pair_bias: bfloat16 [4, 4096, 4096], P(None, 'col', 'row'), may hold values from -320 to 320
- update_grad: bfloat16 [24, 4096, 128], P('row', 'col'), may hold values from -6 to 6
Outputs:
- update: bfloat16 [24, 4096, 128], P('row', 'col')
- pair_grad: bfloat16 [24, 4096, 128], P('row', 'col')
- bias_grad: bfloat16 [4, 4096, 4096], P(None, 'col', 'row')
The draws below stay inside these ranges and needn't reach their ends.
All inputs are finite; a program needn't handle non-finite values.
Results may differ from the reference program's by a relative error of at most 0.029.
Values may be sent and summed in bfloat16 or wider, within the bound.
A program may use at most 128 MiB of HBM per device.

```python
import math
import jax
import jax.numpy as jnp
from jax import lax

C = 128
H = 4
DH = 32
CB = 128
N = 4096
ROWS = 24


def draw_pair_bias(key, part):
    key = jax.random.fold_in(key, 11)
    keys_list = jax.random.split(key, 2)
    row_scale = jnp.exp(jax.random.uniform(keys_list[0], (H, N, 1), jnp.float32, 0.0, math.log(4.0)))
    base = jax.random.normal(keys_list[1], (H, N, N), jnp.float32) * row_scale
    base = jnp.clip(base, -320.0, 320.0)
    return base.astype(jnp.bfloat16)


def place_ends(result, stream_key, least, high):
    index_at = [jax.random.randint(jax.random.fold_in(stream_key, axis), (), 0, length) for axis, length in enumerate(result.shape)]
    main_axis = result.shape.index(max(result.shape))
    beside = index_at[:main_axis] + [(index_at[main_axis] + 1) % result.shape[main_axis]] + index_at[main_axis + 1:]
    return result.at[tuple(index_at)].set(least).at[tuple(beside)].set(high)


def block_scale(stream_key, dims, cuts, low, high):
    loudness = 1.0
    for dim, blocks in cuts:
        heights = jax.random.uniform(jax.random.fold_in(jax.random.fold_in(stream_key, 6), dim), (blocks,), jnp.float32, low / len(cuts), high / len(cuts))
        loudness = loudness * jnp.repeat(jnp.exp(heights), dims[dim] // blocks).reshape((-1,) + (1,) * (len(dims) - 1 - dim))
    return loudness


def noise(stream_key, dims, spread, bound, cuts=(), kind=jnp.bfloat16):
    factor_of = block_scale(stream_key, dims, cuts, -0.22, 0.18) if cuts else 1.0
    drawn = jax.random.normal(stream_key, dims, jnp.float32) * spread * factor_of
    return jnp.minimum(jnp.maximum(drawn, -bound), bound).astype(kind)


def setup_inputs(seed: int = 0) -> dict:
    seeds = jax.random.split(jax.random.key(seed), 9)
    pair_codes = noise(seeds[0], (ROWS, N, C), 64.0, 448.0, ((0, 8), (1, 32)))
    exponents = place_ends(jax.random.randint(seeds[1], (ROWS, N // CB), -8, -4), jax.random.fold_in(seeds[1], 1), -8, (-4) - 1).astype(jnp.int32)
    token_length = jax.random.randint(seeds[2], (1,), N // 2, N + 1).astype(jnp.int32)
    norm_gain = jnp.clip(1.0 + 0.1 * jax.random.normal(seeds[3], (C,), jnp.float32), 0.5, 1.5)
    proj_weight = noise(seeds[4], (C, 4 * H * DH), C ** -0.5, 0.5)
    out_weight = noise(seeds[5], (H * DH, C), (H * DH // 16) ** -0.5, 2.0)
    pair_bias = draw_pair_bias(jax.random.fold_in(seeds[8], 71), 0)
    update_grad = noise(seeds[7], (ROWS, N, C), 1.0, 6.0, ((0, 8), (1, 32)))
    return {"pair_codes": pair_codes, "exponents": exponents, "token_length": token_length, "norm_gain": norm_gain, "proj_weight": proj_weight, "out_weight": out_weight, "pair_bias": pair_bias, "update_grad": update_grad}


MASKED = -1e+30
EPSILON = 1e-05

def reference(pair_codes, exponents, token_length, norm_gain, proj_weight, out_weight, pair_bias, update_grad):
    inner = H * DH
    qscale = DH ** (-0.5)
    tile_scale = jnp.repeat(jnp.exp2(exponents.astype(jnp.float32)), CB, axis=1)
    pair_values = pair_codes.astype(jnp.float32) * tile_scale[:, :, None]
    average = lax.optimization_barrier(jnp.mean(pair_values, axis=-1, keepdims=True))
    centered = pair_values - average
    variance = lax.optimization_barrier(jnp.mean(centered * centered, axis=-1, keepdims=True))
    inv_std = lax.rsqrt(variance + EPSILON)
    unit_pair = centered * inv_std
    normed = (unit_pair * norm_gain).astype(jnp.bfloat16)
    projected = jnp.dot(normed.reshape(ROWS * N, C), proj_weight, preferred_element_type=jnp.float32).reshape(ROWS, N, 4 * inner)
    queries = (projected[..., :inner] * qscale).astype(jnp.bfloat16)
    keys_all = projected[..., inner:2 * inner].astype(jnp.bfloat16)
    values_all = projected[..., 2 * inner:3 * inner].astype(jnp.bfloat16)
    gates = jax.nn.sigmoid(projected[..., 3 * inner:])
    valid = jnp.arange(N, dtype=jnp.int32) < token_length[0]
    bias_full = pair_bias.astype(jnp.float32)
    weight_f = proj_weight.astype(jnp.float32)
    highest = lax.Precision.HIGHEST

    def one_row(bias_sum, row_items):
        query_row, key_row, value_row, gate_row, grad_row = row_items
        query_heads = query_row.astype(jnp.float32).reshape(N, H, DH)
        key_heads = key_row.astype(jnp.float32).reshape(N, H, DH)
        value_heads = value_row.astype(jnp.float32).reshape(N, H, DH)
        scores = jnp.einsum('jhd,khd->hjk', query_heads, key_heads) + bias_full
        scores = jnp.where(valid[None, None, :], scores, MASKED)
        probs = jax.nn.softmax(scores, axis=-1)
        probs_b = probs.astype(jnp.bfloat16).astype(jnp.float32)
        attended = jnp.einsum('hjk,khd->jhd', probs_b, value_heads).reshape(N, inner)
        gated = (gate_row * attended).astype(jnp.bfloat16)
        update_row = jnp.dot(gated, out_weight, preferred_element_type=jnp.float32).astype(jnp.bfloat16)
        d_gated = jnp.dot(grad_row, out_weight.T, preferred_element_type=jnp.float32)
        d_gate_pre = d_gated * attended * gate_row * (1.0 - gate_row)
        d_attended = (d_gated * gate_row).astype(jnp.bfloat16).astype(jnp.float32)
        delta = lax.optimization_barrier(jnp.sum((d_attended * attended).reshape(N, H, DH), axis=-1))
        d_heads = d_attended.reshape(N, H, DH)
        d_probs = jnp.einsum('jhd,khd->hjk', d_heads, value_heads)
        d_scores = probs * (d_probs - jnp.transpose(delta)[:, :, None])
        d_scores_b = d_scores.astype(jnp.bfloat16).astype(jnp.float32)
        d_queries = jnp.einsum('hjk,khd->jhd', d_scores_b, key_heads).reshape(N, inner) * qscale
        d_keys = jnp.einsum('hjk,jhd->khd', d_scores_b, query_heads).reshape(N, inner)
        d_values = jnp.einsum('hjk,jhd->khd', probs_b, d_heads).reshape(N, inner)
        d_normed = jnp.dot(d_queries, weight_f[:, :inner].T, precision=highest)
        d_normed = d_normed + jnp.dot(d_keys, weight_f[:, inner:2 * inner].T, precision=highest)
        d_normed = d_normed + jnp.dot(d_values, weight_f[:, 2 * inner:3 * inner].T, precision=highest)
        d_normed = d_normed + jnp.dot(d_gate_pre, weight_f[:, 3 * inner:].T, precision=highest)
        return (bias_sum + d_scores, (update_row, d_normed))
    bias_start = jnp.zeros((H, N, N), jnp.float32)
    bias_sum, outputs = lax.scan(one_row, bias_start, (queries, keys_all, values_all, gates, update_grad))
    update, d_normed = outputs
    scaled = d_normed * norm_gain
    pair_grad = inv_std * (scaled - lax.optimization_barrier(jnp.mean(scaled, axis=-1, keepdims=True)) - unit_pair * lax.optimization_barrier(jnp.mean(scaled * unit_pair, axis=-1, keepdims=True)))
    return (update, pair_grad.astype(jnp.bfloat16), bias_sum.astype(jnp.bfloat16))
```

```python
import functools

import jax
import jax.numpy as jnp
from jax import lax
from jax.experimental import pallas as pl
from jax.experimental.pallas import tpu as pltpu
from jax.sharding import PartitionSpec as P

MASKED = -1e30
EPSILON = 1e-05
F32 = jnp.float32
BF = jnp.bfloat16
NX, NZ = 4, 8
HEADS, DH, C, T = 4, 32, 128, 128
KB = 512
ROWS = 3


def nn(a, b):
    return lax.dot_general(a, b, (((1,), (0,)), ((), ())), preferred_element_type=F32)


def nt(a, b):
    return lax.dot_general(a, b, (((1,), (1,)), ((), ())), preferred_element_type=F32)


def split_nn(w, a):
    high = a.astype(BF)
    low = (a - high.astype(F32)).astype(BF)
    return nn(w, high) + nn(w, low)


def per_head(stat):
    return jnp.concatenate(
        [jnp.broadcast_to(stat[h : h + 1, :], (DH, T)) for h in range(HEADS)], axis=0
    )


def kernel(
    tok, codes, expo, gain, w, wo, bias, ug,
    update, pair_grad, bias_grad,
    wt, wot, nb, unit, inv, gates, dgated, kn, qt, dot, bias_g, bias_t, probs, s_ref, qbd, dos,
    m_st, l_st, a_st, vals, keys_t, gk, att_loc, st_loc, att_tx, att_rx, st_rx, back_tx, back_rx, stats, dgp,
    ds_ref, acc, dq, kt, rxc, ytx, rxy, rsum, ztx, zrx, ftx, frx, dqtx, dqrx, gtx, grx,
    bx_s, bx_r, ks_s, ks_r, zr_s, zr_r, sb_s, sb_r, pq_s, pq_r, ex_s, ex_r, kc_s, kc_r,
    ky_s, ky_r, zq_s, zq_r, f_s, f_r, g_s, g_r,
):
    row_id = lax.axis_index("row")
    col_id = lax.axis_index("col")
    yh, x = row_id // NX, lax.rem(row_id, NX)
    yl, z, c = col_id // 16, lax.rem(col_id, 16) // 2, lax.rem(col_id, 2)
    xs = [lax.rem(x + i, NX) for i in range(NX)]
    zs = [lax.rem(z + i, NZ) for i in range(NZ)]

    def dev(x_=x, yh_=yh, yl_=yl, z_=z, c_=c):
        return (yh_ * NX + x_, yl_ * 16 + z_ * 2 + c_)

    def rc(src, dst, send, recv, to):
        return pltpu.make_async_remote_copy(
            src_ref=src, dst_ref=dst, send_sem=send, recv_sem=recv,
            device_id=to, device_id_type=pl.DeviceIdType.MESH,
        )

    xp, xm, zp, zm = dev(x_=xs[1]), dev(x_=xs[3]), dev(z_=zs[1]), dev(z_=zs[7])
    sib = dev(c_=1 - c)
    ypart = dev(yl_=1 - yl)
    hpart = dev(yh_=1 - yh)
    cross = dev(yh_=1 - yh, yl_=1 - yl)
    swap = dev(yh_=yl, yl_=yh)
    is_home = yh == yl

    barrier = pltpu.get_barrier_semaphore()
    for to in (xp, xm, zp, zm, sib, ypart, hpart, cross):
        pl.semaphore_signal(barrier, inc=1, device_id=to, device_id_type=pl.DeviceIdType.MESH)
    pl.semaphore_wait(barrier, 8)

    bias_p = rc(bias, bias_g.at[0], bx_s.at[0], bx_r.at[0], xp)
    bias_m = rc(bias, bias_g.at[1], bx_s.at[1], bx_r.at[1], xm)
    bias_fp = rc(bias_g.at[0, pl.ds(0, 2)], bias_g.at[2, pl.ds(0, 2)], bx_s.at[2], bx_r.at[2], xp)
    bias_fm = rc(bias_g.at[1, pl.ds(2, 2)], bias_g.at[2, pl.ds(2, 2)], bx_s.at[3], bx_r.at[3], xm)
    bias_p.start()
    bias_m.start()

    gain_row = gain[...]
    for r in range(ROWS):
        scale = jnp.exp2(expo[r : r + 1, 0:1].astype(F32))
        value = codes[r].astype(F32) * scale
        mean = jnp.mean(value, axis=-1, keepdims=True)
        centered = value - mean
        var = jnp.mean(centered * centered, axis=-1, keepdims=True)
        inv_std = lax.rsqrt(var + EPSILON)
        unit_pair = centered * inv_std
        unit[r] = unit_pair
        inv[r] = jnp.broadcast_to(inv_std, (T, C))
        nb[r] = (unit_pair * gain_row).astype(BF)

    def key_at(zz, cc):
        return pl.ds(pl.multiple_of(zz * 256 + cc * 128, 128), 128)

    my_set = pl.ds(pl.multiple_of(yh * ROWS, ROWS), ROWS)
    key_send = [
        rc(nb, kn.at[pl.ds(yh * ROWS, ROWS), key_at(z, c)], ks_s.at[t], ks_r.at[yh], dev(yh_=yl, yl_=t))
        for t in range(2)
    ]
    for t in range(2):
        @pl.when(jnp.logical_not(jnp.logical_and(is_home, yl == t)))
        def _():
            key_send[t].start()

    @pl.when(is_home)
    def _():
        kn[pl.ds(yh * ROWS, ROWS), key_at(z, c), :] = nb[...]

    for q in range(4):
        wt[q * 128 : (q + 1) * 128, :] = w[:, q * 128 : (q + 1) * 128].astype(F32).T.astype(BF)
    wot[...] = wo[...].astype(F32).T.astype(BF)

    def set_of(ref, s):
        return ref.at[pl.ds(s * ROWS, ROWS)]

    for r in range(ROWS):
        n = nb[r]
        qt[yh * ROWS + r] = (nt(wt[0:128, :], n) * (DH ** -0.5)).astype(BF)
        gate = jax.nn.sigmoid(nt(wt[384:512, :], n))
        gates[r] = gate
        dg = nt(wo[...], ug[r])
        dgated[r] = dg
        dot[yh * ROWS + r] = (dg * gate).astype(BF)
    q_send = rc(set_of(qt, yh), set_of(qt, yh), pq_s.at[0], pq_r.at[0], hpart)
    d_send = rc(set_of(dot, yh), set_of(dot, yh), pq_s.at[1], pq_r.at[1], hpart)
    q_send.start()
    d_send.start()

    live = tok[0]

    def prep(src, xb):
        for k in range(4):
            first = (yh * NX + xb) * KB + k * 128
            valid = first + lax.broadcasted_iota(jnp.int32, (128, 128), 0) < live
            for h in range(HEADS):
                tile = src[h, :, k * 128 : (k + 1) * 128].astype(F32).T
                bias_t[xb, k * 128 : (k + 1) * 128, h * 128 : (h + 1) * 128] = jnp.where(valid, tile, MASKED)

    qbd[...] = jnp.zeros_like(qbd)
    dos[...] = jnp.zeros_like(dos)
    prep(bias, x)

    for s in range(2):
        @pl.when(jnp.logical_not(jnp.logical_and(is_home, yh == s)))
        def _():
            rc(nb, kn.at[pl.ds(s * ROWS, ROWS), key_at(z, c)], ks_s.at[0], ks_r.at[s], sib).wait_recv()

    def block(zz, cc=c):
        return kn.at[:, key_at(zz, cc)]

    def half(zz, s):
        return kn.at[pl.ds(s * ROWS, ROWS), key_at(zz, c)]

    def up(i):
        src = block(zs[(8 - i) % 8]) if i < 3 else half(zs[5], 0)
        return rc(src, src, zr_s.at[0, i], zr_r.at[0, i], zp)

    def down(i):
        src = block(zs[i]) if i < 3 else half(zs[3], 1)
        return rc(src, src, zr_s.at[1, i], zr_r.at[1, i], zm)

    def to_sib(i):
        return rc(block(zs[i]), block(zs[i]), sb_s.at[i], sb_r.at[i], sib)

    def from_sib(i):
        return rc(block(zs[i], 1 - c), block(zs[i], 1 - c), sb_s.at[i], sb_r.at[i], sib)

    def up_in(i):
        dst = block(zs[7 - i]) if i < 3 else half(zs[4], 0)
        return rc(dst, dst, zr_s.at[0, i], zr_r.at[0, i], zp)

    def down_in(i):
        dst = block(zs[i + 1]) if i < 3 else half(zs[4], 1)
        return rc(dst, dst, zr_s.at[1, i], zr_r.at[1, i], zm)

    def ring_step(i):
        up_in(i).wait_recv()
        if i < 3:
            up(i + 1).start()
            to_sib(7 - i).start()
        down_in(i).wait_recv()
        if i < 3:
            down(i + 1).start()
            to_sib(i + 1).start()
        else:
            to_sib(4).start()

    up(0).start()
    down(0).start()
    to_sib(0).start()
    bias_p.wait_recv()
    bias_fp.start()
    bias_m.wait_recv()
    bias_fm.start()
    prep(bias_g.at[0], xs[3])
    prep(bias_g.at[1], xs[1])
    ring_step(0)
    rc(set_of(qt, yh), set_of(qt, 1 - yh), pq_s.at[0], pq_r.at[0], hpart).wait_recv()

    zb = z // 2
    even = lax.rem(z, 2) == 0
    near = jnp.where(even, zb + 3, zb + 1)
    far = jnp.where(even, zb + 1, zb + 3)

    def arrive(phase):
        for i in ((0, 1, 7), (2, 6), (3, 5), (4,))[phase]:
            from_sib(i).wait_recv()

    ones = jnp.ones((16, KB), BF)

    def load_q(row):
        for h in range(HEADS):
            qbd[h * 32 : (h + 1) * 32, h * 128 : (h + 1) * 128] = qt[row, h * 32 : (h + 1) * 32, :]

    att_copy = rc(att_tx, att_rx, ex_s.at[0], ex_r.at[0], hpart)
    st_copy = rc(set_of(st_loc, 1 - yh), st_rx, ex_s.at[1], ex_r.at[1], hpart)
    back_copy = rc(back_tx, back_rx, ex_s.at[2], ex_r.at[2], hpart)

    def combine(row):
        m_all = [m_st[row * 4 + i] for i in range(4)]
        top_m = jnp.maximum(jnp.maximum(m_all[0], m_all[1]), jnp.maximum(m_all[2], m_all[3]))
        total = jnp.zeros((HEADS, T), F32)
        weighted = jnp.zeros((C, T), F32)
        for i in range(4):
            f = jnp.exp(m_all[i] - top_m)
            total = total + f * l_st[row * 4 + i]
            weighted = weighted + per_head(f) * a_st[row * 4 + i]
        st_loc[row, 0:4, :] = top_m
        st_loc[row, 4:8, :] = total
        return weighted

    def forward(u, carry):
        phase, t = u // 6, lax.rem(u, 6)
        row = lax.rem((1 - yh) * ROWS + t, 2 * ROWS)
        xb = lax.rem(
            jnp.where(phase == 0, zb, jnp.where(phase == 1, near, jnp.where(phase == 2, far, zb + 2))), NX
        )
        slot = row * 4 + xb

        for i in range(4):
            @pl.when(u == 6 * i)
            def _():
                arrive(i)

        @pl.when(jnp.logical_and(t == 0, xb == xs[2]))
        def _():
            bias_fp.wait_recv()
            bias_fm.wait_recv()
            prep(bias_g.at[2], xs[2])

        for i in range(1, 4):
            @pl.when(u == 6 * i - 3)
            def _():
                ring_step(i)

        load_q(row)

        @pl.when(u < 6)
        def _():
            gk[row] = nn(w[:, 128:256], qbd[...]).astype(BF)

        n = kn[row, pl.ds(pl.multiple_of(xb * KB, KB), KB), :]
        kv = nn(n, w[:, 128:384]).astype(BF)
        kvt = nt(wt[128:384, :], n).astype(BF)
        k = kv[:, 0:128]
        vals[slot] = kv[:, 128:256]
        keys_t[slot] = kvt[0:128, :]
        vt = kvt[128:256, :]
        for hp in range(2):
            cols = slice(hp * 256, hp * 256 + 256)
            q2 = qbd[:, cols]
            top = None
            for i in range(4):
                rows = slice(i * 128, (i + 1) * 128)
                s = nn(k[rows, :], q2) + bias_t[xb, rows, cols]
                s_ref[rows, cols] = s
                part = jnp.max(s.reshape(16, 8, 256), axis=0)
                top = part if top is None else jnp.maximum(top, part)
            m = jnp.max(top, axis=0, keepdims=True)
            for i in range(4):
                rows = slice(i * 128, (i + 1) * 128)
                probs[slot, rows, cols] = jnp.exp(s_ref[rows, cols] - m).astype(BF)
            a = nn(jnp.concatenate([vt[hp * 64 : hp * 64 + 64, :], ones], axis=0), probs[slot, :, cols])
            for j in range(2):
                h = hp * 2 + j
                lanes = slice(j * 128, (j + 1) * 128)
                m_st[slot, h : h + 1, :] = m[:, lanes]
                l_st[slot, h : h + 1, :] = a[64:65, lanes]
                a_st[slot, h * 32 : (h + 1) * 32, :] = a[j * 32 : (j + 1) * 32, lanes]

        @pl.when(u == 20)
        def _():
            for r in range(ROWS):
                att_tx[r] = combine((1 - yh) * ROWS + r).astype(BF)
            att_copy.start()
            st_copy.start()

        return carry

    lax.fori_loop(0, 24, forward, 0)

    for r in range(ROWS):
        att_loc[yh * ROWS + r] = combine(yh * ROWS + r)
    att_copy.wait_recv()
    st_copy.wait_recv()
    for r in range(ROWS):
        mine = yh * ROWS + r
        ma, la = st_loc[mine, 0:4, :], st_loc[mine, 4:8, :]
        mb, lb = st_rx[r, 0:4, :], st_rx[r, 4:8, :]
        top_m = jnp.maximum(ma, mb)
        fa, fb = jnp.exp(ma - top_m), jnp.exp(mb - top_m)
        total = fa * la + fb * lb
        attended = (per_head(fa) * att_loc[mine] + per_head(fb) * att_rx[r].astype(F32)) / per_head(total)
        gate = gates[r]
        product = dot[mine].astype(F32) * attended
        lse = top_m + jnp.log(total)
        stats[mine, 0:4, :] = lse
        back_tx[r, 0:4, :] = lse
        for h in range(HEADS):
            delta = jnp.sum(product[h * 32 : (h + 1) * 32, :], axis=0, keepdims=True)
            stats[mine, 4 + h : 5 + h, :] = delta
            back_tx[r, 4 + h : 5 + h, :] = delta
        att_loc[mine] = attended
    back_copy.start()
    for r in range(ROWS):
        attended = att_loc[yh * ROWS + r]
        gate = gates[r]
        dgp[r] = dgated[r] * attended * gate * (1.0 - gate)
        update[r] = nn(wot[...], (gate * attended).astype(BF)).T.astype(BF)
    rc(set_of(dot, yh), set_of(dot, 1 - yh), pq_s.at[1], pq_r.at[1], hpart).wait_recv()
    dq[...] = jnp.zeros_like(dq)

    order = [xs[2], xs[1], xs[3], xs[0]]

    def core_copy(zz):
        return rc(kt.at[:, key_at(zz, 1 - c)], rxc.at[zz], kc_s.at[zz], kc_r.at[zz], sib)

    def y_copy(zz):
        return rc(ytx.at[zz], rxy.at[zz], ky_s.at[zz], ky_r.at[zz], ypart)

    def core_stage(xb):
        for b in range(2):
            core_copy(xb * 2 + b).start()

    def y_stage(xb):
        for b in range(2):
            zz = xb * 2 + b
            core_copy(zz).wait_recv()
            for r in range(ROWS):
                theirs, ours = (1 - yl) * ROWS + r, yl * ROWS + r
                ytx[zz, r] = (kt[theirs, key_at(zz, c), :].astype(F32) + rxc[zz, theirs].astype(F32)).astype(BF)
                rsum[zz, r] = kt[ours, key_at(zz, c), :].astype(F32) + rxc[zz, ours].astype(F32)
            y_copy(zz).start()

    def sum_stage(xb):
        for b in range(2):
            zz = xb * 2 + b
            y_copy(zz).wait_recv()
            rsum[zz] = rsum[zz] + rxy[zz].astype(F32)

    g_half_p = rc(gtx.at[0, pl.ds(0, 2)], grx.at[0, pl.ds(0, 2)], g_s.at[0], g_r.at[0], xp)
    g_half_m = rc(gtx.at[0, pl.ds(2, 2)], grx.at[0, pl.ds(2, 2)], g_s.at[1], g_r.at[1], xm)
    g_p = rc(gtx.at[1], grx.at[1], g_s.at[2], g_r.at[2], xp)
    g_m = rc(gtx.at[2], grx.at[2], g_s.at[3], g_r.at[3], xm)

    def turned(h, k):
        return acc[k * 128 : (k + 1) * 128, h * 128 : (h + 1) * 128].T

    def bias_stage(step):
        if step == 1:
            g_half_p.wait_recv()
        if step == 2:
            g_half_m.wait_recv()
        if step == 3:
            g_p.wait_recv()
            g_m.wait_recv()
        for h in range(HEADS):
            for k in range(4):
                lanes = slice(k * 128, (k + 1) * 128)
                tile = turned(h, k)
                if (step == 1 and h < 2) or (step == 2 and h >= 2):
                    tile = tile + grx[0, h, :, lanes].astype(F32)
                if step == 3:
                    tile = tile + grx[1, h, :, lanes].astype(F32) + grx[2, h, :, lanes].astype(F32)
                    bias_grad[h, :, lanes] = tile.astype(BF)
                else:
                    gtx[step, h, :, lanes] = tile.astype(BF)
        if step == 0:
            g_half_p.start()
            g_half_m.start()
        if step == 1:
            g_p.start()
        if step == 2:
            g_m.start()

    def backward(u, carry):
        step = u // 6
        xb = lax.rem(x + jnp.where(step == 0, 2, jnp.where(step == 1, 1, jnp.where(step == 2, 3, 0))), NX)
        row = lax.rem(yh * ROWS + lax.rem(u, 6), 2 * ROWS)
        slot = row * 4 + xb

        @pl.when(u == 3)
        def _():
            back_copy.wait_recv()
            for r in range(ROWS):
                stats[(1 - yh) * ROWS + r] = back_rx[r]

        @pl.when(lax.rem(u, 6) == 0)
        def _():
            acc[...] = jnp.zeros_like(acc)

        st = stats[row]
        f = jnp.exp(m_st[slot] - st[0:4, :])
        dls = f * st[4:8, :]
        for h in range(HEADS):
            rows = slice(h * 32, (h + 1) * 32)
            dos[rows, h * 128 : (h + 1) * 128] = (dot[row, rows, :].astype(F32) * f[h : h + 1, :]).astype(BF)
        keys = pl.ds(pl.multiple_of(xb * KB, KB), KB)
        v = vals[slot]
        key_t = keys_t[slot]
        for hp in range(2):
            cols = slice(hp * 256, hp * 256 + 256)
            d2 = dos[:, cols]
            l2 = jnp.concatenate([dls[hp * 2 : hp * 2 + 1, :], dls[hp * 2 + 1 : hp * 2 + 2, :]], axis=1)
            for i in range(4):
                rows = slice(i * 128, (i + 1) * 128)
                d_prob = nn(v[rows, :], d2) - l2
                d_score = probs[slot, rows, cols].astype(F32) * d_prob
                acc[rows, cols] = acc[rows, cols] + d_score
                ds_ref[rows, cols] = d_score.astype(BF)
            d_query = nn(key_t[hp * 64 : hp * 64 + 64, :], ds_ref[:, cols])
            for j in range(2):
                rows = slice((hp * 2 + j) * 32, (hp * 2 + j + 1) * 32)
                dq[row, rows, :] = dq[row, rows, :] + d_query[j * 32 : (j + 1) * 32, j * 128 : (j + 1) * 128]
        gv = nn(w[:, 256:384], dos[...]).astype(BF)
        kt[row, keys, :] = (nt(ds_ref[...], gk[row]) + nt(probs[slot], gv)).astype(BF)

        for s in range(4):
            @pl.when(u == 6 * s + 5)
            def _():
                bias_stage(s) if s < 3 else None
                core_stage(order[s])
                if s >= 1:
                    y_stage(order[s - 1])
                if s >= 2:
                    sum_stage(order[s - 2])

        return carry

    lax.fori_loop(0, 24, backward, 0)

    for r in range(ROWS):
        dqtx[r] = dq[(1 - yh) * ROWS + r].astype(BF)
    dq_copy = rc(dqtx, dqrx, f_s.at[0], f_r.at[0], hpart)
    dq_copy.start()
    y_stage(order[3])
    sum_stage(order[2])
    sum_stage(order[3])

    def z_copy(way, i):
        if i == 0:
            part = pl.ds(way * 64, 64)
            src, dst = ztx.at[way, 0, :, part], zrx.at[way, 0, :, part]
        else:
            src, dst = ztx.at[way, i], zrx.at[way, i]
        return rc(src, dst, zq_s.at[way, i], zq_r.at[way, i], zp if way == 0 else zm)

    for i in range(4):
        for way in range(2):
            home = zs[(4 - i) if way == 0 else (4 + i)]
            if i == 0:
                part = slice(way * 64, way * 64 + 64)
                ztx[way, 0, :, part, :] = rsum[home, :, part, :].astype(BF)
            else:
                z_copy(way, i - 1).wait_recv()
                if i == 1:
                    part = slice(way * 64, way * 64 + 64)
                    other = slice(64 - way * 64, 128 - way * 64)
                    ztx[way, 1, :, part, :] = (
                        rsum[home, :, part, :] + zrx[way, 0, :, part, :].astype(F32)
                    ).astype(BF)
                    ztx[way, 1, :, other, :] = rsum[home, :, other, :].astype(BF)
                else:
                    ztx[way, i] = (rsum[home] + zrx[way, i - 1].astype(F32)).astype(BF)
            z_copy(way, i).start()
    bias_stage(3)
    z_copy(0, 3).wait_recv()
    z_copy(1, 3).wait_recv()
    ftx[...] = (rsum[z] + zrx[0, 3].astype(F32) + zrx[1, 3].astype(F32)).astype(BF)
    final = rc(ftx, frx, f_s.at[1], f_r.at[1], swap)

    @pl.when(jnp.logical_not(is_home))
    def _():
        final.start()

    @pl.when(is_home)
    def _():
        frx[...] = ftx[...]

    dq_copy.wait_recv()
    for r in range(ROWS):
        d_query = (dq[yh * ROWS + r] + dqrx[r].astype(F32)) * (DH ** -0.5)
        unit_t = split_nn(w[:, 0:128], d_query) + split_nn(w[:, 384:512], dgp[r])
        dgated[r] = unit_t.T

    @pl.when(jnp.logical_not(is_home))
    def _():
        final.wait_recv()

    for r in range(ROWS):
        d_normed = dgated[r] + frx[r].astype(F32)
        e = d_normed * gain_row
        up_r = unit[r]
        pair_grad[r] = (
            inv[r]
            * (e - jnp.mean(e, axis=-1, keepdims=True) - up_r * jnp.mean(e * up_r, axis=-1, keepdims=True))
        ).astype(BF)

    for copy in (bias_p, bias_m, bias_fp, bias_fm, q_send, d_send, att_copy, st_copy, back_copy, dq_copy,
                 g_half_p, g_half_m, g_p, g_m):
        copy.wait_send()
    for t in range(2):
        @pl.when(jnp.logical_not(jnp.logical_and(is_home, yl == t)))
        def _():
            key_send[t].wait_send()
    for i in range(4):
        up(i).wait_send()
        down(i).wait_send()
        z_copy(0, i).wait_send()
        z_copy(1, i).wait_send()
    for i in range(8):
        to_sib(i).wait_send()
        core_copy(zs[i]).wait_send()
        y_copy(zs[i]).wait_send()

    @pl.when(jnp.logical_not(is_home))
    def _():
        final.wait_send()


def shards(codes, expo, tok, gain, w, wo, bias, ug):
    vm = pltpu.VMEM
    dma = pltpu.SemaphoreType.DMA
    blk = (ROWS, T, C)
    scratch = [
        vm((512, C), BF), vm((C, C), BF), vm(blk, BF), vm(blk, F32), vm(blk, F32), vm(blk, F32), vm(blk, F32),
        vm((6, 2048, C), BF), vm((6, C, T), BF), vm((6, C, T), BF), vm((3, HEADS, T, KB), BF),
        vm((4, KB, 512), F32), vm((24, KB, 512), BF), vm((KB, 512), F32), vm((C, 512), BF), vm((C, 512), BF),
        vm((24, HEADS, T), F32), vm((24, HEADS, T), F32), vm((24, C, T), F32),
        vm((24, KB, C), BF), vm((24, C, KB), BF), vm((6, C, 512), BF), vm((6, C, T), F32), vm((6, 8, T), F32),
        vm(blk, BF), vm(blk, BF), vm((ROWS, 8, T), F32), vm((ROWS, 8, T), F32), vm((ROWS, 8, T), F32),
        vm((6, 8, T), F32), vm(blk, F32),
        vm((KB, 512), BF), vm((KB, 512), F32), vm((6, C, T), F32), vm((6, 2048, C), BF),
        vm((8, 6, T, C), BF), vm((8, 3, T, C), BF), vm((8, 3, T, C), BF), vm((8, 3, T, C), F32),
        vm((2, 4, 3, T, C), BF), vm((2, 4, 3, T, C), BF), vm(blk, BF), vm(blk, BF), vm(blk, BF), vm(blk, BF),
        vm((3, HEADS, T, KB), BF), vm((3, HEADS, T, KB), BF),
        dma((4,)), dma((4,)), dma((2,)), dma((2,)), dma((2, 4)), dma((2, 4)), dma((8,)), dma((8,)),
        dma((2,)), dma((2,)), dma((3,)), dma((3,)), dma((8,)), dma((8,)), dma((8,)), dma((8,)),
        dma((2, 4)), dma((2, 4)), dma((2,)), dma((2,)), dma((4,)), dma((4,)),
    ]
    v = pl.BlockSpec(memory_space=pltpu.VMEM)
    return pl.pallas_call(
        kernel,
        out_shape=(
            jax.ShapeDtypeStruct(blk, BF),
            jax.ShapeDtypeStruct(blk, BF),
            jax.ShapeDtypeStruct((HEADS, T, KB), BF),
        ),
        in_specs=[pl.BlockSpec(memory_space=pltpu.SMEM)] + [v] * 7,
        out_specs=(v, v, v),
        scratch_shapes=scratch,
        compiler_params=pltpu.CompilerParams(
            collective_id=0, has_side_effects=True, vmem_limit_bytes=58 * 1024 * 1024
        ),
        cost_estimate=pl.CostEstimate(flops=8_000_000_000, bytes_accessed=4_000_000, transcendentals=6_300_000),
    )(tok, codes, expo, gain.reshape(1, C), w, wo, bias, ug)


def solution(mesh):
    in_specs = (
        P("row", "col", None), P("row", "col"), P(), P(), P(), P(), P(None, "col", "row"), P("row", "col", None),
    )
    out_specs = (P("row", "col", None), P("row", "col", None), P(None, "col", "row"))
    return jax.shard_map(shards, mesh=mesh, in_specs=in_specs, out_specs=out_specs, check_vma=False)
```

```python
import jax
import jax.numpy as jnp
from jax import lax
from jax.experimental import pallas as pl
from jax.experimental.pallas import tpu as pltpu
from jax.sharding import PartitionSpec as P

MASKED = -1e30
EPSILON = 1e-05
F32 = jnp.float32
BF = jnp.bfloat16
NX, NZ = 4, 8
HEADS, DH, C, T = 4, 32, 128, 128
KB = 512
ROWS = 3


def nn(a, b):
    return lax.dot_general(a, b, (((1,), (0,)), ((), ())), preferred_element_type=F32)


def nt(a, b):
    return lax.dot_general(a, b, (((1,), (1,)), ((), ())), preferred_element_type=F32)


def split_nn(w, a):
    high = a.astype(BF)
    low = (a - high.astype(F32)).astype(BF)
    return nn(w, high) + nn(w, low)


def per_head(stat):
    return jnp.concatenate(
        [jnp.broadcast_to(stat[h : h + 1, :], (DH, T)) for h in range(HEADS)], axis=0
    )


def normalised(codes, expo, r):
    value = codes[r].astype(F32) * jnp.exp2(expo[0:1, r : r + 1].astype(F32))
    centered = value - jnp.mean(value, axis=-1, keepdims=True)
    inv_std = lax.rsqrt(jnp.mean(centered * centered, axis=-1, keepdims=True) + EPSILON)
    return centered * inv_std, inv_std


def norm_back(codes, expo, gain, d_normed, update_in, bias_in, update, pair_grad, bias_grad):
    update[...] = update_in[...]
    bias_grad[...] = bias_in[...]
    for r in range(ROWS):
        unit, inv_std = normalised(codes, expo, r)
        e = d_normed[r] * gain[...]
        pair_grad[r] = (
            inv_std
            * (e - jnp.mean(e, axis=-1, keepdims=True) - unit * jnp.mean(e * unit, axis=-1, keepdims=True))
        ).astype(BF)


def kernel(
    tok, codes, expo, gain, w, wo, bias, ug,
    update_hbm, normed_hbm, bias_hbm,
    update, bias_grad,
    wt, wot, nb, gates, dgated, kn, qt, dot, bias_g, bias_t, probs, s_ref, qbd, dos,
    m_st, l_st, a_st, vals, keys_t, gk, att_loc, st_loc, att_tx, att_rx, st_rx, back_tx, back_rx, stats, dgp,
    ds_ref, k_ref, vt_ref, gv_ref, acc, dq, kt, rxc, ytx, rxy, rsum, ztx, zrx, ftx, frx, dqtx, dqrx, gtx, grx,
    bx_s, bx_r, ks_s, ks_r, zr_s, zr_r, sb_s, sb_r, pq_s, pq_r, ex_s, ex_r, kc_s, kc_r,
    ky_s, ky_r, zq_s, zq_r, f_s, f_r, g_s, g_r, o_s,
):
    row_id = lax.axis_index("row")
    col_id = lax.axis_index("col")
    yh, x = row_id // NX, lax.rem(row_id, NX)
    yl, z, c = col_id // 16, lax.rem(col_id, 16) // 2, lax.rem(col_id, 2)
    xs = [lax.rem(x + i, NX) for i in range(NX)]
    zs = [lax.rem(z + i, NZ) for i in range(NZ)]

    def dev(x_=x, yh_=yh, yl_=yl, z_=z, c_=c):
        return (yh_ * NX + x_, yl_ * 16 + z_ * 2 + c_)

    def rc(src, dst, send, recv, to):
        return pltpu.make_async_remote_copy(
            src_ref=src, dst_ref=dst, send_sem=send, recv_sem=recv,
            device_id=to, device_id_type=pl.DeviceIdType.MESH,
        )

    xp, xm, zp, zm = dev(x_=xs[1]), dev(x_=xs[3]), dev(z_=zs[1]), dev(z_=zs[7])
    sib = dev(c_=1 - c)
    ypart = dev(yl_=1 - yl)
    hpart = dev(yh_=1 - yh)
    cross = dev(yh_=1 - yh, yl_=1 - yl)
    swap = dev(yh_=yl, yl_=yh)
    is_home = yh == yl

    barrier = pltpu.get_barrier_semaphore()
    for to in (xp, xm, zp, zm, sib, ypart, hpart, cross):
        pl.semaphore_signal(barrier, inc=1, device_id=to, device_id_type=pl.DeviceIdType.MESH)

    gain_row = gain[...]
    for r in range(ROWS):
        nb[r] = (normalised(codes, expo, r)[0] * gain_row).astype(BF)

    pl.semaphore_wait(barrier, 8)

    bias_p = rc(bias, bias_g.at[0], bx_s.at[0], bx_r.at[0], xp)
    bias_m = rc(bias, bias_g.at[1], bx_s.at[1], bx_r.at[1], xm)
    bias_fp = rc(bias_g.at[0, pl.ds(0, 2)], bias_g.at[2, pl.ds(0, 2)], bx_s.at[2], bx_r.at[2], xp)
    bias_fm = rc(bias_g.at[1, pl.ds(2, 2)], bias_g.at[2, pl.ds(2, 2)], bx_s.at[3], bx_r.at[3], xm)
    bias_p.start()
    bias_m.start()

    def key_at(zz, cc):
        return pl.ds(pl.multiple_of(zz * 256 + cc * 128, 128), 128)

    my_set = pl.ds(pl.multiple_of(yh * ROWS, ROWS), ROWS)
    key_send = [
        rc(nb, kn.at[pl.ds(yh * ROWS, ROWS), key_at(z, c)], ks_s.at[t], ks_r.at[yh], dev(yh_=yl, yl_=t))
        for t in range(2)
    ]
    for t in range(2):
        @pl.when(jnp.logical_not(jnp.logical_and(is_home, yl == t)))
        def _():
            key_send[t].start()

    @pl.when(is_home)
    def _():
        kn[pl.ds(yh * ROWS, ROWS), key_at(z, c), :] = nb[...]

    for q in range(4):
        wt[q * 128 : (q + 1) * 128, :] = w[:, q * 128 : (q + 1) * 128].astype(F32).T.astype(BF)
    wot[...] = wo[...].astype(F32).T.astype(BF)

    def set_of(ref, s):
        return ref.at[pl.ds(s * ROWS, ROWS)]

    for r in range(ROWS):
        n = nb[r]
        qt[yh * ROWS + r] = (nt(wt[0:128, :], n) * (DH ** -0.5)).astype(BF)
        gate = jax.nn.sigmoid(nt(wt[384:512, :], n))
        gates[r] = gate
        dg = nt(wo[...], ug[r])
        dgated[r] = dg
        dot[yh * ROWS + r] = (dg * gate).astype(BF)
    q_send = rc(set_of(qt, yh), set_of(qt, yh), pq_s.at[0], pq_r.at[0], hpart)
    d_send = rc(set_of(dot, yh), set_of(dot, yh), pq_s.at[1], pq_r.at[1], hpart)
    q_send.start()

    live = tok[...].reshape(1, 1)

    def prep(src, xb):
        for k in range(4):
            first = (yh * NX + xb) * KB + k * 128
            valid = first + lax.broadcasted_iota(jnp.int32, (128, 128), 0) < live
            for h in range(HEADS):
                tile = src[h, :, k * 128 : (k + 1) * 128].astype(F32).T
                bias_t[xb, k * 128 : (k + 1) * 128, h * 128 : (h + 1) * 128] = jnp.where(valid, tile, MASKED)

    qbd[...] = jnp.zeros_like(qbd)
    dos[...] = jnp.zeros_like(dos)
    prep(bias, x)

    for s in range(2):
        @pl.when(jnp.logical_not(jnp.logical_and(is_home, yh == s)))
        def _():
            rc(nb, kn.at[pl.ds(s * ROWS, ROWS), key_at(z, c)], ks_s.at[0], ks_r.at[s], sib).wait_recv()

    def block(zz, cc=c):
        return kn.at[:, key_at(zz, cc)]

    def half(zz, s):
        return kn.at[pl.ds(s * ROWS, ROWS), key_at(zz, c)]

    def up(i):
        src = block(zs[(8 - i) % 8]) if i < 3 else half(zs[5], 0)
        return rc(src, src, zr_s.at[0, i], zr_r.at[0, i], zp)

    def down(i):
        src = block(zs[i]) if i < 3 else half(zs[3], 1)
        return rc(src, src, zr_s.at[1, i], zr_r.at[1, i], zm)

    def to_sib(i):
        return rc(block(zs[i]), block(zs[i]), sb_s.at[i], sb_r.at[i], sib)

    def from_sib(i):
        return rc(block(zs[i], 1 - c), block(zs[i], 1 - c), sb_s.at[i], sb_r.at[i], sib)

    def up_in(i):
        dst = block(zs[7 - i]) if i < 3 else half(zs[4], 0)
        return rc(dst, dst, zr_s.at[0, i], zr_r.at[0, i], zp)

    def down_in(i):
        dst = block(zs[i + 1]) if i < 3 else half(zs[4], 1)
        return rc(dst, dst, zr_s.at[1, i], zr_r.at[1, i], zm)

    def ring_step(i):
        up_in(i).wait_recv()
        if i < 3:
            up(i + 1).start()
            to_sib(7 - i).start()
        down_in(i).wait_recv()
        if i < 3:
            down(i + 1).start()
            to_sib(i + 1).start()
        else:
            to_sib(4).start()

    up(0).start()
    down(0).start()
    to_sib(0).start()
    bias_p.wait_recv()
    bias_fp.start()
    bias_m.wait_recv()
    bias_fm.start()
    prep(bias_g.at[0], xs[3])
    prep(bias_g.at[1], xs[1])
    ring_step(0)

    zb = z // 2
    even = lax.rem(z, 2) == 0
    near = jnp.where(even, zb + 3, zb + 1)
    far = jnp.where(even, zb + 1, zb + 3)

    def arrive(phase):
        for i in ((0, 1, 7), (2, 6), (3, 5), (4,))[phase]:
            from_sib(i).wait_recv()

    vt_ref[64:80, :] = jnp.ones((16, KB), BF)
    vt_ref[144:160, :] = jnp.ones((16, KB), BF)

    def load_q(row):
        for h in range(HEADS):
            qbd[h * 32 : (h + 1) * 32, h * 128 : (h + 1) * 128] = qt[row, h * 32 : (h + 1) * 32, :]

    att_copy = rc(att_tx, att_rx, ex_s.at[0], ex_r.at[0], hpart)
    st_copy = rc(set_of(st_loc, 1 - yh), st_rx, ex_s.at[1], ex_r.at[1], hpart)
    back_copy = rc(back_tx, back_rx, ex_s.at[2], ex_r.at[2], hpart)

    def combine(row):
        m_all = [m_st[row * 4 + i] for i in range(4)]
        top_m = jnp.maximum(jnp.maximum(m_all[0], m_all[1]), jnp.maximum(m_all[2], m_all[3]))
        total = jnp.zeros((HEADS, T), F32)
        weighted = jnp.zeros((C, T), F32)
        for i in range(4):
            f = jnp.exp(m_all[i] - top_m)
            total = total + f * l_st[row * 4 + i]
            weighted = weighted + per_head(f) * a_st[row * 4 + i]
        st_loc[row, 0:4, :] = top_m
        st_loc[row, 4:8, :] = total
        return weighted

    def forward(u, carry):
        phase, t = u // 6, lax.rem(u, 6)
        row = lax.rem(jnp.where(phase == 3, 1 - yh, yh) * ROWS + t, 2 * ROWS)
        xb = lax.rem(
            jnp.where(phase == 0, zb, jnp.where(phase == 1, near, jnp.where(phase == 2, far, zb + 2))), NX
        )
        slot = row * 4 + xb

        for i in range(4):
            @pl.when(u == 6 * i)
            def _():
                arrive(i)

        @pl.when(jnp.logical_and(t == 0, xb == xs[2]))
        def _():
            bias_fp.wait_recv()
            bias_fm.wait_recv()
            prep(bias_g.at[2], xs[2])

        for i in range(1, 4):
            @pl.when(u == 6 * i - 3)
            def _():
                ring_step(i)

        @pl.when(u == 3)
        def _():
            rc(set_of(qt, yh), set_of(qt, 1 - yh), pq_s.at[0], pq_r.at[0], hpart).wait_recv()
            d_send.start()

        load_q(row)

        @pl.when(u < 6)
        def _():
            gk[row] = nn(w[:, 128:256], qbd[...]).astype(BF)

        n = kn[row, pl.ds(pl.multiple_of(xb * KB, KB), KB), :]
        for i in range(4):
            rows = slice(i * 128, (i + 1) * 128)
            kv = nn(n[rows, :], w[:, 128:384]).astype(BF)
            k_ref[rows, :] = kv[:, 0:128]
            vals[slot, rows, :] = kv[:, 128:256]
        for i in range(2):
            lanes = slice(i * 256, (i + 1) * 256)
            keys_t[slot, :, lanes] = nt(wt[128:256, :], n[lanes, :]).astype(BF)
            vt_ref[0:64, lanes] = nt(wt[256:320, :], n[lanes, :]).astype(BF)
            vt_ref[80:144, lanes] = nt(wt[320:384, :], n[lanes, :]).astype(BF)
        for hp in range(2):
            cols = slice(hp * 256, hp * 256 + 256)
            q2 = qbd[:, cols]
            top = None
            for i in range(4):
                rows = slice(i * 128, (i + 1) * 128)
                s = nn(k_ref[rows, :], q2) + bias_t[xb, rows, cols]
                s_ref[rows, cols] = s
                part = jnp.max(s.reshape(16, 8, 256), axis=0)
                top = part if top is None else jnp.maximum(top, part)
            m = jnp.max(top, axis=0, keepdims=True)
            for i in range(4):
                rows = slice(i * 128, (i + 1) * 128)
                probs[slot, rows, cols] = jnp.exp(s_ref[rows, cols] - m).astype(BF)
            a = nn(vt_ref[hp * 80 : hp * 80 + 80, :], probs[slot, :, cols])
            for j in range(2):
                h = hp * 2 + j
                lanes = slice(j * 128, (j + 1) * 128)
                m_st[slot, h : h + 1, :] = m[:, lanes]
                l_st[slot, h : h + 1, :] = a[64:65, lanes]
                a_st[slot, h * 32 : (h + 1) * 32, :] = a[j * 32 : (j + 1) * 32, lanes]

        @pl.when(u == 20)
        def _():
            for r in range(ROWS):
                att_tx[r] = combine((1 - yh) * ROWS + r).astype(BF)
            att_copy.start()
            st_copy.start()

        return carry

    lax.fori_loop(0, 24, forward, 0)

    for r in range(ROWS):
        att_loc[yh * ROWS + r] = combine(yh * ROWS + r)
    att_copy.wait_recv()
    st_copy.wait_recv()
    for r in range(ROWS):
        mine = yh * ROWS + r
        ma, la = st_loc[mine, 0:4, :], st_loc[mine, 4:8, :]
        mb, lb = st_rx[r, 0:4, :], st_rx[r, 4:8, :]
        top_m = jnp.maximum(ma, mb)
        fa, fb = jnp.exp(ma - top_m), jnp.exp(mb - top_m)
        total = fa * la + fb * lb
        attended = (per_head(fa) * att_loc[mine] + per_head(fb) * att_rx[r].astype(F32)) / per_head(total)
        gate = gates[r]
        product = dot[mine].astype(F32) * attended
        lse = top_m + jnp.log(total)
        stats[mine, 0:4, :] = lse
        back_tx[r, 0:4, :] = lse
        for h in range(HEADS):
            delta = jnp.sum(product[h * 32 : (h + 1) * 32, :], axis=0, keepdims=True)
            stats[mine, 4 + h : 5 + h, :] = delta
            back_tx[r, 4 + h : 5 + h, :] = delta
        att_loc[mine] = attended
    back_copy.start()
    for r in range(ROWS):
        attended = att_loc[yh * ROWS + r]
        gate = gates[r]
        dgp[r] = dgated[r] * attended * gate * (1.0 - gate)
        update[r] = nn(wot[...], (gate * attended).astype(BF)).T.astype(BF)
    update_out = pltpu.make_async_copy(update, update_hbm, o_s.at[0])
    update_out.start()
    rc(set_of(dot, yh), set_of(dot, 1 - yh), pq_s.at[1], pq_r.at[1], hpart).wait_recv()
    dq[...] = jnp.zeros_like(dq)

    order = [xs[2], xs[1], xs[3], xs[0]]

    def core_copy(zz):
        return rc(kt.at[:, key_at(zz, 1 - c)], rxc.at[zz], kc_s.at[zz], kc_r.at[zz], sib)

    def y_copy(zz):
        return rc(ytx.at[zz], rxy.at[zz], ky_s.at[zz], ky_r.at[zz], ypart)

    def core_stage(xb):
        for b in range(2):
            core_copy(xb * 2 + b).start()

    def y_stage(xb):
        for b in range(2):
            zz = xb * 2 + b
            core_copy(zz).wait_recv()
            for r in range(ROWS):
                theirs, ours = (1 - yl) * ROWS + r, yl * ROWS + r
                ytx[zz, r] = (kt[theirs, key_at(zz, c), :].astype(F32) + rxc[zz, theirs].astype(F32)).astype(BF)
                rsum[zz, r] = kt[ours, key_at(zz, c), :].astype(F32) + rxc[zz, ours].astype(F32)
            y_copy(zz).start()

    def sum_stage(xb):
        for b in range(2):
            zz = xb * 2 + b
            y_copy(zz).wait_recv()
            rsum[zz] = rsum[zz] + rxy[zz].astype(F32)

    g_half_p = rc(gtx.at[0, pl.ds(0, 2)], grx.at[0, pl.ds(0, 2)], g_s.at[0], g_r.at[0], xp)
    g_half_m = rc(gtx.at[0, pl.ds(2, 2)], grx.at[0, pl.ds(2, 2)], g_s.at[1], g_r.at[1], xm)
    g_p = rc(gtx.at[1], grx.at[1], g_s.at[2], g_r.at[2], xp)
    g_m = rc(gtx.at[2], grx.at[2], g_s.at[3], g_r.at[3], xm)

    def turned(h, k):
        return acc[k * 128 : (k + 1) * 128, h * 128 : (h + 1) * 128].T

    def bias_stage(step):
        if step == 1:
            g_half_p.wait_recv()
        if step == 2:
            g_half_m.wait_recv()
        if step == 3:
            g_p.wait_recv()
            g_m.wait_recv()
        for h in range(HEADS):
            for k in range(4):
                lanes = slice(k * 128, (k + 1) * 128)
                tile = turned(h, k)
                if (step == 1 and h < 2) or (step == 2 and h >= 2):
                    tile = tile + grx[0, h, :, lanes].astype(F32)
                if step == 3:
                    tile = tile + grx[1, h, :, lanes].astype(F32) + grx[2, h, :, lanes].astype(F32)
                    bias_grad[h, :, lanes] = tile.astype(BF)
                else:
                    gtx[step, h, :, lanes] = tile.astype(BF)
        if step == 0:
            g_half_p.start()
            g_half_m.start()
        if step == 1:
            g_p.start()
        if step == 2:
            g_m.start()

    def backward(u, carry):
        step = u // 6
        xb = lax.rem(x + jnp.where(step == 0, 2, jnp.where(step == 1, 1, jnp.where(step == 2, 3, 0))), NX)
        row = lax.rem(yh * ROWS + lax.rem(u, 6), 2 * ROWS)
        slot = row * 4 + xb

        @pl.when(u == 3)
        def _():
            back_copy.wait_recv()
            for r in range(ROWS):
                stats[(1 - yh) * ROWS + r] = back_rx[r]

        @pl.when(lax.rem(u, 6) == 0)
        def _():
            acc[...] = jnp.zeros_like(acc)

        st = stats[row]
        f = jnp.exp(m_st[slot] - st[0:4, :])
        dls = f * st[4:8, :]
        for h in range(HEADS):
            rows = slice(h * 32, (h + 1) * 32)
            dos[rows, h * 128 : (h + 1) * 128] = (dot[row, rows, :].astype(F32) * f[h : h + 1, :]).astype(BF)
        key_t = keys_t[slot]
        for hp in range(2):
            cols = slice(hp * 256, hp * 256 + 256)
            d2 = dos[:, cols]
            l2 = jnp.concatenate([dls[hp * 2 : hp * 2 + 1, :], dls[hp * 2 + 1 : hp * 2 + 2, :]], axis=1)
            for i in range(4):
                rows = slice(i * 128, (i + 1) * 128)
                d_score = probs[slot, rows, cols].astype(F32) * (nn(vals[slot, rows, :], d2) - l2)
                acc[rows, cols] = acc[rows, cols] + d_score
                ds_ref[rows, cols] = d_score.astype(BF)
            d_query = nn(key_t[hp * 64 : hp * 64 + 64, :], ds_ref[:, cols])
            for j in range(2):
                rows = slice((hp * 2 + j) * 32, (hp * 2 + j + 1) * 32)
                dq[row, rows, :] = dq[row, rows, :] + d_query[j * 32 : (j + 1) * 32, j * 128 : (j + 1) * 128]
        for i in range(2):
            lanes = slice(i * 256, (i + 1) * 256)
            gv_ref[:, lanes] = nn(w[:, 256:384], dos[:, lanes]).astype(BF)
        for i in range(4):
            rows = slice(i * 128, (i + 1) * 128)
            term = nt(ds_ref[rows, :], gk[row]) + nt(probs[slot, rows, :], gv_ref[...])
            kt[row, pl.ds(pl.multiple_of(xb * KB + i * 128, 128), 128), :] = term.astype(BF)

        for s in range(4):
            @pl.when(u == 6 * s + 5)
            def _():
                bias_stage(s) if s < 3 else None
                core_stage(order[s])
                if s >= 1:
                    y_stage(order[s - 1])
                if s >= 2:
                    sum_stage(order[s - 2])

        return carry

    lax.fori_loop(0, 24, backward, 0)

    for r in range(ROWS):
        dqtx[r] = dq[(1 - yh) * ROWS + r].astype(BF)
    dq_copy = rc(dqtx, dqrx, f_s.at[0], f_r.at[0], hpart)
    dq_copy.start()
    y_stage(order[3])
    sum_stage(order[2])
    sum_stage(order[3])

    def z_copy(way, i):
        if i == 0:
            part = pl.ds(way * 64, 64)
            src, dst = ztx.at[way, 0, :, part], zrx.at[way, 0, :, part]
        else:
            src, dst = ztx.at[way, i], zrx.at[way, i]
        return rc(src, dst, zq_s.at[way, i], zq_r.at[way, i], zp if way == 0 else zm)

    for i in range(4):
        for way in range(2):
            home = zs[(4 - i) if way == 0 else (4 + i)]
            if i == 0:
                part = slice(way * 64, way * 64 + 64)
                ztx[way, 0, :, part, :] = rsum[home, :, part, :].astype(BF)
            else:
                z_copy(way, i - 1).wait_recv()
                if i == 1:
                    part = slice(way * 64, way * 64 + 64)
                    other = slice(64 - way * 64, 128 - way * 64)
                    ztx[way, 1, :, part, :] = (
                        rsum[home, :, part, :] + zrx[way, 0, :, part, :].astype(F32)
                    ).astype(BF)
                    ztx[way, 1, :, other, :] = rsum[home, :, other, :].astype(BF)
                else:
                    ztx[way, i] = (rsum[home] + zrx[way, i - 1].astype(F32)).astype(BF)
            z_copy(way, i).start()
    bias_stage(3)
    bias_out = pltpu.make_async_copy(bias_grad, bias_hbm, o_s.at[1])
    bias_out.start()
    z_copy(0, 3).wait_recv()
    z_copy(1, 3).wait_recv()
    ftx[...] = (rsum[z] + zrx[0, 3].astype(F32) + zrx[1, 3].astype(F32)).astype(BF)
    final = rc(ftx, frx, f_s.at[1], f_r.at[1], swap)

    @pl.when(jnp.logical_not(is_home))
    def _():
        final.start()

    @pl.when(is_home)
    def _():
        frx[...] = ftx[...]

    dq_copy.wait_recv()
    for r in range(ROWS):
        d_query = (dq[yh * ROWS + r] + dqrx[r].astype(F32)) * (DH ** -0.5)
        unit_t = split_nn(w[:, 0:128], d_query) + split_nn(w[:, 384:512], dgp[r])
        dgated[r] = unit_t.T

    @pl.when(jnp.logical_not(is_home))
    def _():
        final.wait_recv()

    for r in range(ROWS):
        dgated[r] = dgated[r] + frx[r].astype(F32)
    normed_out = pltpu.make_async_copy(dgated, normed_hbm, o_s.at[2])
    normed_out.start()

    for copy in (bias_p, bias_m, bias_fp, bias_fm, q_send, d_send, att_copy, st_copy, back_copy, dq_copy,
                 g_half_p, g_half_m, g_p, g_m):
        copy.wait_send()
    for t in range(2):
        @pl.when(jnp.logical_not(jnp.logical_and(is_home, yl == t)))
        def _():
            key_send[t].wait_send()
    for i in range(4):
        up(i).wait_send()
        down(i).wait_send()
        z_copy(0, i).wait_send()
        z_copy(1, i).wait_send()
    for i in range(8):
        to_sib(i).wait_send()
        core_copy(zs[i]).wait_send()
        y_copy(zs[i]).wait_send()

    @pl.when(jnp.logical_not(is_home))
    def _():
        final.wait_send()

    update_out.wait()
    bias_out.wait()
    normed_out.wait()


def shards(codes, expo, tok, gain, w, wo, bias, ug):
    vm = pltpu.VMEM
    dma = pltpu.SemaphoreType.DMA
    blk = (ROWS, T, C)
    scratch = [
        vm(blk, BF), vm((HEADS, T, KB), BF),
        vm((512, C), BF), vm((C, C), BF), vm(blk, BF), vm(blk, F32), vm(blk, F32),
        vm((6, 2048, C), BF), vm((6, C, T), BF), vm((6, C, T), BF), vm((3, HEADS, T, KB), BF),
        vm((4, KB, 512), F32), vm((24, KB, 512), BF), vm((KB, 512), F32), vm((C, 512), BF), vm((C, 512), BF),
        vm((24, HEADS, T), F32), vm((24, HEADS, T), F32), vm((24, C, T), F32),
        vm((24, KB, C), BF), vm((24, C, KB), BF), vm((6, C, 512), BF), vm((6, C, T), F32), vm((6, 8, T), F32),
        vm(blk, BF), vm(blk, BF), vm((ROWS, 8, T), F32), vm((ROWS, 8, T), F32), vm((ROWS, 8, T), F32),
        vm((6, 8, T), F32), vm(blk, F32),
        vm((KB, 512), BF), vm((KB, C), BF), vm((160, KB), BF), vm((C, 512), BF), vm((KB, 512), F32), vm((6, C, T), F32), vm((6, 2048, C), BF),
        vm((8, 6, T, C), BF), vm((8, 3, T, C), BF), vm((8, 3, T, C), BF), vm((8, 3, T, C), F32),
        vm((2, 4, 3, T, C), BF), vm((2, 4, 3, T, C), BF), vm(blk, BF), vm(blk, BF), vm(blk, BF), vm(blk, BF),
        vm((3, HEADS, T, KB), BF), vm((3, HEADS, T, KB), BF),
        dma((4,)), dma((4,)), dma((2,)), dma((2,)), dma((2, 4)), dma((2, 4)), dma((8,)), dma((8,)),
        dma((2,)), dma((2,)), dma((3,)), dma((3,)), dma((8,)), dma((8,)), dma((8,)), dma((8,)),
        dma((2, 4)), dma((2, 4)), dma((2,)), dma((2,)), dma((4,)), dma((4,)), dma((3,)),
    ]
    v = pl.BlockSpec(memory_space=pltpu.VMEM)
    hbm = pl.BlockSpec(memory_space=pl.ANY)
    shapes = (
        jax.ShapeDtypeStruct(blk, BF),
        jax.ShapeDtypeStruct(blk, F32),
        jax.ShapeDtypeStruct((HEADS, T, KB), BF),
    )
    gain, expo = gain.reshape(1, C), expo.reshape(1, ROWS)
    update, d_normed, bias_grad = pl.pallas_call(
        kernel,
        out_shape=shapes,
        in_specs=[v] * 8,
        out_specs=(hbm, hbm, hbm),
        scratch_shapes=scratch,
        compiler_params=pltpu.CompilerParams(
            collective_id=0, has_side_effects=True, vmem_limit_bytes=58 * 1024 * 1024
        ),
        cost_estimate=pl.CostEstimate(flops=8_000_000_000, bytes_accessed=4_000_000, transcendentals=6_300_000),
    )(tok, codes, expo, gain, w, wo, bias, ug)
    return pl.pallas_call(
        norm_back,
        out_shape=(shapes[0], shapes[0], shapes[2]),
        in_specs=[v] * 6,
        out_specs=(v, v, v),
        compiler_params=pltpu.CompilerParams(vmem_limit_bytes=58 * 1024 * 1024),
    )(codes, expo, gain, d_normed, update, bias_grad)


def solution(mesh):
    in_specs = (
        P("row", "col", None), P("row", "col"), P(), P(), P(), P(), P(None, "col", "row"), P("row", "col", None),
    )
    out_specs = (P("row", "col", None), P("row", "col", None), P(None, "col", "row"))
    return jax.shard_map(shards, mesh=mesh, in_specs=in_specs, out_specs=out_specs, check_vma=False)
```

```python
import jax
import jax.numpy as jnp
from jax import lax
from jax.experimental import pallas as pl
from jax.experimental.pallas import tpu as pltpu
from jax.sharding import PartitionSpec as P

MASKED = -1e30
EPSILON = 1e-05
F32 = jnp.float32
BF = jnp.bfloat16
NX, NZ = 4, 8
HEADS, DH, C, T = 4, 32, 128, 128
KB = 512
ROWS = 3


def nn(a, b):
    return lax.dot_general(a, b, (((1,), (0,)), ((), ())), preferred_element_type=F32)


def nt(a, b):
    return lax.dot_general(a, b, (((1,), (1,)), ((), ())), preferred_element_type=F32)


def split_nn(w, a):
    high = a.astype(BF)
    low = (a - high.astype(F32)).astype(BF)
    return nn(w, high) + nn(w, low)


def per_head(stat):
    return jnp.concatenate(
        [jnp.broadcast_to(stat[h : h + 1, :], (DH, T)) for h in range(HEADS)], axis=0
    )


def normalised(codes, expo, r):
    value = codes[r].astype(F32) * jnp.exp2(expo[0:1, r : r + 1].astype(F32))
    centered = value - jnp.mean(value, axis=-1, keepdims=True)
    inv_std = lax.rsqrt(jnp.mean(centered * centered, axis=-1, keepdims=True) + EPSILON)
    return centered * inv_std, inv_std


def norm_back(codes, expo, gain, d_normed, update_in, bias_in, update, pair_grad, bias_grad):
    update[...] = update_in[...]
    bias_grad[...] = bias_in[...]
    for r in range(ROWS):
        unit, inv_std = normalised(codes, expo, r)
        e = d_normed[r] * gain[...]
        pair_grad[r] = (
            inv_std
            * (e - jnp.mean(e, axis=-1, keepdims=True) - unit * jnp.mean(e * unit, axis=-1, keepdims=True))
        ).astype(BF)


def kernel(
    tok, codes, expo, gain, w, wo, bias, ug,
    update_hbm, normed_hbm, bias_hbm,
    update, bias_grad,
    wt, wot, nb, gates, dgated, kn, qt, dot, bias_g, bias_t, probs, s_ref, qbd, dos,
    m_st, l_st, a_st, vals, keys_t, gk, att_loc, st_loc, att_tx, att_rx, st_rx, back_tx, back_rx, stats, dgp,
    ds_ref, k_ref, vt_ref, acc, dq, kt, rxc, ytx, rxy, rsum, ztx, zrx, htx, frx, dqtx, dqrx, gtx, grx,
    bx_s, bx_r, ks_s, ks_r, zr_s, zr_r, sb_s, sb_r, pq_s, pq_r, ex_s, ex_r, kc_s, kc_r,
    ky_s, ky_r, zq_s, zq_r, f_s, f_r, g_s, g_r, o_s,
):
    row_id = lax.axis_index("row")
    col_id = lax.axis_index("col")
    yh, x = row_id // NX, lax.rem(row_id, NX)
    yl, z, c = col_id // 16, lax.rem(col_id, 16) // 2, lax.rem(col_id, 2)
    xs = [lax.rem(x + i, NX) for i in range(NX)]
    zs = [lax.rem(z + i, NZ) for i in range(NZ)]

    def dev(x_=x, yh_=yh, yl_=yl, z_=z, c_=c):
        return (yh_ * NX + x_, yl_ * 16 + z_ * 2 + c_)

    def rc(src, dst, send, recv, to):
        return pltpu.make_async_remote_copy(
            src_ref=src, dst_ref=dst, send_sem=send, recv_sem=recv,
            device_id=to, device_id_type=pl.DeviceIdType.MESH,
        )

    xp, xm, zp, zm = dev(x_=xs[1]), dev(x_=xs[3]), dev(z_=zs[1]), dev(z_=zs[7])
    sib = dev(c_=1 - c)
    ypart = dev(yl_=1 - yl)
    hpart = dev(yh_=1 - yh)
    cross = dev(yh_=1 - yh, yl_=1 - yl)
    is_home = yh == yl
    self_home = jnp.logical_and(is_home, jnp.logical_and(z // 4 == c, lax.rem(z, 2) == c))

    barrier = pltpu.get_barrier_semaphore()
    def greet(to):
        pl.semaphore_signal(barrier, inc=1, device_id=to, device_id_type=pl.DeviceIdType.MESH)

    for to in (xp, xm, sib, ypart, hpart, cross):
        greet(to)
    for i in range(1, 8):
        greet(dev(z_=zs[i]))
    for i in range(4):
        @pl.when(jnp.logical_not(jnp.logical_and(self_home, z // 2 == i)))
        def _():
            greet(dev(yh_=yl, yl_=yh, z_=2 * i + c, c_=z // 4))

        @pl.when(jnp.logical_not(jnp.logical_and(self_home, lax.rem(z, 4) == i)))
        def _():
            greet(dev(yh_=yl, yl_=yh, z_=4 * c + i, c_=lax.rem(z, 2)))


    gain_row = gain[...]
    for r in range(ROWS):
        nb[r] = (normalised(codes, expo, r)[0] * gain_row).astype(BF)

    pl.semaphore_wait(barrier, jnp.where(self_home, 19, 21))

    bias_p = rc(bias, bias_g.at[0], bx_s.at[0], bx_r.at[0], xp)
    bias_m = rc(bias, bias_g.at[1], bx_s.at[1], bx_r.at[1], xm)
    bias_fp = rc(bias_g.at[0, pl.ds(0, 2)], bias_g.at[2, pl.ds(0, 2)], bx_s.at[2], bx_r.at[2], xp)
    bias_fm = rc(bias_g.at[1, pl.ds(2, 2)], bias_g.at[2, pl.ds(2, 2)], bx_s.at[3], bx_r.at[3], xm)
    bias_p.start()
    bias_m.start()

    def key_at(zz, cc):
        return pl.ds(pl.multiple_of(zz * 256 + cc * 128, 128), 128)

    my_set = pl.ds(pl.multiple_of(yh * ROWS, ROWS), ROWS)
    key_send = [
        rc(nb, kn.at[pl.ds(yh * ROWS, ROWS), key_at(z, c)], ks_s.at[t], ks_r.at[yh], dev(yh_=yl, yl_=t))
        for t in range(2)
    ]
    for t in range(2):
        @pl.when(jnp.logical_not(jnp.logical_and(is_home, yl == t)))
        def _():
            key_send[t].start()

    @pl.when(is_home)
    def _():
        kn[pl.ds(yh * ROWS, ROWS), key_at(z, c), :] = nb[...]

    for q in range(4):
        wt[q * 128 : (q + 1) * 128, :] = w[:, q * 128 : (q + 1) * 128].astype(F32).T.astype(BF)
    wot[...] = wo[...].astype(F32).T.astype(BF)

    def set_of(ref, s):
        return ref.at[pl.ds(s * ROWS, ROWS)]

    for r in range(ROWS):
        n = nb[r]
        qt[yh * ROWS + r] = (nt(wt[0:128, :], n) * (DH ** -0.5)).astype(BF)
        gate = jax.nn.sigmoid(nt(wt[384:512, :], n))
        gates[r] = gate
        dg = nt(wo[...], ug[r])
        dgated[r] = dg
        dot[yh * ROWS + r] = (dg * gate).astype(BF)
    q_send = rc(set_of(qt, yh), set_of(qt, yh), pq_s.at[0], pq_r.at[0], hpart)
    d_send = rc(set_of(dot, yh), set_of(dot, yh), pq_s.at[1], pq_r.at[1], hpart)
    q_send.start()

    live = tok[...].reshape(1, 1)

    def prep(src, xb):
        for k in range(4):
            first = (yh * NX + xb) * KB + k * 128
            valid = first + lax.broadcasted_iota(jnp.int32, (128, 128), 0) < live
            for h in range(HEADS):
                tile = src[h, :, k * 128 : (k + 1) * 128].astype(F32).T
                bias_t[xb, k * 128 : (k + 1) * 128, h * 128 : (h + 1) * 128] = jnp.where(valid, tile, MASKED)

    qbd[...] = jnp.zeros_like(qbd)
    dos[...] = jnp.zeros_like(dos)
    prep(bias, x)

    for s in range(2):
        @pl.when(jnp.logical_not(jnp.logical_and(is_home, yh == s)))
        def _():
            rc(nb, kn.at[pl.ds(s * ROWS, ROWS), key_at(z, c)], ks_s.at[0], ks_r.at[s], sib).wait_recv()

    def block(zz, cc=c):
        return kn.at[:, key_at(zz, cc)]

    def half(zz, s):
        return kn.at[pl.ds(s * ROWS, ROWS), key_at(zz, c)]

    def up(i):
        src = block(zs[(8 - i) % 8]) if i < 3 else half(zs[5], 0)
        return rc(src, src, zr_s.at[0, i], zr_r.at[0, i], zp)

    def down(i):
        src = block(zs[i]) if i < 3 else half(zs[3], 1)
        return rc(src, src, zr_s.at[1, i], zr_r.at[1, i], zm)

    def to_sib(i):
        return rc(block(zs[i]), block(zs[i]), sb_s.at[i], sb_r.at[i], sib)

    def from_sib(i):
        return rc(block(zs[i], 1 - c), block(zs[i], 1 - c), sb_s.at[i], sb_r.at[i], sib)

    def up_in(i):
        dst = block(zs[7 - i]) if i < 3 else half(zs[4], 0)
        return rc(dst, dst, zr_s.at[0, i], zr_r.at[0, i], zp)

    def down_in(i):
        dst = block(zs[i + 1]) if i < 3 else half(zs[4], 1)
        return rc(dst, dst, zr_s.at[1, i], zr_r.at[1, i], zm)

    def ring_step(i):
        up_in(i).wait_recv()
        if i < 3:
            up(i + 1).start()
            to_sib(7 - i).start()
        down_in(i).wait_recv()
        if i < 3:
            down(i + 1).start()
            to_sib(i + 1).start()
        else:
            to_sib(4).start()

    up(0).start()
    down(0).start()
    to_sib(0).start()
    bias_p.wait_recv()
    bias_fp.start()
    bias_m.wait_recv()
    bias_fm.start()
    prep(bias_g.at[0], xs[3])
    prep(bias_g.at[1], xs[1])
    ring_step(0)

    zb = z // 2
    even = lax.rem(z, 2) == 0
    near = jnp.where(even, zb + 3, zb + 1)
    far = jnp.where(even, zb + 1, zb + 3)

    def arrive(phase):
        for i in ((0, 1, 7), (2, 6), (3, 5), (4,))[phase]:
            from_sib(i).wait_recv()

    vt_ref[64:80, :] = jnp.ones((16, KB), BF)
    vt_ref[144:160, :] = jnp.ones((16, KB), BF)

    def load_q(row):
        for h in range(HEADS):
            qbd[h * 32 : (h + 1) * 32, h * 128 : (h + 1) * 128] = qt[row, h * 32 : (h + 1) * 32, :]

    att_copy = rc(att_tx, att_rx, ex_s.at[0], ex_r.at[0], hpart)
    st_copy = rc(set_of(st_loc, 1 - yh), st_rx, ex_s.at[1], ex_r.at[1], hpart)
    back_copy = rc(back_tx, back_rx, ex_s.at[2], ex_r.at[2], hpart)

    def combine(row):
        m_all = [m_st[row * 4 + i] for i in range(4)]
        top_m = jnp.maximum(jnp.maximum(m_all[0], m_all[1]), jnp.maximum(m_all[2], m_all[3]))
        total = jnp.zeros((HEADS, T), F32)
        weighted = jnp.zeros((C, T), F32)
        for i in range(4):
            f = jnp.exp(m_all[i] - top_m)
            total = total + f * l_st[row * 4 + i]
            weighted = weighted + per_head(f) * a_st[row * 4 + i]
        st_loc[row, 0:4, :] = top_m
        st_loc[row, 4:8, :] = total
        return weighted

    def forward(u, carry):
        phase, t = u // 6, lax.rem(u, 6)
        row = lax.rem(jnp.where(phase == 3, 1 - yh, yh) * ROWS + t, 2 * ROWS)
        xb = lax.rem(
            jnp.where(phase == 0, zb, jnp.where(phase == 1, near, jnp.where(phase == 2, far, zb + 2))), NX
        )
        slot = row * 4 + xb

        for i in range(4):
            @pl.when(u == 6 * i)
            def _():
                arrive(i)

        @pl.when(jnp.logical_and(t == 0, xb == xs[2]))
        def _():
            bias_fp.wait_recv()
            bias_fm.wait_recv()
            prep(bias_g.at[2], xs[2])

        for i in range(1, 4):
            @pl.when(u == 6 * i - 3)
            def _():
                ring_step(i)

        @pl.when(u == 3)
        def _():
            rc(set_of(qt, yh), set_of(qt, 1 - yh), pq_s.at[0], pq_r.at[0], hpart).wait_recv()
            d_send.start()

        load_q(row)

        @pl.when(u < 6)
        def _():
            gk[row] = nn(w[:, 128:256], qbd[...]).astype(BF)

        n = kn[row, pl.ds(pl.multiple_of(xb * KB, KB), KB), :]
        kv = nn(n, w[:, 128:384]).astype(BF)
        kvt = nt(wt[128:384, :], n).astype(BF)
        k_ref[...] = kv[:, 0:128]
        vals[slot] = kv[:, 128:256]
        keys_t[slot] = kvt[0:128, :]
        vt_ref[0:64, :] = kvt[128:192, :]
        vt_ref[80:144, :] = kvt[192:256, :]
        for hp in range(2):
            cols = slice(hp * 256, hp * 256 + 256)
            q2 = qbd[:, cols]
            top = None
            for i in range(4):
                rows = slice(i * 128, (i + 1) * 128)
                s = nn(k_ref[rows, :], q2) + bias_t[xb, rows, cols]
                s_ref[rows, cols] = s
                part = jnp.max(s.reshape(16, 8, 256), axis=0)
                top = part if top is None else jnp.maximum(top, part)
            m = jnp.max(top, axis=0, keepdims=True)
            for i in range(4):
                rows = slice(i * 128, (i + 1) * 128)
                probs[slot, rows, cols] = jnp.exp(s_ref[rows, cols] - m).astype(BF)
            a = nn(vt_ref[hp * 80 : hp * 80 + 80, :], probs[slot, :, cols])
            for j in range(2):
                h = hp * 2 + j
                lanes = slice(j * 128, (j + 1) * 128)
                m_st[slot, h : h + 1, :] = m[:, lanes]
                l_st[slot, h : h + 1, :] = a[64:65, lanes]
                a_st[slot, h * 32 : (h + 1) * 32, :] = a[j * 32 : (j + 1) * 32, lanes]

        @pl.when(u == 20)
        def _():
            for r in range(ROWS):
                att_tx[r] = combine((1 - yh) * ROWS + r).astype(BF)
            att_copy.start()
            st_copy.start()

        return carry

    lax.fori_loop(0, 24, forward, 0)

    for r in range(ROWS):
        att_loc[yh * ROWS + r] = combine(yh * ROWS + r)
    att_copy.wait_recv()
    st_copy.wait_recv()
    for r in range(ROWS):
        mine = yh * ROWS + r
        ma, la = st_loc[mine, 0:4, :], st_loc[mine, 4:8, :]
        mb, lb = st_rx[r, 0:4, :], st_rx[r, 4:8, :]
        top_m = jnp.maximum(ma, mb)
        fa, fb = jnp.exp(ma - top_m), jnp.exp(mb - top_m)
        total = fa * la + fb * lb
        attended = (per_head(fa) * att_loc[mine] + per_head(fb) * att_rx[r].astype(F32)) / per_head(total)
        gate = gates[r]
        product = dot[mine].astype(F32) * attended
        lse = top_m + jnp.log(total)
        stats[mine, 0:4, :] = lse
        back_tx[r, 0:4, :] = lse
        for h in range(HEADS):
            delta = jnp.sum(product[h * 32 : (h + 1) * 32, :], axis=0, keepdims=True)
            stats[mine, 4 + h : 5 + h, :] = delta
            back_tx[r, 4 + h : 5 + h, :] = delta
        att_loc[mine] = attended
    back_copy.start()
    for r in range(ROWS):
        attended = att_loc[yh * ROWS + r]
        gate = gates[r]
        dgp[r] = dgated[r] * attended * gate * (1.0 - gate)
        update[r] = nn(wot[...], (gate * attended).astype(BF)).T.astype(BF)
    update_out = pltpu.make_async_copy(update, update_hbm, o_s.at[0])
    update_out.start()
    rc(set_of(dot, yh), set_of(dot, 1 - yh), pq_s.at[1], pq_r.at[1], hpart).wait_recv()
    dq[...] = jnp.zeros_like(dq)

    def core_half(xb, cc):
        return pl.ds(pl.multiple_of(xb * KB + cc * 256, 256), 256)

    def z_part(zz):
        return pl.ds(pl.multiple_of(zz * 32, 32), 32)

    def core_copy(xb):
        return rc(kt.at[:, core_half(xb, 1 - c)], rxc.at[xb], kc_s.at[xb], kc_r.at[xb], sib)

    def y_copy(xb):
        return rc(ytx.at[xb], rxy.at[xb], ky_s.at[xb], ky_r.at[xb], ypart)

    def z_copy(xb, i):
        return rc(
            ztx.at[xb, :, z_part(zs[i])], zrx.at[xb, i], zq_s.at[xb, i], zq_r.at[xb, i], dev(z_=zs[i])
        )

    def own_copy(xb):
        part = lax.rem(z, 4)
        return rc(
            htx.at[xb], frx.at[:, z_part(part)], f_s.at[xb], f_r.at[part],
            dev(yh_=yl, yl_=yh, z_=2 * xb + c, c_=z // 4),
        )

    def y_stage(xb):
        core_copy(xb).wait_recv()
        for r in range(ROWS):
            theirs, ours = (1 - yl) * ROWS + r, yl * ROWS + r
            ytx[xb, r] = (kt[theirs, core_half(xb, c), :].astype(F32) + rxc[xb, theirs].astype(F32)).astype(BF)
        y_copy(xb).start()
        for r in range(ROWS):
            ours = yl * ROWS + r
            rsum[xb, r] = kt[ours, core_half(xb, c), :].astype(F32) + rxc[xb, ours].astype(F32)

    def z_stage(xb):
        y_copy(xb).wait_recv()
        for r in range(ROWS):
            total = rsum[xb, r] + rxy[xb, r].astype(F32)
            rsum[xb, r] = total
            ztx[xb, r] = total.astype(BF)
        for i in (4, 3, 5, 2, 6, 1, 7):
            z_copy(xb, i).start()

    def home_stage(xb):
        total = rsum[xb, :, z_part(z), :]
        for i in range(1, 8):
            z_copy(xb, i).wait_recv()
            total = total + zrx[xb, i].astype(F32)
        htx[xb] = total.astype(BF)
        stays = jnp.logical_and(self_home, z // 2 == xb)

        @pl.when(stays)
        def _():
            frx[:, z_part(lax.rem(z, 4)), :] = htx[xb]

        @pl.when(jnp.logical_not(stays))
        def _():
            own_copy(xb).start()

    g_half_p = rc(gtx.at[0, pl.ds(0, 2)], grx.at[0, pl.ds(0, 2)], g_s.at[0], g_r.at[0], xp)
    g_half_m = rc(gtx.at[0, pl.ds(2, 2)], grx.at[0, pl.ds(2, 2)], g_s.at[1], g_r.at[1], xm)
    g_p = rc(gtx.at[1], grx.at[1], g_s.at[2], g_r.at[2], xp)
    g_m = rc(gtx.at[2], grx.at[2], g_s.at[3], g_r.at[3], xm)

    def turned(h, k):
        return acc[k * 128 : (k + 1) * 128, h * 128 : (h + 1) * 128].T

    def bias_stage(step):
        if step == 1:
            g_half_p.wait_recv()
        if step == 2:
            g_half_m.wait_recv()
        if step == 3:
            g_p.wait_recv()
            g_m.wait_recv()
        for h in range(HEADS):
            for k in range(4):
                lanes = slice(k * 128, (k + 1) * 128)
                tile = turned(h, k)
                if (step == 1 and h < 2) or (step == 2 and h >= 2):
                    tile = tile + grx[0, h, :, lanes].astype(F32)
                if step == 3:
                    tile = tile + grx[1, h, :, lanes].astype(F32) + grx[2, h, :, lanes].astype(F32)
                    bias_grad[h, :, lanes] = tile.astype(BF)
                else:
                    gtx[step, h, :, lanes] = tile.astype(BF)
        if step == 0:
            g_half_p.start()
            g_half_m.start()
        if step == 1:
            g_p.start()
        if step == 2:
            g_m.start()

    def backward(u, carry):
        step = u // 6
        xb = lax.rem(x + jnp.where(step == 0, 2, jnp.where(step == 1, 1, jnp.where(step == 2, 3, 0))), NX)
        row = lax.rem(yh * ROWS + lax.rem(u, 6), 2 * ROWS)
        slot = row * 4 + xb

        @pl.when(u == 3)
        def _():
            back_copy.wait_recv()
            for r in range(ROWS):
                stats[(1 - yh) * ROWS + r] = back_rx[r]

        @pl.when(lax.rem(u, 6) == 0)
        def _():
            acc[...] = jnp.zeros_like(acc)

        st = stats[row]
        f = jnp.exp(m_st[slot] - st[0:4, :])
        dls = f * st[4:8, :]
        for h in range(HEADS):
            rows = slice(h * 32, (h + 1) * 32)
            dos[rows, h * 128 : (h + 1) * 128] = (dot[row, rows, :].astype(F32) * f[h : h + 1, :]).astype(BF)
        keys = pl.ds(pl.multiple_of(xb * KB, KB), KB)
        key_t = keys_t[slot]
        for hp in range(2):
            cols = slice(hp * 256, hp * 256 + 256)
            d2 = dos[:, cols]
            l2 = jnp.concatenate([dls[hp * 2 : hp * 2 + 1, :], dls[hp * 2 + 1 : hp * 2 + 2, :]], axis=1)
            for i in range(4):
                rows = slice(i * 128, (i + 1) * 128)
                d_score = probs[slot, rows, cols].astype(F32) * (nn(vals[slot, rows, :], d2) - l2)
                acc[rows, cols] = acc[rows, cols] + d_score
                ds_ref[rows, cols] = d_score.astype(BF)
            d_query = nn(key_t[hp * 64 : hp * 64 + 64, :], ds_ref[:, cols])
            for j in range(2):
                rows = slice((hp * 2 + j) * 32, (hp * 2 + j + 1) * 32)
                dq[row, rows, :] = dq[row, rows, :] + d_query[j * 32 : (j + 1) * 32, j * 128 : (j + 1) * 128]
        gv = nn(w[:, 256:384], dos[...]).astype(BF)
        kt[row, keys, :] = (nt(ds_ref[...], gk[row]) + nt(probs[slot], gv)).astype(BF)

        def block_at(back):
            return lax.rem(x + jnp.where(step == back, 2, jnp.where(step == back + 1, 1, 3)), NX)

        @pl.when(jnp.logical_and(step >= 1, lax.rem(u, 6) == 1))
        def _():
            y_stage(block_at(1))

        @pl.when(jnp.logical_and(step >= 2, lax.rem(u, 6) == 3))
        def _():
            home_stage(block_at(2))

        @pl.when(jnp.logical_and(step >= 1, lax.rem(u, 6) == 5))
        def _():
            z_stage(block_at(1))

        @pl.when(lax.rem(u, 6) == 5)
        def _():
            core_copy(xb).start()

        for s in range(3):
            @pl.when(u == 6 * s + 5)
            def _():
                bias_stage(s)

        return carry

    lax.fori_loop(0, 24, backward, 0)

    for r in range(ROWS):
        dqtx[r] = dq[(1 - yh) * ROWS + r].astype(BF)
    dq_copy = rc(dqtx, dqrx, f_s.at[4], f_r.at[4], hpart)
    dq_copy.start()
    y_stage(x)
    bias_stage(3)
    bias_out = pltpu.make_async_copy(bias_grad, bias_hbm, o_s.at[1])
    bias_out.start()
    dq_copy.wait_recv()
    for r in range(ROWS):
        d_query = (dq[yh * ROWS + r] + dqrx[r].astype(F32)) * (DH ** -0.5)
        unit_t = split_nn(w[:, 0:128], d_query) + split_nn(w[:, 384:512], dgp[r])
        dgated[r] = unit_t.T
    z_stage(x)
    home_stage(xs[3])
    home_stage(x)
    for j in range(4):
        @pl.when(jnp.logical_not(jnp.logical_and(self_home, lax.rem(z, 4) == j)))
        def _():
            rc(htx.at[0], frx.at[:, pl.ds(j * 32, 32)], f_s.at[0], f_r.at[j], sib).wait_recv()
    for r in range(ROWS):
        dgated[r] = dgated[r] + frx[r].astype(F32)
    normed_out = pltpu.make_async_copy(dgated, normed_hbm, o_s.at[2])
    normed_out.start()

    for copy in (bias_p, bias_m, bias_fp, bias_fm, q_send, d_send, att_copy, st_copy, back_copy, dq_copy,
                 g_half_p, g_half_m, g_p, g_m):
        copy.wait_send()
    for t in range(2):
        @pl.when(jnp.logical_not(jnp.logical_and(is_home, yl == t)))
        def _():
            key_send[t].wait_send()
    for i in range(4):
        up(i).wait_send()
        down(i).wait_send()
        core_copy(i).wait_send()
        y_copy(i).wait_send()
        for j in range(1, 8):
            z_copy(i, j).wait_send()

        @pl.when(jnp.logical_not(jnp.logical_and(self_home, z // 2 == i)))
        def _():
            own_copy(i).wait_send()

    for i in range(8):
        to_sib(i).wait_send()

    update_out.wait()
    bias_out.wait()
    normed_out.wait()


def shards(codes, expo, tok, gain, w, wo, bias, ug):
    vm = pltpu.VMEM
    dma = pltpu.SemaphoreType.DMA
    blk = (ROWS, T, C)
    scratch = [
        vm(blk, BF), vm((HEADS, T, KB), BF),
        vm((512, C), BF), vm((C, C), BF), vm(blk, BF), vm(blk, F32), vm(blk, F32),
        vm((6, 2048, C), BF), vm((6, C, T), BF), vm((6, C, T), BF), vm((3, HEADS, T, KB), BF),
        vm((4, KB, 512), F32), vm((24, KB, 512), BF), vm((KB, 512), F32), vm((C, 512), BF), vm((C, 512), BF),
        vm((24, HEADS, T), F32), vm((24, HEADS, T), F32), vm((24, C, T), F32),
        vm((24, KB, C), BF), vm((24, C, KB), BF), vm((6, C, 512), BF), vm((6, C, T), F32), vm((6, 8, T), F32),
        vm(blk, BF), vm(blk, BF), vm((ROWS, 8, T), F32), vm((ROWS, 8, T), F32), vm((ROWS, 8, T), F32),
        vm((6, 8, T), F32), vm(blk, F32),
        vm((KB, 512), BF), vm((KB, C), BF), vm((160, KB), BF), vm((KB, 512), F32), vm((6, C, T), F32), vm((6, 2048, C), BF),
        vm((4, 6, 256, C), BF), vm((4, 3, 256, C), BF), vm((4, 3, 256, C), BF), vm((4, 3, 256, C), F32),
        vm((4, 3, 256, C), BF), vm((4, 8, 3, 32, C), BF), vm((4, 3, 32, C), BF), vm(blk, BF), vm(blk, BF), vm(blk, BF),
        vm((3, HEADS, T, KB), BF), vm((3, HEADS, T, KB), BF),
        dma((4,)), dma((4,)), dma((2,)), dma((2,)), dma((2, 4)), dma((2, 4)), dma((8,)), dma((8,)),
        dma((2,)), dma((2,)), dma((3,)), dma((3,)), dma((4,)), dma((4,)), dma((4,)), dma((4,)),
        dma((4, 8)), dma((4, 8)), dma((5,)), dma((5,)), dma((4,)), dma((4,)), dma((3,)),
    ]
    v = pl.BlockSpec(memory_space=pltpu.VMEM)
    hbm = pl.BlockSpec(memory_space=pl.ANY)
    shapes = (
        jax.ShapeDtypeStruct(blk, BF),
        jax.ShapeDtypeStruct(blk, F32),
        jax.ShapeDtypeStruct((HEADS, T, KB), BF),
    )
    gain, expo = gain.reshape(1, C), expo.reshape(1, ROWS)
    update, d_normed, bias_grad = pl.pallas_call(
        kernel,
        out_shape=shapes,
        in_specs=[v] * 8,
        out_specs=(hbm, hbm, hbm),
        scratch_shapes=scratch,
        compiler_params=pltpu.CompilerParams(
            collective_id=0, has_side_effects=True, vmem_limit_bytes=58 * 1024 * 1024
        ),
        cost_estimate=pl.CostEstimate(flops=8_000_000_000, bytes_accessed=4_000_000, transcendentals=6_300_000),
    )(tok, codes, expo, gain, w, wo, bias, ug)
    return pl.pallas_call(
        norm_back,
        out_shape=(shapes[0], shapes[0], shapes[2]),
        in_specs=[v] * 6,
        out_specs=(v, v, v),
        compiler_params=pltpu.CompilerParams(vmem_limit_bytes=58 * 1024 * 1024),
    )(codes, expo, gain, d_normed, update, bias_grad)


def solution(mesh):
    in_specs = (
        P("row", "col", None), P("row", "col"), P(), P(), P(), P(), P(None, "col", "row"), P("row", "col", None),
    )
    out_specs = (P("row", "col", None), P("row", "col", None), P(None, "col", "row"))
    return jax.shard_map(shards, mesh=mesh, in_specs=in_specs, out_specs=out_specs, check_vma=False)
```

```python
import jax
import jax.numpy as jnp
from jax import lax
from jax.experimental import pallas as pl
from jax.experimental.pallas import tpu as pltpu
from jax.sharding import PartitionSpec as P

MASKED = -1e30
EPSILON = 1e-05
F32 = jnp.float32
BF = jnp.bfloat16
NX, NZ = 4, 8
HEADS, DH, C, T = 4, 32, 128, 128
KB = 512
ROWS = 3


def nn(a, b):
    return lax.dot_general(a, b, (((1,), (0,)), ((), ())), preferred_element_type=F32)


def nt(a, b):
    return lax.dot_general(a, b, (((1,), (1,)), ((), ())), preferred_element_type=F32)


def split_nn(w, a):
    high = a.astype(BF)
    low = (a - high.astype(F32)).astype(BF)
    return nn(w, high) + nn(w, low)


def per_head(stat):
    return jnp.concatenate(
        [jnp.broadcast_to(stat[h : h + 1, :], (DH, T)) for h in range(HEADS)], axis=0
    )


def normalised(codes, expo, r):
    value = codes[r].astype(F32) * jnp.exp2(expo[0:1, r : r + 1].astype(F32))
    centered = value - jnp.mean(value, axis=-1, keepdims=True)
    inv_std = lax.rsqrt(jnp.mean(centered * centered, axis=-1, keepdims=True) + EPSILON)
    return centered * inv_std, inv_std


def norm_back(codes, expo, gain, d_normed, update_in, bias_in, update, pair_grad, bias_grad):
    update[...] = update_in[...]
    bias_grad[...] = bias_in[...]
    for r in range(ROWS):
        unit, inv_std = normalised(codes, expo, r)
        e = d_normed[r] * gain[...]
        pair_grad[r] = (
            inv_std
            * (e - jnp.mean(e, axis=-1, keepdims=True) - unit * jnp.mean(e * unit, axis=-1, keepdims=True))
        ).astype(BF)


def kernel(
    tok, codes, expo, gain, w, wo, bias, ug,
    update_hbm, normed_hbm, bias_hbm,
    update, bias_grad,
    wt, wot, nb, gates, dgated, kn, qt, dot, bias_g, bias_t, probs, s_ref, qbd, dos,
    m_st, l_st, a_st, vals, keys_t, gk, att_loc, st_loc, att_tx, att_rx, st_rx, back_tx, back_rx, stats, dgp,
    ds_ref, k_ref, vt_ref, gv_ref, acc, dq, kt, rxc, ytx, rxy, rsum, ztx, zrx, htx, frx, dqtx, dqrx, gtx, grx,
    bx_s, bx_r, ks_s, ks_r, zr_s, zr_r, sb_s, sb_r, pq_s, pq_r, ex_s, ex_r, kc_s, kc_r,
    ky_s, ky_r, zq_s, zq_r, f_s, f_r, g_s, g_r, o_s,
):
    row_id = lax.axis_index("row")
    col_id = lax.axis_index("col")
    yh, x = row_id // NX, lax.rem(row_id, NX)
    yl, z, c = col_id // 16, lax.rem(col_id, 16) // 2, lax.rem(col_id, 2)
    xs = [lax.rem(x + i, NX) for i in range(NX)]
    zs = [lax.rem(z + i, NZ) for i in range(NZ)]

    def dev(x_=x, yh_=yh, yl_=yl, z_=z, c_=c):
        return (yh_ * NX + x_, yl_ * 16 + z_ * 2 + c_)

    def rc(src, dst, send, recv, to):
        return pltpu.make_async_remote_copy(
            src_ref=src, dst_ref=dst, send_sem=send, recv_sem=recv,
            device_id=to, device_id_type=pl.DeviceIdType.MESH,
        )

    xp, xm, zp, zm = dev(x_=xs[1]), dev(x_=xs[3]), dev(z_=zs[1]), dev(z_=zs[7])
    sib = dev(c_=1 - c)
    ypart = dev(yl_=1 - yl)
    hpart = dev(yh_=1 - yh)
    cross = dev(yh_=1 - yh, yl_=1 - yl)
    is_home = yh == yl
    self_home = jnp.logical_and(is_home, jnp.logical_and(z // 4 == c, lax.rem(z, 2) == c))

    barrier = pltpu.get_barrier_semaphore()
    def greet(to):
        pl.semaphore_signal(barrier, inc=1, device_id=to, device_id_type=pl.DeviceIdType.MESH)

    for to in (xp, xm, sib, ypart, hpart, cross):
        greet(to)
    for i in range(1, 8):
        greet(dev(z_=zs[i]))
    for i in range(4):
        @pl.when(jnp.logical_not(jnp.logical_and(self_home, z // 2 == i)))
        def _():
            greet(dev(yh_=yl, yl_=yh, z_=2 * i + c, c_=z // 4))

        @pl.when(jnp.logical_not(jnp.logical_and(self_home, lax.rem(z, 4) == i)))
        def _():
            greet(dev(yh_=yl, yl_=yh, z_=4 * c + i, c_=lax.rem(z, 2)))


    gain_row = gain[...]
    for r in range(ROWS):
        nb[r] = (normalised(codes, expo, r)[0] * gain_row).astype(BF)

    pl.semaphore_wait(barrier, jnp.where(self_home, 19, 21))

    bias_p = rc(bias, bias_g.at[0], bx_s.at[0], bx_r.at[0], xp)
    bias_m = rc(bias, bias_g.at[1], bx_s.at[1], bx_r.at[1], xm)
    bias_fp = rc(bias_g.at[0, pl.ds(0, 2)], bias_g.at[2, pl.ds(0, 2)], bx_s.at[2], bx_r.at[2], xp)
    bias_fm = rc(bias_g.at[1, pl.ds(2, 2)], bias_g.at[2, pl.ds(2, 2)], bx_s.at[3], bx_r.at[3], xm)
    bias_p.start()
    bias_m.start()

    def key_at(zz, cc):
        return pl.ds(pl.multiple_of(zz * 256 + cc * 128, 128), 128)

    my_set = pl.ds(pl.multiple_of(yh * ROWS, ROWS), ROWS)
    key_send = [
        rc(nb, kn.at[pl.ds(yh * ROWS, ROWS), key_at(z, c)], ks_s.at[t], ks_r.at[yh], dev(yh_=yl, yl_=t))
        for t in range(2)
    ]
    for t in range(2):
        @pl.when(jnp.logical_not(jnp.logical_and(is_home, yl == t)))
        def _():
            key_send[t].start()

    @pl.when(is_home)
    def _():
        kn[pl.ds(yh * ROWS, ROWS), key_at(z, c), :] = nb[...]

    for q in range(4):
        wt[q * 128 : (q + 1) * 128, :] = w[:, q * 128 : (q + 1) * 128].astype(F32).T.astype(BF)
    wot[...] = wo[...].astype(F32).T.astype(BF)

    def set_of(ref, s):
        return ref.at[pl.ds(s * ROWS, ROWS)]

    for r in range(ROWS):
        n = nb[r]
        qt[yh * ROWS + r] = (nt(wt[0:128, :], n) * (DH ** -0.5)).astype(BF)
        gate = jax.nn.sigmoid(nt(wt[384:512, :], n))
        gates[r] = gate
        dg = nt(wo[...], ug[r])
        dgated[r] = dg
        dot[yh * ROWS + r] = (dg * gate).astype(BF)
    q_send = rc(set_of(qt, yh), set_of(qt, yh), pq_s.at[0], pq_r.at[0], hpart)
    d_send = rc(set_of(dot, yh), set_of(dot, yh), pq_s.at[1], pq_r.at[1], hpart)
    q_send.start()

    live = tok[...].reshape(1, 1)

    def prep(src, xb):
        for k in range(4):
            first = (yh * NX + xb) * KB + k * 128
            valid = first + lax.broadcasted_iota(jnp.int32, (128, 128), 0) < live
            for h in range(HEADS):
                tile = src[h, :, k * 128 : (k + 1) * 128].astype(F32).T
                bias_t[xb, k * 128 : (k + 1) * 128, h * 128 : (h + 1) * 128] = jnp.where(valid, tile, MASKED)

    qbd[...] = jnp.zeros_like(qbd)
    dos[...] = jnp.zeros_like(dos)
    prep(bias, x)

    for s in range(2):
        @pl.when(jnp.logical_not(jnp.logical_and(is_home, yh == s)))
        def _():
            rc(nb, kn.at[pl.ds(s * ROWS, ROWS), key_at(z, c)], ks_s.at[0], ks_r.at[s], sib).wait_recv()

    def block(zz, cc=c):
        return kn.at[:, key_at(zz, cc)]

    def half(zz, s):
        return kn.at[pl.ds(s * ROWS, ROWS), key_at(zz, c)]

    def up(i):
        src = block(zs[(8 - i) % 8]) if i < 3 else half(zs[5], 0)
        return rc(src, src, zr_s.at[0, i], zr_r.at[0, i], zp)

    def down(i):
        src = block(zs[i]) if i < 3 else half(zs[3], 1)
        return rc(src, src, zr_s.at[1, i], zr_r.at[1, i], zm)

    def to_sib(i):
        return rc(block(zs[i]), block(zs[i]), sb_s.at[i], sb_r.at[i], sib)

    def from_sib(i):
        return rc(block(zs[i], 1 - c), block(zs[i], 1 - c), sb_s.at[i], sb_r.at[i], sib)

    def up_in(i):
        dst = block(zs[7 - i]) if i < 3 else half(zs[4], 0)
        return rc(dst, dst, zr_s.at[0, i], zr_r.at[0, i], zp)

    def down_in(i):
        dst = block(zs[i + 1]) if i < 3 else half(zs[4], 1)
        return rc(dst, dst, zr_s.at[1, i], zr_r.at[1, i], zm)

    def ring_step(i):
        up_in(i).wait_recv()
        if i < 3:
            up(i + 1).start()
            to_sib(7 - i).start()
        down_in(i).wait_recv()
        if i < 3:
            down(i + 1).start()
            to_sib(i + 1).start()
        else:
            to_sib(4).start()

    up(0).start()
    down(0).start()
    to_sib(0).start()
    bias_p.wait_recv()
    bias_fp.start()
    bias_m.wait_recv()
    bias_fm.start()
    prep(bias_g.at[0], xs[3])
    prep(bias_g.at[1], xs[1])
    ring_step(0)

    zb = z // 2
    even = lax.rem(z, 2) == 0
    near = jnp.where(even, zb + 3, zb + 1)
    far = jnp.where(even, zb + 1, zb + 3)

    def arrive(phase):
        for i in ((0, 1, 7), (2, 6), (3, 5), (4,))[phase]:
            from_sib(i).wait_recv()

    for r in range(ROWS):
        vt_ref[r, 64:80, :] = jnp.ones((16, KB), BF)
        vt_ref[r, 144:160, :] = jnp.ones((16, KB), BF)

    def load_q(r, row):
        for h in range(HEADS):
            qbd[r, h * 32 : (h + 1) * 32, h * 128 : (h + 1) * 128] = qt[row, h * 32 : (h + 1) * 32, :]

    att_copy = rc(att_tx, att_rx, ex_s.at[0], ex_r.at[0], hpart)
    st_copy = rc(set_of(st_loc, 1 - yh), st_rx, ex_s.at[1], ex_r.at[1], hpart)
    back_copy = rc(back_tx, back_rx, ex_s.at[2], ex_r.at[2], hpart)

    def combine(side, r):
        m_all = [m_st[side * 4 + i, r] for i in range(4)]
        top_m = jnp.maximum(jnp.maximum(m_all[0], m_all[1]), jnp.maximum(m_all[2], m_all[3]))
        total = jnp.zeros((HEADS, T), F32)
        weighted = jnp.zeros((C, T), F32)
        for i in range(4):
            f = jnp.exp(m_all[i] - top_m)
            total = total + f * l_st[side * 4 + i, r]
            weighted = weighted + per_head(f) * a_st[side * 4 + i, r]
        st_loc[side * ROWS + r, 0:4, :] = top_m
        st_loc[side * ROWS + r, 4:8, :] = total
        return weighted

    def forward(u, carry):
        phase, second = u // 2, lax.rem(u, 2)
        side = lax.rem(jnp.where(phase == 3, 1 - yh, yh) + second, 2)
        xb = lax.rem(
            jnp.where(phase == 0, zb, jnp.where(phase == 1, near, jnp.where(phase == 2, far, zb + 2))), NX
        )
        sx = side * 4 + xb

        for i in range(4):
            @pl.when(u == 2 * i)
            def _():
                arrive(i)

        @pl.when(jnp.logical_and(second == 0, xb == xs[2]))
        def _():
            bias_fp.wait_recv()
            bias_fm.wait_recv()
            prep(bias_g.at[2], xs[2])

        for i in range(1, 4):
            @pl.when(u == 2 * i - 1)
            def _():
                ring_step(i)

        @pl.when(u == 1)
        def _():
            rc(set_of(qt, yh), set_of(qt, 1 - yh), pq_s.at[0], pq_r.at[0], hpart).wait_recv()
            d_send.start()

        for r in range(ROWS):
            row = side * ROWS + r
            load_q(r, row)
            n = kn[row, pl.ds(pl.multiple_of(xb * KB, KB), KB), :]
            kv = nn(n, w[:, 128:384]).astype(BF)
            kvt = nt(wt[128:384, :], n).astype(BF)
            k_ref[r] = kv[:, 0:128]
            vals[sx, r] = kv[:, 128:256]
            keys_t[sx, r] = kvt[0:128, :]
            vt_ref[r, 0:64, :] = kvt[128:192, :]
            vt_ref[r, 80:144, :] = kvt[192:256, :]

        items = [(r, hp) for r in range(ROWS) for hp in range(2)]
        tops = {}

        def score(t):
            r, hp = items[t]
            cols = slice(hp * 256, hp * 256 + 256)
            q2 = qbd[r, :, cols]
            top = None
            for i in range(4):
                rows = slice(i * 128, (i + 1) * 128)
                s = nn(k_ref[r, rows, :], q2) + bias_t[xb, rows, cols]
                s_ref[t % 3, rows, :] = s
                part = jnp.max(s.reshape(16, 8, 256), axis=0)
                top = part if top is None else jnp.maximum(top, part)
            tops[t] = jnp.max(top, axis=0, keepdims=True)

        def weigh(t):
            r, hp = items[t]
            cols = slice(hp * 256, hp * 256 + 256)
            for i in range(4):
                rows = slice(i * 128, (i + 1) * 128)
                probs[sx, r, rows, cols] = jnp.exp(s_ref[t % 3, rows, :] - tops[t]).astype(BF)

        def attend(t):
            r, hp = items[t]
            cols = slice(hp * 256, hp * 256 + 256)
            a = nn(vt_ref[r, hp * 80 : hp * 80 + 80, :], probs[sx, r, :, cols])
            for j in range(2):
                h = hp * 2 + j
                lanes = slice(j * 128, (j + 1) * 128)
                m_st[sx, r, h : h + 1, :] = tops[t][:, lanes]
                l_st[sx, r, h : h + 1, :] = a[64:65, lanes]
                a_st[sx, r, h * 32 : (h + 1) * 32, :] = a[j * 32 : (j + 1) * 32, lanes]

        for t in range(8):
            if t < 6:
                score(t)
            if 1 <= t < 7:
                weigh(t - 1)
            if t >= 2:
                attend(t - 2)

        @pl.when(u == 6)
        def _():
            for r in range(ROWS):
                att_tx[r] = combine(1 - yh, r).astype(BF)
            att_copy.start()
            st_copy.start()

        return carry

    lax.fori_loop(0, 8, forward, 0)

    for row in range(6):
        load_q(0, row)
        gk[row] = nn(w[:, 128:256], qbd[0]).astype(BF)

    for r in range(ROWS):
        att_loc[yh * ROWS + r] = combine(yh, r)
    att_copy.wait_recv()
    st_copy.wait_recv()
    for r in range(ROWS):
        mine = yh * ROWS + r
        ma, la = st_loc[mine, 0:4, :], st_loc[mine, 4:8, :]
        mb, lb = st_rx[r, 0:4, :], st_rx[r, 4:8, :]
        top_m = jnp.maximum(ma, mb)
        fa, fb = jnp.exp(ma - top_m), jnp.exp(mb - top_m)
        total = fa * la + fb * lb
        attended = (per_head(fa) * att_loc[mine] + per_head(fb) * att_rx[r].astype(F32)) / per_head(total)
        gate = gates[r]
        product = dot[mine].astype(F32) * attended
        lse = top_m + jnp.log(total)
        stats[mine, 0:4, :] = lse
        back_tx[r, 0:4, :] = lse
        for h in range(HEADS):
            delta = jnp.sum(product[h * 32 : (h + 1) * 32, :], axis=0, keepdims=True)
            stats[mine, 4 + h : 5 + h, :] = delta
            back_tx[r, 4 + h : 5 + h, :] = delta
        att_loc[mine] = attended
    back_copy.start()
    for r in range(ROWS):
        attended = att_loc[yh * ROWS + r]
        gate = gates[r]
        dgp[r] = dgated[r] * attended * gate * (1.0 - gate)
        update[r] = nn(wot[...], (gate * attended).astype(BF)).T.astype(BF)
    update_out = pltpu.make_async_copy(update, update_hbm, o_s.at[0])
    update_out.start()
    rc(set_of(dot, yh), set_of(dot, 1 - yh), pq_s.at[1], pq_r.at[1], hpart).wait_recv()
    dq[...] = jnp.zeros_like(dq)

    def core_half(xb, cc):
        return pl.ds(pl.multiple_of(xb * KB + cc * 256, 256), 256)

    def z_part(zz):
        return pl.ds(pl.multiple_of(zz * 32, 32), 32)

    def core_copy(xb):
        return rc(kt.at[:, core_half(xb, 1 - c)], rxc.at[xb], kc_s.at[xb], kc_r.at[xb], sib)

    def y_copy(xb):
        return rc(ytx.at[xb], rxy.at[xb], ky_s.at[xb], ky_r.at[xb], ypart)

    def z_copy(xb, i):
        return rc(
            ztx.at[xb, :, z_part(zs[i])], zrx.at[xb, i], zq_s.at[xb, i], zq_r.at[xb, i], dev(z_=zs[i])
        )

    def own_copy(xb):
        part = lax.rem(z, 4)
        return rc(
            htx.at[xb], frx.at[:, z_part(part)], f_s.at[xb], f_r.at[part],
            dev(yh_=yl, yl_=yh, z_=2 * xb + c, c_=z // 4),
        )

    def y_stage(xb):
        core_copy(xb).wait_recv()
        for r in range(ROWS):
            theirs, ours = (1 - yl) * ROWS + r, yl * ROWS + r
            ytx[xb, r] = (kt[theirs, core_half(xb, c), :].astype(F32) + rxc[xb, theirs].astype(F32)).astype(BF)
        y_copy(xb).start()
        for r in range(ROWS):
            ours = yl * ROWS + r
            rsum[xb, r] = kt[ours, core_half(xb, c), :].astype(F32) + rxc[xb, ours].astype(F32)

    def z_stage(xb):
        y_copy(xb).wait_recv()
        for r in range(ROWS):
            total = rsum[xb, r] + rxy[xb, r].astype(F32)
            rsum[xb, r] = total
            ztx[xb, r] = total.astype(BF)
        for i in (4, 3, 5, 2, 6, 1, 7):
            z_copy(xb, i).start()

    def home_stage(xb):
        total = rsum[xb, :, z_part(z), :]
        for i in range(1, 8):
            z_copy(xb, i).wait_recv()
            total = total + zrx[xb, i].astype(F32)
        htx[xb] = total.astype(BF)
        stays = jnp.logical_and(self_home, z // 2 == xb)

        @pl.when(stays)
        def _():
            frx[:, z_part(lax.rem(z, 4)), :] = htx[xb]

        @pl.when(jnp.logical_not(stays))
        def _():
            own_copy(xb).start()

    g_half_p = rc(gtx.at[0, pl.ds(0, 2)], grx.at[0, pl.ds(0, 2)], g_s.at[0], g_r.at[0], xp)
    g_half_m = rc(gtx.at[0, pl.ds(2, 2)], grx.at[0, pl.ds(2, 2)], g_s.at[1], g_r.at[1], xm)
    g_p = rc(gtx.at[1], grx.at[1], g_s.at[2], g_r.at[2], xp)
    g_m = rc(gtx.at[2], grx.at[2], g_s.at[3], g_r.at[3], xm)

    def turned(h, k):
        return acc[k * 128 : (k + 1) * 128, h * 128 : (h + 1) * 128].T

    def bias_stage(step):
        if step == 1:
            g_half_p.wait_recv()
        if step == 2:
            g_half_m.wait_recv()
        if step == 3:
            g_p.wait_recv()
            g_m.wait_recv()
        for h in range(HEADS):
            for k in range(4):
                lanes = slice(k * 128, (k + 1) * 128)
                tile = turned(h, k)
                if (step == 1 and h < 2) or (step == 2 and h >= 2):
                    tile = tile + grx[0, h, :, lanes].astype(F32)
                if step == 3:
                    tile = tile + grx[1, h, :, lanes].astype(F32) + grx[2, h, :, lanes].astype(F32)
                    bias_grad[h, :, lanes] = tile.astype(BF)
                else:
                    gtx[step, h, :, lanes] = tile.astype(BF)
        if step == 0:
            g_half_p.start()
            g_half_m.start()
        if step == 1:
            g_p.start()
        if step == 2:
            g_m.start()

    def backward(u, carry):
        step, second = u // 2, lax.rem(u, 2)
        side = lax.rem(yh + second, 2)
        xb = lax.rem(x + jnp.where(step == 0, 2, jnp.where(step == 1, 1, jnp.where(step == 2, 3, 0))), NX)
        sx = side * 4 + xb

        @pl.when(u == 1)
        def _():
            back_copy.wait_recv()
            for r in range(ROWS):
                stats[(1 - yh) * ROWS + r] = back_rx[r]

        @pl.when(second == 0)
        def _():
            acc[...] = jnp.zeros_like(acc)

        deltas, gvs = [], []
        for r in range(ROWS):
            row = side * ROWS + r
            st = stats[row]
            f = jnp.exp(m_st[sx, r] - st[0:4, :])
            dls = f * st[4:8, :]
            deltas.append([jnp.concatenate([dls[h : h + 1, :], dls[h + 1 : h + 2, :]], axis=1) for h in (0, 2)])
            for h in range(HEADS):
                rows = slice(h * 32, (h + 1) * 32)
                dos[r, rows, h * 128 : (h + 1) * 128] = (
                    dot[row, rows, :].astype(F32) * f[h : h + 1, :]
                ).astype(BF)
        for r in range(ROWS):
            gv_ref[r] = nn(w[:, 256:384], dos[r]).astype(BF)
        for hp in range(2):
            cols = slice(hp * 256, hp * 256 + 256)
            for i in range(4):
                rows = slice(i * 128, (i + 1) * 128)
                total = acc[rows, cols]
                for r in range(ROWS):
                    d_prob = nn(vals[sx, r, rows, :], dos[r, :, cols]) - deltas[r][hp]
                    d_score = probs[sx, r, rows, cols].astype(F32) * d_prob
                    total = total + d_score
                    ds_ref[r, rows, cols] = d_score.astype(BF)
                acc[rows, cols] = total
            for r in range(ROWS):
                row = side * ROWS + r
                d_query = nn(keys_t[sx, r, hp * 64 : hp * 64 + 64, :], ds_ref[r, :, cols])
                for j in range(2):
                    rows = slice((hp * 2 + j) * 32, (hp * 2 + j + 1) * 32)
                    dq[row, rows, :] = dq[row, rows, :] + d_query[j * 32 : (j + 1) * 32, j * 128 : (j + 1) * 128]
        for r in range(ROWS):
            row = side * ROWS + r
            kt[row, pl.ds(pl.multiple_of(xb * KB, KB), KB), :] = (
                nt(ds_ref[r], gk[row]) + nt(probs[sx, r], gv_ref[r])
            ).astype(BF)

        def block_at(back):
            return lax.rem(x + jnp.where(step == back, 2, jnp.where(step == back + 1, 1, 3)), NX)

        @pl.when(jnp.logical_and(step >= 1, second == 0))
        def _():
            y_stage(block_at(1))

        @pl.when(jnp.logical_and(step >= 2, second == 0))
        def _():
            home_stage(block_at(2))

        @pl.when(second == 1)
        def _():
            core_copy(xb).start()

        @pl.when(jnp.logical_and(step >= 1, second == 1))
        def _():
            z_stage(block_at(1))

        for s in range(3):
            @pl.when(u == 2 * s + 1)
            def _():
                bias_stage(s)

        return carry

    lax.fori_loop(0, 8, backward, 0)

    for r in range(ROWS):
        dqtx[r] = dq[(1 - yh) * ROWS + r].astype(BF)
    dq_copy = rc(dqtx, dqrx, f_s.at[4], f_r.at[4], hpart)
    dq_copy.start()
    y_stage(x)
    dq_copy.wait_recv()
    for r in range(ROWS):
        d_query = (dq[yh * ROWS + r] + dqrx[r].astype(F32)) * (DH ** -0.5)
        unit_t = split_nn(w[:, 0:128], d_query) + split_nn(w[:, 384:512], dgp[r])
        dgated[r] = unit_t.T
    z_stage(x)
    bias_stage(3)
    bias_out = pltpu.make_async_copy(bias_grad, bias_hbm, o_s.at[1])
    bias_out.start()
    home_stage(xs[3])
    home_stage(x)
    for j in range(4):
        @pl.when(jnp.logical_not(jnp.logical_and(self_home, lax.rem(z, 4) == j)))
        def _():
            rc(htx.at[0], frx.at[:, pl.ds(j * 32, 32)], f_s.at[0], f_r.at[j], sib).wait_recv()
    for r in range(ROWS):
        dgated[r] = dgated[r] + frx[r].astype(F32)
    normed_out = pltpu.make_async_copy(dgated, normed_hbm, o_s.at[2])
    normed_out.start()

    for copy in (bias_p, bias_m, bias_fp, bias_fm, q_send, d_send, att_copy, st_copy, back_copy, dq_copy,
                 g_half_p, g_half_m, g_p, g_m):
        copy.wait_send()
    for t in range(2):
        @pl.when(jnp.logical_not(jnp.logical_and(is_home, yl == t)))
        def _():
            key_send[t].wait_send()
    for i in range(4):
        up(i).wait_send()
        down(i).wait_send()
        core_copy(i).wait_send()
        y_copy(i).wait_send()
        for j in range(1, 8):
            z_copy(i, j).wait_send()

        @pl.when(jnp.logical_not(jnp.logical_and(self_home, z // 2 == i)))
        def _():
            own_copy(i).wait_send()

    for i in range(8):
        to_sib(i).wait_send()

    update_out.wait()
    bias_out.wait()
    normed_out.wait()


def shards(codes, expo, tok, gain, w, wo, bias, ug):
    vm = pltpu.VMEM
    dma = pltpu.SemaphoreType.DMA
    blk = (ROWS, T, C)
    scratch = [
        vm(blk, BF), vm((HEADS, T, KB), BF),
        vm((512, C), BF), vm((C, C), BF), vm(blk, BF), vm(blk, F32), vm(blk, F32),
        vm((6, 2048, C), BF), vm((6, C, T), BF), vm((6, C, T), BF), vm((3, HEADS, T, KB), BF),
        vm((4, KB, 512), F32), vm((8, 3, KB, 512), BF), vm((3, KB, 256), F32), vm((3, C, 512), BF),
        vm((3, C, 512), BF),
        vm((8, 3, HEADS, T), F32), vm((8, 3, HEADS, T), F32), vm((8, 3, C, T), F32),
        vm((8, 3, KB, C), BF), vm((8, 3, C, KB), BF), vm((6, C, 512), BF), vm((6, C, T), F32), vm((6, 8, T), F32),
        vm(blk, BF), vm(blk, BF), vm((ROWS, 8, T), F32), vm((ROWS, 8, T), F32), vm((ROWS, 8, T), F32),
        vm((6, 8, T), F32), vm(blk, F32),
        vm((3, KB, 512), BF), vm((3, KB, C), BF), vm((3, 160, KB), BF), vm((3, C, 512), BF), vm((KB, 512), F32),
        vm((6, C, T), F32), vm((6, 2048, C), BF),
        vm((4, 6, 256, C), BF), vm((4, 3, 256, C), BF), vm((4, 3, 256, C), BF), vm((4, 3, 256, C), F32),
        vm((4, 3, 256, C), BF), vm((4, 8, 3, 32, C), BF), vm((4, 3, 32, C), BF), vm(blk, BF), vm(blk, BF), vm(blk, BF),
        vm((3, HEADS, T, KB), BF), vm((3, HEADS, T, KB), BF),
        dma((4,)), dma((4,)), dma((2,)), dma((2,)), dma((2, 4)), dma((2, 4)), dma((8,)), dma((8,)),
        dma((2,)), dma((2,)), dma((3,)), dma((3,)), dma((4,)), dma((4,)), dma((4,)), dma((4,)),
        dma((4, 8)), dma((4, 8)), dma((5,)), dma((5,)), dma((4,)), dma((4,)), dma((3,)),
    ]
    v = pl.BlockSpec(memory_space=pltpu.VMEM)
    hbm = pl.BlockSpec(memory_space=pl.ANY)
    shapes = (
        jax.ShapeDtypeStruct(blk, BF),
        jax.ShapeDtypeStruct(blk, F32),
        jax.ShapeDtypeStruct((HEADS, T, KB), BF),
    )
    gain, expo = gain.reshape(1, C), expo.reshape(1, ROWS)
    update, d_normed, bias_grad = pl.pallas_call(
        kernel,
        out_shape=shapes,
        in_specs=[v] * 8,
        out_specs=(hbm, hbm, hbm),
        scratch_shapes=scratch,
        compiler_params=pltpu.CompilerParams(
            collective_id=0, has_side_effects=True, vmem_limit_bytes=58 * 1024 * 1024
        ),
        cost_estimate=pl.CostEstimate(flops=8_000_000_000, bytes_accessed=4_000_000, transcendentals=6_300_000),
    )(tok, codes, expo, gain, w, wo, bias, ug)
    return pl.pallas_call(
        norm_back,
        out_shape=(shapes[0], shapes[0], shapes[2]),
        in_specs=[v] * 6,
        out_specs=(v, v, v),
        compiler_params=pltpu.CompilerParams(vmem_limit_bytes=58 * 1024 * 1024),
    )(codes, expo, gain, d_normed, update, bias_grad)


def solution(mesh):
    in_specs = (
        P("row", "col", None), P("row", "col"), P(), P(), P(), P(), P(None, "col", "row"), P("row", "col", None),
    )
    out_specs = (P("row", "col", None), P("row", "col", None), P(None, "col", "row"))
    return jax.shard_map(shards, mesh=mesh, in_specs=in_specs, out_specs=out_specs, check_vma=False)
```

```python
import jax
import jax.numpy as jnp
from jax import lax
from jax.experimental import pallas as pl
from jax.experimental.pallas import tpu as pltpu
from jax.sharding import PartitionSpec as P

MASKED = -1e30
EPSILON = 1e-05
F32 = jnp.float32
BF = jnp.bfloat16
NX, NZ = 4, 8
HEADS, DH, C, T = 4, 32, 128, 128
KB = 512
ROWS = 3


def nn(a, b):
    return lax.dot_general(a, b, (((1,), (0,)), ((), ())), preferred_element_type=F32)


def nt(a, b):
    return lax.dot_general(a, b, (((1,), (1,)), ((), ())), preferred_element_type=F32)


def split_nn(w, a):
    high = a.astype(BF)
    low = (a - high.astype(F32)).astype(BF)
    return nn(w, high) + nn(w, low)


def per_head(stat):
    return jnp.concatenate(
        [jnp.broadcast_to(stat[h : h + 1, :], (DH, T)) for h in range(HEADS)], axis=0
    )


def normalised(codes, expo, r):
    value = codes[r].astype(F32) * jnp.exp2(expo[0:1, r : r + 1].astype(F32))
    centered = value - jnp.mean(value, axis=-1, keepdims=True)
    inv_std = lax.rsqrt(jnp.mean(centered * centered, axis=-1, keepdims=True) + EPSILON)
    return centered * inv_std, inv_std


def norm_back(codes, expo, gain, d_normed, update_in, bias_in, update, pair_grad, bias_grad):
    update[...] = update_in[...]
    bias_grad[...] = bias_in[...]
    for r in range(ROWS):
        unit, inv_std = normalised(codes, expo, r)
        e = d_normed[r] * gain[...]
        pair_grad[r] = (
            inv_std
            * (e - jnp.mean(e, axis=-1, keepdims=True) - unit * jnp.mean(e * unit, axis=-1, keepdims=True))
        ).astype(BF)


def kernel(
    tok, codes, expo, gain, w, wo, bias, ug,
    update_hbm, normed_hbm, bias_hbm,
    update, bias_grad,
    wt, wot, nb, gates, dgated, kn, qt, dot, bias_g, bias_t, probs, s_ref, qbd, dos,
    m_st, l_st, a_st, vals, keys_t, gk, att_loc, st_loc, att_tx, att_rx, st_rx, back_tx, back_rx, stats, dgp,
    ds_ref, k_ref, vt_ref, gv_ref, turned, dq, kt, rxc, ytx, rxy, rsum, ztx, zrx, htx, frx, dqtx, dqrx, gtx, grx,
    bx_s, bx_r, ks_s, ks_r, zr_s, zr_r, sb_s, sb_r, pq_s, pq_r, ex_s, ex_r, kc_s, kc_r,
    ky_s, ky_r, zq_s, zq_r, f_s, f_r, g_s, g_r, o_s,
):
    row_id = lax.axis_index("row")
    col_id = lax.axis_index("col")
    yh, x = row_id // NX, lax.rem(row_id, NX)
    yl, z, c = col_id // 16, lax.rem(col_id, 16) // 2, lax.rem(col_id, 2)
    xs = [lax.rem(x + i, NX) for i in range(NX)]
    zs = [lax.rem(z + i, NZ) for i in range(NZ)]

    def dev(x_=x, yh_=yh, yl_=yl, z_=z, c_=c):
        return (yh_ * NX + x_, yl_ * 16 + z_ * 2 + c_)

    def rc(src, dst, send, recv, to):
        return pltpu.make_async_remote_copy(
            src_ref=src, dst_ref=dst, send_sem=send, recv_sem=recv,
            device_id=to, device_id_type=pl.DeviceIdType.MESH,
        )

    xp, xm, zp, zm = dev(x_=xs[1]), dev(x_=xs[3]), dev(z_=zs[1]), dev(z_=zs[7])
    sib = dev(c_=1 - c)
    ypart = dev(yl_=1 - yl)
    hpart = dev(yh_=1 - yh)
    cross = dev(yh_=1 - yh, yl_=1 - yl)
    is_home = yh == yl
    self_home = jnp.logical_and(is_home, jnp.logical_and(z // 4 == c, lax.rem(z, 2) == c))

    barrier = pltpu.get_barrier_semaphore()
    def greet(to):
        pl.semaphore_signal(barrier, inc=1, device_id=to, device_id_type=pl.DeviceIdType.MESH)

    for to in (xp, xm, sib, ypart, hpart, cross):
        greet(to)
    for i in range(1, 8):
        greet(dev(z_=zs[i]))
    for i in range(4):
        @pl.when(jnp.logical_not(jnp.logical_and(self_home, z // 2 == i)))
        def _():
            greet(dev(yh_=yl, yl_=yh, z_=2 * i + c, c_=z // 4))

        @pl.when(jnp.logical_not(jnp.logical_and(self_home, lax.rem(z, 4) == i)))
        def _():
            greet(dev(yh_=yl, yl_=yh, z_=4 * c + i, c_=lax.rem(z, 2)))


    gain_row = gain[...]
    for r in range(ROWS):
        nb[r] = (normalised(codes, expo, r)[0] * gain_row).astype(BF)

    pl.semaphore_wait(barrier, jnp.where(self_home, 19, 21))

    bias_p = rc(bias, bias_g.at[0], bx_s.at[0], bx_r.at[0], xp)
    bias_m = rc(bias, bias_g.at[1], bx_s.at[1], bx_r.at[1], xm)
    bias_fp = rc(bias_g.at[0, pl.ds(0, 2)], bias_g.at[2, pl.ds(0, 2)], bx_s.at[2], bx_r.at[2], xp)
    bias_fm = rc(bias_g.at[1, pl.ds(2, 2)], bias_g.at[2, pl.ds(2, 2)], bx_s.at[3], bx_r.at[3], xm)
    bias_p.start()
    bias_m.start()

    def key_at(zz, cc):
        return pl.ds(pl.multiple_of(zz * 256 + cc * 128, 128), 128)

    my_set = pl.ds(pl.multiple_of(yh * ROWS, ROWS), ROWS)
    key_send = [
        rc(nb, kn.at[pl.ds(yh * ROWS, ROWS), key_at(z, c)], ks_s.at[t], ks_r.at[yh], dev(yh_=yl, yl_=t))
        for t in range(2)
    ]
    for t in range(2):
        @pl.when(jnp.logical_not(jnp.logical_and(is_home, yl == t)))
        def _():
            key_send[t].start()

    @pl.when(is_home)
    def _():
        kn[pl.ds(yh * ROWS, ROWS), key_at(z, c), :] = nb[...]

    for q in range(4):
        wt[q * 128 : (q + 1) * 128, :] = w[:, q * 128 : (q + 1) * 128].astype(F32).T.astype(BF)
    wot[...] = wo[...].astype(F32).T.astype(BF)

    def set_of(ref, s):
        return ref.at[pl.ds(s * ROWS, ROWS)]

    for r in range(ROWS):
        n = nb[r]
        qt[yh * ROWS + r] = (nt(wt[0:128, :], n) * (DH ** -0.5)).astype(BF)
        gate = jax.nn.sigmoid(nt(wt[384:512, :], n))
        gates[r] = gate
        dg = nt(wo[...], ug[r])
        dgated[r] = dg
        dot[yh * ROWS + r] = (dg * gate).astype(BF)
    q_send = rc(set_of(qt, yh), set_of(qt, yh), pq_s.at[0], pq_r.at[0], hpart)
    d_send = rc(set_of(dot, yh), set_of(dot, yh), pq_s.at[1], pq_r.at[1], hpart)
    q_send.start()

    live = tok[...].reshape(1, 1)

    def prep(src, xb):
        for k in range(4):
            first = (yh * NX + xb) * KB + k * 128
            valid = first + lax.broadcasted_iota(jnp.int32, (128, 128), 0) < live
            for h in range(HEADS):
                tile = src[h, :, k * 128 : (k + 1) * 128].astype(F32).T
                bias_t[xb, k * 128 : (k + 1) * 128, h * 128 : (h + 1) * 128] = jnp.where(valid, tile, MASKED)

    qbd[...] = jnp.zeros_like(qbd)
    dos[...] = jnp.zeros_like(dos)
    prep(bias, x)

    for s in range(2):
        @pl.when(jnp.logical_not(jnp.logical_and(is_home, yh == s)))
        def _():
            rc(nb, kn.at[pl.ds(s * ROWS, ROWS), key_at(z, c)], ks_s.at[0], ks_r.at[s], sib).wait_recv()

    def block(zz, cc=c):
        return kn.at[:, key_at(zz, cc)]

    def half(zz, s):
        return kn.at[pl.ds(s * ROWS, ROWS), key_at(zz, c)]

    def up(i):
        src = block(zs[(8 - i) % 8]) if i < 3 else half(zs[5], 0)
        return rc(src, src, zr_s.at[0, i], zr_r.at[0, i], zp)

    def down(i):
        src = block(zs[i]) if i < 3 else half(zs[3], 1)
        return rc(src, src, zr_s.at[1, i], zr_r.at[1, i], zm)

    def to_sib(i):
        return rc(block(zs[i]), block(zs[i]), sb_s.at[i], sb_r.at[i], sib)

    def from_sib(i):
        return rc(block(zs[i], 1 - c), block(zs[i], 1 - c), sb_s.at[i], sb_r.at[i], sib)

    def up_in(i):
        dst = block(zs[7 - i]) if i < 3 else half(zs[4], 0)
        return rc(dst, dst, zr_s.at[0, i], zr_r.at[0, i], zp)

    def down_in(i):
        dst = block(zs[i + 1]) if i < 3 else half(zs[4], 1)
        return rc(dst, dst, zr_s.at[1, i], zr_r.at[1, i], zm)

    def ring_step(i):
        up_in(i).wait_recv()
        if i < 3:
            up(i + 1).start()
            to_sib(7 - i).start()
        down_in(i).wait_recv()
        if i < 3:
            down(i + 1).start()
            to_sib(i + 1).start()
        else:
            to_sib(4).start()

    up(0).start()
    down(0).start()
    to_sib(0).start()
    bias_p.wait_recv()
    bias_fp.start()
    bias_m.wait_recv()
    bias_fm.start()
    prep(bias_g.at[0], xs[3])
    prep(bias_g.at[1], xs[1])
    ring_step(0)

    zb = z // 2
    even = lax.rem(z, 2) == 0
    near = jnp.where(even, zb + 3, zb + 1)
    far = jnp.where(even, zb + 1, zb + 3)

    def arrive(phase):
        for i in ((0, 1, 7), (2, 6), (3, 5), (4,))[phase]:
            from_sib(i).wait_recv()

    for r in range(ROWS):
        vt_ref[r, 64:80, :] = jnp.ones((16, KB), BF)
        vt_ref[r, 144:160, :] = jnp.ones((16, KB), BF)

    def load_q(r, row):
        for h in range(HEADS):
            qbd[r, h * 32 : (h + 1) * 32, h * 128 : (h + 1) * 128] = qt[row, h * 32 : (h + 1) * 32, :]

    att_copy = rc(att_tx, att_rx, ex_s.at[0], ex_r.at[0], hpart)
    st_copy = rc(set_of(st_loc, 1 - yh), st_rx, ex_s.at[1], ex_r.at[1], hpart)
    back_copy = rc(back_tx, back_rx, ex_s.at[2], ex_r.at[2], hpart)

    def combine(side, r):
        m_all = [m_st[side * 4 + i, r] for i in range(4)]
        top_m = jnp.maximum(jnp.maximum(m_all[0], m_all[1]), jnp.maximum(m_all[2], m_all[3]))
        total = jnp.zeros((HEADS, T), F32)
        weighted = jnp.zeros((C, T), F32)
        for i in range(4):
            f = jnp.exp(m_all[i] - top_m)
            total = total + f * l_st[side * 4 + i, r]
            weighted = weighted + per_head(f) * a_st[side * 4 + i, r]
        st_loc[side * ROWS + r, 0:4, :] = top_m
        st_loc[side * ROWS + r, 4:8, :] = total
        return weighted

    def forward(u, carry):
        phase, second = u // 2, lax.rem(u, 2)
        side = lax.rem(jnp.where(phase == 3, 1 - yh, yh) + second, 2)
        xb = lax.rem(
            jnp.where(phase == 0, zb, jnp.where(phase == 1, near, jnp.where(phase == 2, far, zb + 2))), NX
        )
        sx = side * 4 + xb

        for i in range(4):
            @pl.when(u == 2 * i)
            def _():
                arrive(i)

        @pl.when(jnp.logical_and(second == 0, xb == xs[2]))
        def _():
            bias_fp.wait_recv()
            bias_fm.wait_recv()
            prep(bias_g.at[2], xs[2])

        for i in range(1, 4):
            @pl.when(u == 2 * i - 1)
            def _():
                ring_step(i)

        @pl.when(u == 1)
        def _():
            rc(set_of(qt, yh), set_of(qt, 1 - yh), pq_s.at[0], pq_r.at[0], hpart).wait_recv()
            d_send.start()

        for r in range(ROWS):
            row = side * ROWS + r
            load_q(r, row)
            n = kn[row, pl.ds(pl.multiple_of(xb * KB, KB), KB), :]
            kv = nn(n, w[:, 128:384]).astype(BF)
            kvt = nt(wt[128:384, :], n).astype(BF)
            k_ref[r] = kv[:, 0:128]
            vals[sx, r] = kv[:, 128:256]
            keys_t[sx, r] = kvt[0:128, :]
            vt_ref[r, 0:64, :] = kvt[128:192, :]
            vt_ref[r, 80:144, :] = kvt[192:256, :]

        items = [(r, hp) for r in range(ROWS) for hp in range(2)]
        tops = {}

        def score(t):
            r, hp = items[t]
            cols = slice(hp * 256, hp * 256 + 256)
            q2 = qbd[r, :, cols]
            top = None
            for i in range(4):
                rows = slice(i * 128, (i + 1) * 128)
                s = nn(k_ref[r, rows, :], q2) + bias_t[xb, rows, cols]
                s_ref[t % 3, rows, :] = s
                part = jnp.max(s.reshape(16, 8, 256), axis=0)
                top = part if top is None else jnp.maximum(top, part)
            tops[t] = jnp.max(top, axis=0, keepdims=True)

        def weigh(t):
            r, hp = items[t]
            cols = slice(hp * 256, hp * 256 + 256)
            for i in range(4):
                rows = slice(i * 128, (i + 1) * 128)
                probs[sx, r, rows, cols] = jnp.exp(s_ref[t % 3, rows, :] - tops[t]).astype(BF)

        def attend(t):
            r, hp = items[t]
            cols = slice(hp * 256, hp * 256 + 256)
            a = nn(vt_ref[r, hp * 80 : hp * 80 + 80, :], probs[sx, r, :, cols])
            for j in range(2):
                h = hp * 2 + j
                lanes = slice(j * 128, (j + 1) * 128)
                m_st[sx, r, h : h + 1, :] = tops[t][:, lanes]
                l_st[sx, r, h : h + 1, :] = a[64:65, lanes]
                a_st[sx, r, h * 32 : (h + 1) * 32, :] = a[j * 32 : (j + 1) * 32, lanes]

        for t in range(8):
            if t < 6:
                score(t)
            if 1 <= t < 7:
                weigh(t - 1)
            if t >= 2:
                attend(t - 2)

        @pl.when(u == 6)
        def _():
            for r in range(ROWS):
                att_tx[r] = combine(1 - yh, r).astype(BF)
            att_copy.start()
            st_copy.start()

        return carry

    lax.fori_loop(0, 8, forward, 0)

    for r in range(ROWS):
        att_loc[yh * ROWS + r] = combine(yh, r)
    att_copy.wait_recv()
    st_copy.wait_recv()
    for r in range(ROWS):
        mine = yh * ROWS + r
        ma, la = st_loc[mine, 0:4, :], st_loc[mine, 4:8, :]
        mb, lb = st_rx[r, 0:4, :], st_rx[r, 4:8, :]
        top_m = jnp.maximum(ma, mb)
        fa, fb = jnp.exp(ma - top_m), jnp.exp(mb - top_m)
        total = fa * la + fb * lb
        attended = (per_head(fa) * att_loc[mine] + per_head(fb) * att_rx[r].astype(F32)) / per_head(total)
        gate = gates[r]
        product = dot[mine].astype(F32) * attended
        lse = top_m + jnp.log(total)
        stats[mine, 0:4, :] = lse
        back_tx[r, 0:4, :] = lse
        for h in range(HEADS):
            delta = jnp.sum(product[h * 32 : (h + 1) * 32, :], axis=0, keepdims=True)
            stats[mine, 4 + h : 5 + h, :] = delta
            back_tx[r, 4 + h : 5 + h, :] = delta
        att_loc[mine] = attended
    back_copy.start()
    for r in range(ROWS):
        attended = att_loc[yh * ROWS + r]
        gate = gates[r]
        dgp[r] = dgated[r] * attended * gate * (1.0 - gate)
        update[r] = nn(wot[...], (gate * attended).astype(BF)).T.astype(BF)
    update_out = pltpu.make_async_copy(update, update_hbm, o_s.at[0])
    update_out.start()
    for row in range(6):
        load_q(0, row)
        gk[row] = nn(w[:, 128:256], qbd[0]).astype(BF)

    rc(set_of(dot, yh), set_of(dot, 1 - yh), pq_s.at[1], pq_r.at[1], hpart).wait_recv()
    back_copy.wait_recv()
    for r in range(ROWS):
        stats[(1 - yh) * ROWS + r] = back_rx[r]
    dq[...] = jnp.zeros_like(dq)

    def core_half(xb, cc):
        return pl.ds(pl.multiple_of(xb * KB + cc * 256, 256), 256)

    def z_part(zz):
        return pl.ds(pl.multiple_of(zz * 32, 32), 32)

    def core_copy(xb):
        return rc(kt.at[:, core_half(xb, 1 - c)], rxc.at[xb], kc_s.at[xb], kc_r.at[xb], sib)

    def y_copy(xb):
        return rc(ytx.at[xb], rxy.at[xb], ky_s.at[xb], ky_r.at[xb], ypart)

    def z_copy(xb, i):
        return rc(
            ztx.at[xb, :, z_part(zs[i])], zrx.at[xb, i], zq_s.at[xb, i], zq_r.at[xb, i], dev(z_=zs[i])
        )

    def own_copy(xb):
        part = lax.rem(z, 4)
        return rc(
            htx.at[xb], frx.at[:, z_part(part)], f_s.at[xb], f_r.at[part],
            dev(yh_=yl, yl_=yh, z_=2 * xb + c, c_=z // 4),
        )

    def y_stage(xb):
        core_copy(xb).wait_recv()
        for r in range(ROWS):
            theirs, ours = (1 - yl) * ROWS + r, yl * ROWS + r
            ytx[xb, r] = (kt[theirs, core_half(xb, c), :].astype(F32) + rxc[xb, theirs].astype(F32)).astype(BF)
        y_copy(xb).start()
        for r in range(ROWS):
            ours = yl * ROWS + r
            rsum[xb, r] = kt[ours, core_half(xb, c), :].astype(F32) + rxc[xb, ours].astype(F32)

    def z_stage(xb):
        y_copy(xb).wait_recv()
        for r in range(ROWS):
            total = rsum[xb, r] + rxy[xb, r].astype(F32)
            rsum[xb, r] = total
            ztx[xb, r] = total.astype(BF)
        for i in (4, 3, 5, 2, 6, 1, 7):
            z_copy(xb, i).start()

    def home_stage(xb):
        total = rsum[xb, :, z_part(z), :]
        for i in range(1, 8):
            z_copy(xb, i).wait_recv()
            total = total + zrx[xb, i].astype(F32)
        htx[xb] = total.astype(BF)
        stays = jnp.logical_and(self_home, z // 2 == xb)

        @pl.when(stays)
        def _():
            frx[:, z_part(lax.rem(z, 4)), :] = htx[xb]

        @pl.when(jnp.logical_not(stays))
        def _():
            own_copy(xb).start()

    g_half_p = rc(gtx.at[0, pl.ds(0, 2)], grx.at[0, pl.ds(0, 2)], g_s.at[0], g_r.at[0], xp)
    g_half_m = rc(gtx.at[0, pl.ds(2, 2)], grx.at[0, pl.ds(2, 2)], g_s.at[1], g_r.at[1], xm)
    g_p = rc(gtx.at[1], grx.at[1], g_s.at[2], g_r.at[2], xp)
    g_m = rc(gtx.at[2], grx.at[2], g_s.at[3], g_r.at[3], xm)

    def bias_stage(step):
        if step == 1:
            g_half_p.wait_recv()
        if step == 2:
            g_half_m.wait_recv()
        if step == 3:
            g_p.wait_recv()
            g_m.wait_recv()
        for h in range(HEADS):
            for k in range(4):
                lanes = slice(k * 128, (k + 1) * 128)
                tile = turned[h, :, lanes]
                if (step == 1 and h < 2) or (step == 2 and h >= 2):
                    tile = tile + grx[0, h, :, lanes].astype(F32)
                if step == 3:
                    tile = tile + grx[1, h, :, lanes].astype(F32) + grx[2, h, :, lanes].astype(F32)
                    bias_grad[h, :, lanes] = tile.astype(BF)
                else:
                    gtx[step, h, :, lanes] = tile.astype(BF)
        if step == 0:
            g_half_p.start()
            g_half_m.start()
        if step == 1:
            g_p.start()
        if step == 2:
            g_m.start()

    def backward(step, carry):
        xb = lax.rem(x + jnp.where(step == 0, 2, jnp.where(step == 1, 1, jnp.where(step == 2, 3, 0))), NX)
        places = []
        for q in range(2 * ROWS):
            side = yh if q < ROWS else 1 - yh
            places.append((side * 4 + xb, q % ROWS, side * ROWS + q % ROWS))

        deltas = []
        for q, (sx, r, row) in enumerate(places):
            st = stats[row]
            f = jnp.exp(m_st[sx, r] - st[0:4, :])
            dls = f * st[4:8, :]
            deltas.append([jnp.concatenate([dls[h : h + 1, :], dls[h + 1 : h + 2, :]], axis=1) for h in (0, 2)])
            for h in range(HEADS):
                rows = slice(h * 32, (h + 1) * 32)
                dos[q, rows, h * 128 : (h + 1) * 128] = (
                    dot[row, rows, :].astype(F32) * f[h : h + 1, :]
                ).astype(BF)
            gv_ref[q] = nn(w[:, 256:384], dos[q]).astype(BF)
        for hp in range(2):
            cols = slice(hp * 256, hp * 256 + 256)
            for i in range(4):
                rows = slice(i * 128, (i + 1) * 128)
                total = None
                for q, (sx, r, row) in enumerate(places):
                    d_prob = nn(vals[sx, r, rows, :], dos[q, :, cols]) - deltas[q][hp]
                    d_score = probs[sx, r, rows, cols].astype(F32) * d_prob
                    total = d_score if total is None else total + d_score
                    ds_ref[q, rows, cols] = d_score.astype(BF)
                for j in range(2):
                    turned[hp * 2 + j, :, rows] = total[:, j * 128 : (j + 1) * 128].T
            for q, (sx, r, row) in enumerate(places):
                d_query = nn(keys_t[sx, r, hp * 64 : hp * 64 + 64, :], ds_ref[q, :, cols])
                for j in range(2):
                    rows = slice((hp * 2 + j) * 32, (hp * 2 + j + 1) * 32)
                    dq[q, rows, :] = dq[q, rows, :] + d_query[j * 32 : (j + 1) * 32, j * 128 : (j + 1) * 128]
        for q, (sx, r, row) in enumerate(places):
            kt[row, pl.ds(pl.multiple_of(xb * KB, KB), KB), :] = (
                nt(ds_ref[q], gk[row]) + nt(probs[sx, r], gv_ref[q])
            ).astype(BF)

        def block_at(back):
            return lax.rem(x + jnp.where(step == back, 2, jnp.where(step == back + 1, 1, 3)), NX)

        core_copy(xb).start()
        for s in range(3):
            @pl.when(step == s)
            def _():
                bias_stage(s)

        @pl.when(step >= 1)
        def _():
            z_stage(block_at(1))

        @pl.when(step >= 2)
        def _():
            home_stage(block_at(2))

        y_stage(xb)
        return carry

    lax.fori_loop(0, 4, backward, 0)

    for r in range(ROWS):
        dqtx[r] = dq[ROWS + r].astype(BF)
    dq_copy = rc(dqtx, dqrx, f_s.at[4], f_r.at[4], hpart)
    dq_copy.start()
    dq_copy.wait_recv()
    for r in range(ROWS):
        d_query = (dq[r] + dqrx[r].astype(F32)) * (DH ** -0.5)
        unit_t = split_nn(w[:, 0:128], d_query) + split_nn(w[:, 384:512], dgp[r])
        dgated[r] = unit_t.T
    z_stage(x)
    bias_stage(3)
    bias_out = pltpu.make_async_copy(bias_grad, bias_hbm, o_s.at[1])
    bias_out.start()
    home_stage(xs[3])
    home_stage(x)
    for j in range(4):
        @pl.when(jnp.logical_not(jnp.logical_and(self_home, lax.rem(z, 4) == j)))
        def _():
            rc(htx.at[0], frx.at[:, pl.ds(j * 32, 32)], f_s.at[0], f_r.at[j], sib).wait_recv()
    for r in range(ROWS):
        dgated[r] = dgated[r] + frx[r].astype(F32)
    normed_out = pltpu.make_async_copy(dgated, normed_hbm, o_s.at[2])
    normed_out.start()

    for copy in (bias_p, bias_m, bias_fp, bias_fm, q_send, d_send, att_copy, st_copy, back_copy, dq_copy,
                 g_half_p, g_half_m, g_p, g_m):
        copy.wait_send()
    for t in range(2):
        @pl.when(jnp.logical_not(jnp.logical_and(is_home, yl == t)))
        def _():
            key_send[t].wait_send()
    for i in range(4):
        up(i).wait_send()
        down(i).wait_send()
        core_copy(i).wait_send()
        y_copy(i).wait_send()
        for j in range(1, 8):
            z_copy(i, j).wait_send()

        @pl.when(jnp.logical_not(jnp.logical_and(self_home, z // 2 == i)))
        def _():
            own_copy(i).wait_send()

    for i in range(8):
        to_sib(i).wait_send()

    update_out.wait()
    bias_out.wait()
    normed_out.wait()


def shards(codes, expo, tok, gain, w, wo, bias, ug):
    vm = pltpu.VMEM
    dma = pltpu.SemaphoreType.DMA
    blk = (ROWS, T, C)
    scratch = [
        vm(blk, BF), vm((HEADS, T, KB), BF),
        vm((512, C), BF), vm((C, C), BF), vm(blk, BF), vm(blk, F32), vm(blk, F32),
        vm((6, 2048, C), BF), vm((6, C, T), BF), vm((6, C, T), BF), vm((3, HEADS, T, KB), BF),
        vm((4, KB, 512), F32), vm((8, 3, KB, 512), BF), vm((3, KB, 256), F32), vm((3, C, 512), BF),
        vm((6, C, 512), BF),
        vm((8, 3, HEADS, T), F32), vm((8, 3, HEADS, T), F32), vm((8, 3, C, T), F32),
        vm((8, 3, KB, C), BF), vm((8, 3, C, KB), BF), vm((6, C, 512), BF), vm((6, C, T), F32), vm((6, 8, T), F32),
        vm(blk, BF), vm(blk, BF), vm((ROWS, 8, T), F32), vm((ROWS, 8, T), F32), vm((ROWS, 8, T), F32),
        vm((6, 8, T), F32), vm(blk, F32),
        vm((6, KB, 512), BF), vm((3, KB, C), BF), vm((3, 160, KB), BF), vm((6, C, 512), BF), vm((HEADS, T, KB), F32),
        vm((6, C, T), F32), vm((6, 2048, C), BF),
        vm((4, 6, 256, C), BF), vm((4, 3, 256, C), BF), vm((4, 3, 256, C), BF), vm((4, 3, 256, C), F32),
        vm((4, 3, 256, C), BF), vm((4, 8, 3, 32, C), BF), vm((4, 3, 32, C), BF), vm(blk, BF), vm(blk, BF), vm(blk, BF),
        vm((3, HEADS, T, KB), BF), vm((3, HEADS, T, KB), BF),
        dma((4,)), dma((4,)), dma((2,)), dma((2,)), dma((2, 4)), dma((2, 4)), dma((8,)), dma((8,)),
        dma((2,)), dma((2,)), dma((3,)), dma((3,)), dma((4,)), dma((4,)), dma((4,)), dma((4,)),
        dma((4, 8)), dma((4, 8)), dma((5,)), dma((5,)), dma((4,)), dma((4,)), dma((3,)),
    ]
    v = pl.BlockSpec(memory_space=pltpu.VMEM)
    hbm = pl.BlockSpec(memory_space=pl.ANY)
    shapes = (
        jax.ShapeDtypeStruct(blk, BF),
        jax.ShapeDtypeStruct(blk, F32),
        jax.ShapeDtypeStruct((HEADS, T, KB), BF),
    )
    gain, expo = gain.reshape(1, C), expo.reshape(1, ROWS)
    update, d_normed, bias_grad = pl.pallas_call(
        kernel,
        out_shape=shapes,
        in_specs=[v] * 8,
        out_specs=(hbm, hbm, hbm),
        scratch_shapes=scratch,
        compiler_params=pltpu.CompilerParams(
            collective_id=0, has_side_effects=True, vmem_limit_bytes=58 * 1024 * 1024
        ),
        cost_estimate=pl.CostEstimate(flops=8_000_000_000, bytes_accessed=4_000_000, transcendentals=6_300_000),
    )(tok, codes, expo, gain, w, wo, bias, ug)
    return pl.pallas_call(
        norm_back,
        out_shape=(shapes[0], shapes[0], shapes[2]),
        in_specs=[v] * 6,
        out_specs=(v, v, v),
        compiler_params=pltpu.CompilerParams(vmem_limit_bytes=58 * 1024 * 1024),
    )(codes, expo, gain, d_normed, update, bias_grad)


def solution(mesh):
    in_specs = (
        P("row", "col", None), P("row", "col"), P(), P(), P(), P(), P(None, "col", "row"), P("row", "col", None),
    )
    out_specs = (P("row", "col", None), P("row", "col", None), P(None, "col", "row"))
    return jax.shard_map(shards, mesh=mesh, in_specs=in_specs, out_specs=out_specs, check_vma=False)
```

```python
import jax
import jax.numpy as jnp
from jax import lax
from jax.experimental import pallas as pl
from jax.experimental.pallas import tpu as pltpu
from jax.sharding import PartitionSpec as P

MASKED = -1e30
EPSILON = 1e-05
F32 = jnp.float32
BF = jnp.bfloat16
NX, NZ = 4, 8
HEADS, DH, C, T = 4, 32, 128, 128
KB = 512
ROWS = 3


def nn(a, b):
    return lax.dot_general(a, b, (((1,), (0,)), ((), ())), preferred_element_type=F32)


def nt(a, b):
    return lax.dot_general(a, b, (((1,), (1,)), ((), ())), preferred_element_type=F32)


def split_nn(w, a):
    high = a.astype(BF)
    low = (a - high.astype(F32)).astype(BF)
    return nn(w, high) + nn(w, low)


def per_head(stat):
    return jnp.concatenate(
        [jnp.broadcast_to(stat[h : h + 1, :], (DH, T)) for h in range(HEADS)], axis=0
    )


def normalised(codes, expo, r):
    value = codes[r].astype(F32) * jnp.exp2(expo[0:1, r : r + 1].astype(F32))
    centered = value - jnp.mean(value, axis=-1, keepdims=True)
    inv_std = lax.rsqrt(jnp.mean(centered * centered, axis=-1, keepdims=True) + EPSILON)
    return centered * inv_std, inv_std


def norm_back(codes, expo, gain, d_normed, update_in, bias_in, update, pair_grad, bias_grad):
    update[...] = update_in[...]
    bias_grad[...] = bias_in[...]
    for r in range(ROWS):
        unit, inv_std = normalised(codes, expo, r)
        e = d_normed[r] * gain[...]
        pair_grad[r] = (
            inv_std
            * (e - jnp.mean(e, axis=-1, keepdims=True) - unit * jnp.mean(e * unit, axis=-1, keepdims=True))
        ).astype(BF)


def kernel(
    tok, codes, expo, gain, w, wo, bias, ug,
    update_hbm, normed_hbm, bias_hbm,
    update, bias_grad,
    wt, wot, nb, gates, dgated, kn, qt, dot, bias_g, bias_t, probs, s_ref, qbd, dos,
    m_st, l_st, a_st, vals, keys_t, gk, att_loc, st_loc, att_tx, att_rx, st_rx, back_tx, back_rx, stats, dgp,
    ds_ref, k_ref, vt_ref, gv_ref, acc, turned, dq, kt, rxc, ytx, rxy, rsum, ztx, zrx, htx, frx, dqtx, dqrx, gtx, grx,
    bx_s, bx_r, ks_s, ks_r, zr_s, zr_r, sb_s, sb_r, pq_s, pq_r, ex_s, ex_r, kc_s, kc_r,
    ky_s, ky_r, zq_s, zq_r, f_s, f_r, g_s, g_r, o_s,
):
    row_id = lax.axis_index("row")
    col_id = lax.axis_index("col")
    yh, x = row_id // NX, lax.rem(row_id, NX)
    yl, z, c = col_id // 16, lax.rem(col_id, 16) // 2, lax.rem(col_id, 2)
    xs = [lax.rem(x + i, NX) for i in range(NX)]
    zs = [lax.rem(z + i, NZ) for i in range(NZ)]

    def dev(x_=x, yh_=yh, yl_=yl, z_=z, c_=c):
        return (yh_ * NX + x_, yl_ * 16 + z_ * 2 + c_)

    def rc(src, dst, send, recv, to):
        return pltpu.make_async_remote_copy(
            src_ref=src, dst_ref=dst, send_sem=send, recv_sem=recv,
            device_id=to, device_id_type=pl.DeviceIdType.MESH,
        )

    xp, xm, zp, zm = dev(x_=xs[1]), dev(x_=xs[3]), dev(z_=zs[1]), dev(z_=zs[7])
    sib = dev(c_=1 - c)
    ypart = dev(yl_=1 - yl)
    hpart = dev(yh_=1 - yh)
    cross = dev(yh_=1 - yh, yl_=1 - yl)
    is_home = yh == yl
    self_home = jnp.logical_and(is_home, jnp.logical_and(z // 4 == c, lax.rem(z, 2) == c))

    barrier = pltpu.get_barrier_semaphore()
    def greet(to):
        pl.semaphore_signal(barrier, inc=1, device_id=to, device_id_type=pl.DeviceIdType.MESH)

    for to in (xp, xm, sib, ypart, hpart, cross):
        greet(to)
    for i in range(1, 8):
        greet(dev(z_=zs[i]))
    for i in range(4):
        @pl.when(jnp.logical_not(jnp.logical_and(self_home, z // 2 == i)))
        def _():
            greet(dev(yh_=yl, yl_=yh, z_=2 * i + c, c_=z // 4))

        @pl.when(jnp.logical_not(jnp.logical_and(self_home, lax.rem(z, 4) == i)))
        def _():
            greet(dev(yh_=yl, yl_=yh, z_=4 * c + i, c_=lax.rem(z, 2)))


    gain_row = gain[...]
    for r in range(ROWS):
        nb[r] = (normalised(codes, expo, r)[0] * gain_row).astype(BF)

    pl.semaphore_wait(barrier, jnp.where(self_home, 19, 21))

    bias_p = rc(bias, bias_g.at[0], bx_s.at[0], bx_r.at[0], xp)
    bias_m = rc(bias, bias_g.at[1], bx_s.at[1], bx_r.at[1], xm)
    bias_fp = rc(bias_g.at[0, pl.ds(0, 2)], bias_g.at[2, pl.ds(0, 2)], bx_s.at[2], bx_r.at[2], xp)
    bias_fm = rc(bias_g.at[1, pl.ds(2, 2)], bias_g.at[2, pl.ds(2, 2)], bx_s.at[3], bx_r.at[3], xm)
    bias_p.start()
    bias_m.start()

    def key_at(zz, cc):
        return pl.ds(pl.multiple_of(zz * 256 + cc * 128, 128), 128)

    my_set = pl.ds(pl.multiple_of(yh * ROWS, ROWS), ROWS)
    key_send = [
        rc(nb, kn.at[pl.ds(yh * ROWS, ROWS), key_at(z, c)], ks_s.at[t], ks_r.at[yh], dev(yh_=yl, yl_=t))
        for t in range(2)
    ]
    for t in range(2):
        @pl.when(jnp.logical_not(jnp.logical_and(is_home, yl == t)))
        def _():
            key_send[t].start()

    @pl.when(is_home)
    def _():
        kn[pl.ds(yh * ROWS, ROWS), key_at(z, c), :] = nb[...]

    for q in range(4):
        wt[q * 128 : (q + 1) * 128, :] = w[:, q * 128 : (q + 1) * 128].astype(F32).T.astype(BF)
    wot[...] = wo[...].astype(F32).T.astype(BF)

    def set_of(ref, s):
        return ref.at[pl.ds(s * ROWS, ROWS)]

    for r in range(ROWS):
        n = nb[r]
        qt[yh * ROWS + r] = (nt(wt[0:128, :], n) * (DH ** -0.5)).astype(BF)
        gate = jax.nn.sigmoid(nt(wt[384:512, :], n))
        gates[r] = gate
        dg = nt(wo[...], ug[r])
        dgated[r] = dg
        dot[yh * ROWS + r] = (dg * gate).astype(BF)
    q_send = rc(set_of(qt, yh), set_of(qt, yh), pq_s.at[0], pq_r.at[0], hpart)
    d_send = rc(set_of(dot, yh), set_of(dot, yh), pq_s.at[1], pq_r.at[1], hpart)
    q_send.start()

    live = tok[...].reshape(1, 1)

    def prep(src, xb):
        for k in range(4):
            first = (yh * NX + xb) * KB + k * 128
            valid = first + lax.broadcasted_iota(jnp.int32, (128, 128), 0) < live
            for h in range(HEADS):
                tile = src[h, :, k * 128 : (k + 1) * 128].astype(F32).T
                bias_t[xb, k * 128 : (k + 1) * 128, h * 128 : (h + 1) * 128] = jnp.where(valid, tile, MASKED)

    qbd[...] = jnp.zeros_like(qbd)
    dos[...] = jnp.zeros_like(dos)
    prep(bias, x)

    def block(zz, cc=c):
        return kn.at[:, key_at(zz, cc)]

    def half(zz, s):
        return kn.at[pl.ds(s * ROWS, ROWS), key_at(zz, c)]

    sides = [yh, 1 - yh]

    def up(i, p):
        src = half(zs[(8 - i) % 8], sides[p])
        return rc(src, src, zr_s.at[0, i, p], zr_r.at[0, i, p], zp)

    def down(i, p):
        src = half(zs[i], sides[p])
        return rc(src, src, zr_s.at[1, i, p], zr_r.at[1, i, p], zm)

    def to_sib(i):
        return rc(block(zs[i]), block(zs[i]), sb_s.at[i], sb_r.at[i], sib)

    def from_sib(i):
        return rc(block(zs[i], 1 - c), block(zs[i], 1 - c), sb_s.at[i], sb_r.at[i], sib)

    def up_in(i, p):
        dst = half(zs[7 - i], sides[p])
        return rc(dst, dst, zr_s.at[0, i, p], zr_r.at[0, i, p], zp)

    def down_in(i, p):
        dst = half(zs[i + 1], sides[p])
        return rc(dst, dst, zr_s.at[1, i, p], zr_r.at[1, i, p], zm)

    def goes_up(i, p):
        return i < 3 or (i == 3 and p == 0)

    def goes_down(i, p):
        return i < 3 or (i == 3 and p == 1)

    def ring_step(i):
        for p in range(2):
            if goes_up(i, p):
                up_in(i, p).wait_recv()
                if goes_up(i + 1, p):
                    up(i + 1, p).start()
            if goes_down(i, p):
                down_in(i, p).wait_recv()
                if goes_down(i + 1, p):
                    down(i + 1, p).start()
        if i < 3:
            to_sib(7 - i).start()
            to_sib(i + 1).start()
        else:
            to_sib(4).start()

    for p in range(2):
        @pl.when(jnp.logical_not(jnp.logical_and(is_home, p == 0)))
        def _():
            rc(nb, half(z, sides[p]), ks_s.at[0], ks_r.at[sides[p]], sib).wait_recv()

        up(0, p).start()
        down(0, p).start()
    to_sib(0).start()
    bias_p.wait_recv()
    bias_fp.start()
    bias_m.wait_recv()
    bias_fm.start()
    prep(bias_g.at[0], xs[3])
    prep(bias_g.at[1], xs[1])
    ring_step(0)

    zb = z // 2
    even = lax.rem(z, 2) == 0
    near = jnp.where(even, zb + 3, zb + 1)
    far = jnp.where(even, zb + 1, zb + 3)

    def arrive(phase):
        for i in ((0, 1, 7), (2, 6), (3, 5), (4,))[phase]:
            from_sib(i).wait_recv()

    for r in range(ROWS):
        vt_ref[r, 64:80, :] = jnp.ones((16, KB), BF)
        vt_ref[r, 144:160, :] = jnp.ones((16, KB), BF)

    def load_q(r, row):
        for h in range(HEADS):
            qbd[r, h * 32 : (h + 1) * 32, h * 128 : (h + 1) * 128] = qt[row, h * 32 : (h + 1) * 32, :]

    att_copy = rc(att_tx, att_rx, ex_s.at[0], ex_r.at[0], hpart)
    st_copy = rc(set_of(st_loc, 1 - yh), st_rx, ex_s.at[1], ex_r.at[1], hpart)
    back_copy = rc(back_tx, back_rx, ex_s.at[2], ex_r.at[2], hpart)

    def combine(side, r):
        m_all = [m_st[side * 4 + i, r] for i in range(4)]
        top_m = jnp.maximum(jnp.maximum(m_all[0], m_all[1]), jnp.maximum(m_all[2], m_all[3]))
        total = jnp.zeros((HEADS, T), F32)
        weighted = jnp.zeros((C, T), F32)
        for i in range(4):
            f = jnp.exp(m_all[i] - top_m)
            total = total + f * l_st[side * 4 + i, r]
            weighted = weighted + per_head(f) * a_st[side * 4 + i, r]
        st_loc[side * ROWS + r, 0:4, :] = top_m
        st_loc[side * ROWS + r, 4:8, :] = total
        return weighted

    def forward(u, carry):
        phase, second = u // 2, lax.rem(u, 2)
        side = lax.rem(jnp.where(phase == 3, 1 - yh, yh) + second, 2)
        xb = lax.rem(
            jnp.where(phase == 0, zb, jnp.where(phase == 1, near, jnp.where(phase == 2, far, zb + 2))), NX
        )
        sx = side * 4 + xb

        for i in range(4):
            @pl.when(u == 2 * i)
            def _():
                arrive(i)

        @pl.when(jnp.logical_and(second == 0, xb == xs[2]))
        def _():
            bias_fp.wait_recv()
            bias_fm.wait_recv()
            prep(bias_g.at[2], xs[2])

        for i in range(1, 4):
            @pl.when(u == 2 * i - 1)
            def _():
                ring_step(i)

        @pl.when(u == 1)
        def _():
            rc(set_of(qt, yh), set_of(qt, 1 - yh), pq_s.at[0], pq_r.at[0], hpart).wait_recv()
            d_send.start()

        for r in range(ROWS):
            row = side * ROWS + r
            load_q(r, row)
            n = kn[row, pl.ds(pl.multiple_of(xb * KB, KB), KB), :]
            kv = nn(n, w[:, 128:384]).astype(BF)
            kvt = nt(wt[128:384, :], n).astype(BF)
            k_ref[r] = kv[:, 0:128]
            vals[sx, r] = kv[:, 128:256]
            keys_t[sx, r] = kvt[0:128, :]
            vt_ref[r, 0:64, :] = kvt[128:192, :]
            vt_ref[r, 80:144, :] = kvt[192:256, :]

        items = [(r, hp) for r in range(ROWS) for hp in range(2)]
        tops = {}

        def score(t):
            r, hp = items[t]
            cols = slice(hp * 256, hp * 256 + 256)
            q2 = qbd[r, :, cols]
            top = None
            for i in range(4):
                rows = slice(i * 128, (i + 1) * 128)
                s = nn(k_ref[r, rows, :], q2) + bias_t[xb, rows, cols]
                s_ref[t % 3, rows, :] = s
                part = jnp.max(s.reshape(16, 8, 256), axis=0)
                top = part if top is None else jnp.maximum(top, part)
            tops[t] = jnp.max(top, axis=0, keepdims=True)

        def weigh(t):
            r, hp = items[t]
            cols = slice(hp * 256, hp * 256 + 256)
            for i in range(4):
                rows = slice(i * 128, (i + 1) * 128)
                probs[sx, r, rows, cols] = jnp.exp(s_ref[t % 3, rows, :] - tops[t]).astype(BF)

        def attend(t):
            r, hp = items[t]
            cols = slice(hp * 256, hp * 256 + 256)
            a = nn(vt_ref[r, hp * 80 : hp * 80 + 80, :], probs[sx, r, :, cols])
            for j in range(2):
                h = hp * 2 + j
                lanes = slice(j * 128, (j + 1) * 128)
                m_st[sx, r, h : h + 1, :] = tops[t][:, lanes]
                l_st[sx, r, h : h + 1, :] = a[64:65, lanes]
                a_st[sx, r, h * 32 : (h + 1) * 32, :] = a[j * 32 : (j + 1) * 32, lanes]

        for t in range(8):
            if t < 6:
                score(t)
            if 1 <= t < 7:
                weigh(t - 1)
            if t >= 2:
                attend(t - 2)

        @pl.when(u == 6)
        def _():
            for r in range(ROWS):
                att_tx[r] = combine(1 - yh, r).astype(BF)
            att_copy.start()
            st_copy.start()

        return carry

    lax.fori_loop(0, 8, forward, 0)

    for r in range(ROWS):
        att_loc[yh * ROWS + r] = combine(yh, r)
    att_copy.wait_recv()
    st_copy.wait_recv()
    for r in range(ROWS):
        mine = yh * ROWS + r
        ma, la = st_loc[mine, 0:4, :], st_loc[mine, 4:8, :]
        mb, lb = st_rx[r, 0:4, :], st_rx[r, 4:8, :]
        top_m = jnp.maximum(ma, mb)
        fa, fb = jnp.exp(ma - top_m), jnp.exp(mb - top_m)
        total = fa * la + fb * lb
        attended = (per_head(fa) * att_loc[mine] + per_head(fb) * att_rx[r].astype(F32)) / per_head(total)
        gate = gates[r]
        product = dot[mine].astype(F32) * attended
        lse = top_m + jnp.log(total)
        stats[mine, 0:4, :] = lse
        back_tx[r, 0:4, :] = lse
        for h in range(HEADS):
            delta = jnp.sum(product[h * 32 : (h + 1) * 32, :], axis=0, keepdims=True)
            stats[mine, 4 + h : 5 + h, :] = delta
            back_tx[r, 4 + h : 5 + h, :] = delta
        att_loc[mine] = attended
    back_copy.start()
    for r in range(ROWS):
        attended = att_loc[yh * ROWS + r]
        gate = gates[r]
        dgp[r] = dgated[r] * attended * gate * (1.0 - gate)
        update[r] = nn(wot[...], (gate * attended).astype(BF)).T.astype(BF)
    update_out = pltpu.make_async_copy(update, update_hbm, o_s.at[0])
    update_out.start()
    for row in range(6):
        load_q(0, row)
        gk[row] = nn(w[:, 128:256], qbd[0]).astype(BF)

    rc(set_of(dot, yh), set_of(dot, 1 - yh), pq_s.at[1], pq_r.at[1], hpart).wait_recv()
    back_copy.wait_recv()
    for r in range(ROWS):
        stats[(1 - yh) * ROWS + r] = back_rx[r]
    dq[...] = jnp.zeros_like(dq)

    def core_half(xb, cc):
        return pl.ds(pl.multiple_of(xb * KB + cc * 256, 256), 256)

    def z_part(zz):
        return pl.ds(pl.multiple_of(zz * 32, 32), 32)

    def core_copy(xb, p):
        rows = pl.ds((yl if p else 1 - yl) * ROWS, ROWS)
        return rc(
            kt.at[rows, core_half(xb, 1 - c)], rxc.at[xb, rows], kc_s.at[xb, p], kc_r.at[xb, p], sib
        )

    def y_copy(xb):
        return rc(ytx.at[xb], rxy.at[xb], ky_s.at[xb], ky_r.at[xb], ypart)

    def z_copy(xb, i):
        return rc(
            ztx.at[xb, :, z_part(zs[i])], zrx.at[xb, i], zq_s.at[xb, i], zq_r.at[xb, i], dev(z_=zs[i])
        )

    def own_copy(xb):
        part = lax.rem(z, 4)
        return rc(
            htx.at[xb], frx.at[:, z_part(part)], f_s.at[xb], f_r.at[part],
            dev(yh_=yl, yl_=yh, z_=2 * xb + c, c_=z // 4),
        )

    def y_stage(xb):
        core_copy(xb, 0).wait_recv()
        for r in range(ROWS):
            theirs = (1 - yl) * ROWS + r
            ytx[xb, r] = (kt[theirs, core_half(xb, c), :].astype(F32) + rxc[xb, theirs].astype(F32)).astype(BF)
        y_copy(xb).start()

    def z_stage(xb):
        core_copy(xb, 1).wait_recv()
        y_copy(xb).wait_recv()
        for r in range(ROWS):
            ours = yl * ROWS + r
            total = kt[ours, core_half(xb, c), :].astype(F32) + rxc[xb, ours].astype(F32)
            total = total + rxy[xb, r].astype(F32)
            rsum[xb, r] = total
            ztx[xb, r] = total.astype(BF)
        for i in (4, 3, 5, 2, 6, 1, 7):
            z_copy(xb, i).start()

    def home_stage(xb):
        total = rsum[xb, :, z_part(z), :]
        for i in range(1, 8):
            z_copy(xb, i).wait_recv()
            total = total + zrx[xb, i].astype(F32)
        htx[xb] = total.astype(BF)
        stays = jnp.logical_and(self_home, z // 2 == xb)

        @pl.when(stays)
        def _():
            frx[:, z_part(lax.rem(z, 4)), :] = htx[xb]

        @pl.when(jnp.logical_not(stays))
        def _():
            own_copy(xb).start()

    g_half_p = rc(gtx.at[0, pl.ds(0, 2)], grx.at[0, pl.ds(0, 2)], g_s.at[0], g_r.at[0], xp)
    g_half_m = rc(gtx.at[0, pl.ds(2, 2)], grx.at[0, pl.ds(2, 2)], g_s.at[1], g_r.at[1], xm)
    g_p = rc(gtx.at[1], grx.at[1], g_s.at[2], g_r.at[2], xp)
    g_m = rc(gtx.at[2], grx.at[2], g_s.at[3], g_r.at[3], xm)

    def bias_stage(step):
        if step == 1:
            g_half_p.wait_recv()
        if step == 2:
            g_half_m.wait_recv()
        if step == 3:
            g_p.wait_recv()
            g_m.wait_recv()
        for h in range(HEADS):
            for k in range(4):
                lanes = slice(k * 128, (k + 1) * 128)
                tile = turned[h, :, lanes]
                if (step == 1 and h < 2) or (step == 2 and h >= 2):
                    tile = tile + grx[0, h, :, lanes].astype(F32)
                if step == 3:
                    tile = tile + grx[1, h, :, lanes].astype(F32) + grx[2, h, :, lanes].astype(F32)
                    bias_grad[h, :, lanes] = tile.astype(BF)
                else:
                    gtx[step, h, :, lanes] = tile.astype(BF)
        if step == 0:
            g_half_p.start()
            g_half_m.start()
        if step == 1:
            g_p.start()
        if step == 2:
            g_m.start()

    def backward(step, carry):
        xb = lax.rem(x + jnp.where(step == 0, 2, jnp.where(step == 1, 1, jnp.where(step == 2, 3, 0))), NX)
        places = []
        for q in range(2 * ROWS):
            side = 1 - yl if q < ROWS else yl
            places.append((q, side * 4 + xb, q % ROWS, side * ROWS + q % ROWS))

        deltas = []
        for q, sx, r, row in places:
            st = stats[row]
            f = jnp.exp(m_st[sx, r] - st[0:4, :])
            dls = f * st[4:8, :]
            deltas.append([jnp.concatenate([dls[h : h + 1, :], dls[h + 1 : h + 2, :]], axis=1) for h in (0, 2)])
            for h in range(HEADS):
                rows = slice(h * 32, (h + 1) * 32)
                dos[q, rows, h * 128 : (h + 1) * 128] = (
                    dot[row, rows, :].astype(F32) * f[h : h + 1, :]
                ).astype(BF)
            gv_ref[q] = nn(w[:, 256:384], dos[q]).astype(BF)

        def score_grads(group, hp):
            cols = slice(hp * 256, hp * 256 + 256)
            for i in range(4):
                rows = slice(i * 128, (i + 1) * 128)
                total = acc[rows, cols] if group else None
                for q, sx, r, row in places[group * ROWS : group * ROWS + ROWS]:
                    d_prob = nn(vals[sx, r, rows, :], dos[q, :, cols]) - deltas[q][hp]
                    d_score = probs[sx, r, rows, cols].astype(F32) * d_prob
                    total = d_score if total is None else total + d_score
                    ds_ref[q, rows, cols] = d_score.astype(BF)
                if group:
                    for j in range(2):
                        turned[hp * 2 + j, :, rows] = total[:, j * 128 : (j + 1) * 128].T
                else:
                    acc[rows, cols] = total

        def query_grads(group, hp):
            cols = slice(hp * 256, hp * 256 + 256)
            for q, sx, r, row in places[group * ROWS : group * ROWS + ROWS]:
                d_query = nn(keys_t[sx, r, hp * 64 : hp * 64 + 64, :], ds_ref[q, :, cols])
                for j in range(2):
                    rows = slice((hp * 2 + j) * 32, (hp * 2 + j + 1) * 32)
                    dq[q, rows, :] = dq[q, rows, :] + d_query[j * 32 : (j + 1) * 32, j * 128 : (j + 1) * 128]

        def key_terms(group):
            for q, sx, r, row in places[group * ROWS : group * ROWS + ROWS]:
                kt[row, pl.ds(pl.multiple_of(xb * KB, KB), KB), :] = (
                    nt(ds_ref[q], gk[row]) + nt(probs[sx, r], gv_ref[q])
                ).astype(BF)

        for group in range(2):
            score_grads(group, 0)
            query_grads(group, 0)
            if group:
                y_stage(xb)
            score_grads(group, 1)
            query_grads(group, 1)
            key_terms(group)
            core_copy(xb, group).start()

        def block_at(back):
            return lax.rem(x + jnp.where(step == back, 2, jnp.where(step == back + 1, 1, 3)), NX)

        for s in range(3):
            @pl.when(step == s)
            def _():
                bias_stage(s)

        @pl.when(step >= 1)
        def _():
            z_stage(block_at(1))

        @pl.when(step >= 2)
        def _():
            home_stage(block_at(2))

        return carry

    lax.fori_loop(0, 4, backward, 0)

    mine, theirs = jnp.where(is_home, ROWS, 0), jnp.where(is_home, 0, ROWS)
    for r in range(ROWS):
        dqtx[r] = dq[theirs + r].astype(BF)
    dq_copy = rc(dqtx, dqrx, f_s.at[4], f_r.at[4], hpart)
    dq_copy.start()
    dq_copy.wait_recv()
    for r in range(ROWS):
        d_query = (dq[mine + r] + dqrx[r].astype(F32)) * (DH ** -0.5)
        unit_t = split_nn(w[:, 0:128], d_query) + split_nn(w[:, 384:512], dgp[r])
        dgated[r] = unit_t.T
    z_stage(x)
    bias_stage(3)
    bias_out = pltpu.make_async_copy(bias_grad, bias_hbm, o_s.at[1])
    bias_out.start()
    home_stage(xs[3])
    home_stage(x)
    for j in range(4):
        @pl.when(jnp.logical_not(jnp.logical_and(self_home, lax.rem(z, 4) == j)))
        def _():
            rc(htx.at[0], frx.at[:, pl.ds(j * 32, 32)], f_s.at[0], f_r.at[j], sib).wait_recv()
    for r in range(ROWS):
        dgated[r] = dgated[r] + frx[r].astype(F32)
    normed_out = pltpu.make_async_copy(dgated, normed_hbm, o_s.at[2])
    normed_out.start()

    for copy in (bias_p, bias_m, bias_fp, bias_fm, q_send, d_send, att_copy, st_copy, back_copy, dq_copy,
                 g_half_p, g_half_m, g_p, g_m):
        copy.wait_send()
    for t in range(2):
        @pl.when(jnp.logical_not(jnp.logical_and(is_home, yl == t)))
        def _():
            key_send[t].wait_send()
    for i in range(4):
        for p in range(2):
            if goes_up(i, p):
                up(i, p).wait_send()
            if goes_down(i, p):
                down(i, p).wait_send()
        core_copy(i, 0).wait_send()
        core_copy(i, 1).wait_send()
        y_copy(i).wait_send()
        for j in range(1, 8):
            z_copy(i, j).wait_send()

        @pl.when(jnp.logical_not(jnp.logical_and(self_home, z // 2 == i)))
        def _():
            own_copy(i).wait_send()

    for i in range(8):
        to_sib(i).wait_send()

    update_out.wait()
    bias_out.wait()
    normed_out.wait()


def shards(codes, expo, tok, gain, w, wo, bias, ug):
    vm = pltpu.VMEM
    dma = pltpu.SemaphoreType.DMA
    blk = (ROWS, T, C)
    scratch = [
        vm(blk, BF), vm((HEADS, T, KB), BF),
        vm((512, C), BF), vm((C, C), BF), vm(blk, BF), vm(blk, F32), vm(blk, F32),
        vm((6, 2048, C), BF), vm((6, C, T), BF), vm((6, C, T), BF), vm((3, HEADS, T, KB), BF),
        vm((4, KB, 512), F32), vm((8, 3, KB, 512), BF), vm((3, KB, 256), F32), vm((3, C, 512), BF),
        vm((6, C, 512), BF),
        vm((8, 3, HEADS, T), F32), vm((8, 3, HEADS, T), F32), vm((8, 3, C, T), F32),
        vm((8, 3, KB, C), BF), vm((8, 3, C, KB), BF), vm((6, C, 512), BF), vm((6, C, T), F32), vm((6, 8, T), F32),
        vm(blk, BF), vm(blk, BF), vm((ROWS, 8, T), F32), vm((ROWS, 8, T), F32), vm((ROWS, 8, T), F32),
        vm((6, 8, T), F32), vm(blk, F32),
        vm((6, KB, 512), BF), vm((3, KB, C), BF), vm((3, 160, KB), BF), vm((6, C, 512), BF), vm((KB, 512), F32),
        vm((HEADS, T, KB), F32),
        vm((6, C, T), F32), vm((6, 2048, C), BF),
        vm((4, 6, 256, C), BF), vm((4, 3, 256, C), BF), vm((4, 3, 256, C), BF), vm((4, 3, 256, C), F32),
        vm((4, 3, 256, C), BF), vm((4, 8, 3, 32, C), BF), vm((4, 3, 32, C), BF), vm(blk, BF), vm(blk, BF), vm(blk, BF),
        vm((3, HEADS, T, KB), BF), vm((3, HEADS, T, KB), BF),
        dma((4,)), dma((4,)), dma((2,)), dma((2,)), dma((2, 4, 2)), dma((2, 4, 2)), dma((8,)), dma((8,)),
        dma((2,)), dma((2,)), dma((3,)), dma((3,)), dma((4, 2)), dma((4, 2)), dma((4,)), dma((4,)),
        dma((4, 8)), dma((4, 8)), dma((5,)), dma((5,)), dma((4,)), dma((4,)), dma((3,)),
    ]
    v = pl.BlockSpec(memory_space=pltpu.VMEM)
    hbm = pl.BlockSpec(memory_space=pl.ANY)
    shapes = (
        jax.ShapeDtypeStruct(blk, BF),
        jax.ShapeDtypeStruct(blk, F32),
        jax.ShapeDtypeStruct((HEADS, T, KB), BF),
    )
    gain, expo = gain.reshape(1, C), expo.reshape(1, ROWS)
    update, d_normed, bias_grad = pl.pallas_call(
        kernel,
        out_shape=shapes,
        in_specs=[v] * 8,
        out_specs=(hbm, hbm, hbm),
        scratch_shapes=scratch,
        compiler_params=pltpu.CompilerParams(
            collective_id=0, has_side_effects=True, vmem_limit_bytes=58 * 1024 * 1024
        ),
        cost_estimate=pl.CostEstimate(flops=8_000_000_000, bytes_accessed=4_000_000, transcendentals=6_300_000),
    )(tok, codes, expo, gain, w, wo, bias, ug)
    return pl.pallas_call(
        norm_back,
        out_shape=(shapes[0], shapes[0], shapes[2]),
        in_specs=[v] * 6,
        out_specs=(v, v, v),
        compiler_params=pltpu.CompilerParams(vmem_limit_bytes=58 * 1024 * 1024),
    )(codes, expo, gain, d_normed, update, bias_grad)


def solution(mesh):
    in_specs = (
        P("row", "col", None), P("row", "col"), P(), P(), P(), P(), P(None, "col", "row"), P("row", "col", None),
    )
    out_specs = (P("row", "col", None), P("row", "col", None), P(None, "col", "row"))
    return jax.shard_map(shards, mesh=mesh, in_specs=in_specs, out_specs=out_specs, check_vma=False)
```

```python
import jax
import jax.numpy as jnp
from jax import lax
from jax.experimental import pallas as pl
from jax.experimental.pallas import tpu as pltpu
from jax.sharding import PartitionSpec as P

MASKED = -1e30
EPSILON = 1e-05
F32 = jnp.float32
BF = jnp.bfloat16
NX, NZ = 4, 8
HEADS, DH, C, T = 4, 32, 128, 128
KB = 512
ROWS = 3


def nn(a, b):
    return lax.dot_general(a, b, (((1,), (0,)), ((), ())), preferred_element_type=F32)


def nt(a, b):
    return lax.dot_general(a, b, (((1,), (1,)), ((), ())), preferred_element_type=F32)


def split_nn(w, a):
    high = a.astype(BF)
    low = (a - high.astype(F32)).astype(BF)
    return nn(w, high) + nn(w, low)


def per_head(stat):
    return jnp.concatenate(
        [jnp.broadcast_to(stat[h : h + 1, :], (DH, T)) for h in range(HEADS)], axis=0
    )


def normalised(codes, expo, r):
    value = codes[r].astype(F32) * jnp.exp2(expo[0:1, r : r + 1].astype(F32))
    centered = value - jnp.mean(value, axis=-1, keepdims=True)
    inv_std = lax.rsqrt(jnp.mean(centered * centered, axis=-1, keepdims=True) + EPSILON)
    return centered * inv_std, inv_std


def norm_back(codes, expo, gain, d_normed, update_in, bias_in, update, pair_grad, bias_grad):
    update[...] = update_in[...]
    bias_grad[...] = bias_in[...]
    for r in range(ROWS):
        unit, inv_std = normalised(codes, expo, r)
        e = d_normed[r] * gain[...]
        pair_grad[r] = (
            inv_std
            * (e - jnp.mean(e, axis=-1, keepdims=True) - unit * jnp.mean(e * unit, axis=-1, keepdims=True))
        ).astype(BF)


def kernel(
    tok, codes, expo, gain, w, wo, bias, ug,
    update_hbm, normed_hbm, bias_hbm,
    update, bias_grad,
    wt, wot, nb, gates, dgated, kn, qt, dot, bias_g, bias_t, probs, s_ref, qbd, dos,
    m_st, l_st, a_st, vals, keys_t, g_n, att_loc, st_loc, att_tx, att_rx, st_rx, back_tx, back_rx, stats, dgp,
    ds_ref, k_ref, vt_ref, turned, dq, kt, rxc, ytx, rxy, rsum, ztx, zrx, htx, frx, dqtx, dqrx, gtx, grx,
    bx_s, bx_r, ks_s, ks_r, zr_s, zr_r, sb_s, sb_r, pq_s, pq_r, ex_s, ex_r, kc_s, kc_r,
    ky_s, ky_r, zq_s, zq_r, f_s, f_r, g_s, g_r, o_s,
):
    row_id = lax.axis_index("row")
    col_id = lax.axis_index("col")
    yh, x = row_id // NX, lax.rem(row_id, NX)
    yl, z, c = col_id // 16, lax.rem(col_id, 16) // 2, lax.rem(col_id, 2)
    xs = [lax.rem(x + i, NX) for i in range(NX)]
    zs = [lax.rem(z + i, NZ) for i in range(NZ)]

    def dev(x_=x, yh_=yh, yl_=yl, z_=z, c_=c):
        return (yh_ * NX + x_, yl_ * 16 + z_ * 2 + c_)

    def rc(src, dst, send, recv, to):
        return pltpu.make_async_remote_copy(
            src_ref=src, dst_ref=dst, send_sem=send, recv_sem=recv,
            device_id=to, device_id_type=pl.DeviceIdType.MESH,
        )

    xp, xm, zp, zm = dev(x_=xs[1]), dev(x_=xs[3]), dev(z_=zs[1]), dev(z_=zs[7])
    sib = dev(c_=1 - c)
    ypart = dev(yl_=1 - yl)
    hpart = dev(yh_=1 - yh)
    cross = dev(yh_=1 - yh, yl_=1 - yl)
    is_home = yh == yl
    self_home = jnp.logical_and(is_home, jnp.logical_and(z // 4 == c, lax.rem(z, 2) == c))

    barrier = pltpu.get_barrier_semaphore()
    def greet(to):
        pl.semaphore_signal(barrier, inc=1, device_id=to, device_id_type=pl.DeviceIdType.MESH)

    for to in (xp, xm, sib, ypart, hpart, cross):
        greet(to)
    for i in range(1, 8):
        greet(dev(z_=zs[i]))
    for i in range(4):
        @pl.when(jnp.logical_not(jnp.logical_and(self_home, z // 2 == i)))
        def _():
            greet(dev(yh_=yl, yl_=yh, z_=2 * i + c, c_=z // 4))

        @pl.when(jnp.logical_not(jnp.logical_and(self_home, lax.rem(z, 4) == i)))
        def _():
            greet(dev(yh_=yl, yl_=yh, z_=4 * c + i, c_=lax.rem(z, 2)))


    gain_row = gain[...]
    for r in range(ROWS):
        nb[r] = (normalised(codes, expo, r)[0] * gain_row).astype(BF)

    pl.semaphore_wait(barrier, jnp.where(self_home, 19, 21))

    bias_p = rc(bias, bias_g.at[0], bx_s.at[0], bx_r.at[0], xp)
    bias_m = rc(bias, bias_g.at[1], bx_s.at[1], bx_r.at[1], xm)
    bias_fp = rc(bias_g.at[0, pl.ds(0, 2)], bias_g.at[2, pl.ds(0, 2)], bx_s.at[2], bx_r.at[2], xp)
    bias_fm = rc(bias_g.at[1, pl.ds(2, 2)], bias_g.at[2, pl.ds(2, 2)], bx_s.at[3], bx_r.at[3], xm)
    bias_p.start()
    bias_m.start()

    def key_at(zz, cc):
        return pl.ds(pl.multiple_of(zz * 256 + cc * 128, 128), 128)

    my_set = pl.ds(pl.multiple_of(yh * ROWS, ROWS), ROWS)
    key_send = [
        rc(nb, kn.at[pl.ds(yh * ROWS, ROWS), key_at(z, c)], ks_s.at[t], ks_r.at[yh], dev(yh_=yl, yl_=t))
        for t in range(2)
    ]
    for t in range(2):
        @pl.when(jnp.logical_not(jnp.logical_and(is_home, yl == t)))
        def _():
            key_send[t].start()

    @pl.when(is_home)
    def _():
        kn[pl.ds(yh * ROWS, ROWS), key_at(z, c), :] = nb[...]

    for q in range(4):
        wt[q * 128 : (q + 1) * 128, :] = w[:, q * 128 : (q + 1) * 128].astype(F32).T.astype(BF)
    wot[...] = wo[...].astype(F32).T.astype(BF)

    def set_of(ref, s):
        return ref.at[pl.ds(s * ROWS, ROWS)]

    for r in range(ROWS):
        n = nb[r]
        qt[yh * ROWS + r] = (nt(wt[0:128, :], n) * (DH ** -0.5)).astype(BF)
        gate = jax.nn.sigmoid(nt(wt[384:512, :], n))
        gates[r] = gate
        dg = nt(wo[...], ug[r])
        dgated[r] = dg
        dot[yh * ROWS + r] = (dg * gate).astype(BF)
    q_send = rc(set_of(qt, yh), set_of(qt, yh), pq_s.at[0], pq_r.at[0], hpart)
    d_send = rc(set_of(dot, yh), set_of(dot, yh), pq_s.at[1], pq_r.at[1], hpart)
    q_send.start()

    live = tok[...].reshape(1, 1)

    def prep(src, xb):
        for k in range(4):
            first = (yh * NX + xb) * KB + k * 128
            valid = first + lax.broadcasted_iota(jnp.int32, (128, 128), 0) < live
            for h in range(HEADS):
                tile = src[h, :, k * 128 : (k + 1) * 128].astype(F32).T
                bias_t[xb, k * 128 : (k + 1) * 128, h * 128 : (h + 1) * 128] = jnp.where(valid, tile, MASKED)

    qbd[...] = jnp.zeros_like(qbd)
    dos[...] = jnp.zeros_like(dos)

    def spread(dst, src, row):
        for h in range(HEADS):
            rows = slice(h * 32, (h + 1) * 32)
            dst[row, rows, h * 128 : (h + 1) * 128] = src[row, rows, :]

    def key_factors(row):
        for part, src in enumerate((qbd, dos)):
            g = nn(w[:, 128 + part * 128 : 256 + part * 128], src[row])
            for h in range(HEADS):
                rows = slice(part * 512 + h * 128, part * 512 + (h + 1) * 128)
                g_n[row, rows, :] = g[:, h * 128 : (h + 1) * 128].T.astype(BF)

    for r in range(ROWS):
        spread(qbd, qt, yh * ROWS + r)
        spread(dos, dot, yh * ROWS + r)
        key_factors(yh * ROWS + r)
    prep(bias, x)

    def block(zz, cc=c):
        return kn.at[:, key_at(zz, cc)]

    def half(zz, s):
        return kn.at[pl.ds(s * ROWS, ROWS), key_at(zz, c)]

    sides = [yh, 1 - yh]

    def up(i, p):
        src = half(zs[(8 - i) % 8], sides[p])
        return rc(src, src, zr_s.at[0, i, p], zr_r.at[0, i, p], zp)

    def down(i, p):
        src = half(zs[i], sides[p])
        return rc(src, src, zr_s.at[1, i, p], zr_r.at[1, i, p], zm)

    def to_sib(i):
        return rc(block(zs[i]), block(zs[i]), sb_s.at[i], sb_r.at[i], sib)

    def from_sib(i):
        return rc(block(zs[i], 1 - c), block(zs[i], 1 - c), sb_s.at[i], sb_r.at[i], sib)

    def up_in(i, p):
        dst = half(zs[7 - i], sides[p])
        return rc(dst, dst, zr_s.at[0, i, p], zr_r.at[0, i, p], zp)

    def down_in(i, p):
        dst = half(zs[i + 1], sides[p])
        return rc(dst, dst, zr_s.at[1, i, p], zr_r.at[1, i, p], zm)

    def goes_up(i, p):
        return i < 3 or (i == 3 and p == 0)

    def goes_down(i, p):
        return i < 3 or (i == 3 and p == 1)

    def ring_step(i):
        for p in range(2):
            if goes_up(i, p):
                up_in(i, p).wait_recv()
                if goes_up(i + 1, p):
                    up(i + 1, p).start()
            if goes_down(i, p):
                down_in(i, p).wait_recv()
                if goes_down(i + 1, p):
                    down(i + 1, p).start()
        if i < 3:
            to_sib(7 - i).start()
            to_sib(i + 1).start()
        else:
            to_sib(4).start()

    for p in range(2):
        @pl.when(jnp.logical_not(jnp.logical_and(is_home, p == 0)))
        def _():
            rc(nb, half(z, sides[p]), ks_s.at[0], ks_r.at[sides[p]], sib).wait_recv()

        up(0, p).start()
        down(0, p).start()
    to_sib(0).start()
    bias_p.wait_recv()
    bias_fp.start()
    bias_m.wait_recv()
    bias_fm.start()
    prep(bias_g.at[0], xs[3])
    prep(bias_g.at[1], xs[1])
    ring_step(0)

    zb = z // 2
    even = lax.rem(z, 2) == 0
    near = jnp.where(even, zb + 3, zb + 1)
    far = jnp.where(even, zb + 1, zb + 3)

    def arrive(phase):
        for i in ((0, 1, 7), (2, 6), (3, 5), (4,))[phase]:
            from_sib(i).wait_recv()

    for r in range(ROWS):
        vt_ref[r, 64:80, :] = jnp.ones((16, KB), BF)
        vt_ref[r, 144:160, :] = jnp.ones((16, KB), BF)

    att_copy = rc(att_tx, att_rx, ex_s.at[0], ex_r.at[0], hpart)
    st_copy = rc(set_of(st_loc, 1 - yh), st_rx, ex_s.at[1], ex_r.at[1], hpart)
    back_copy = rc(back_tx, back_rx, ex_s.at[2], ex_r.at[2], hpart)

    def combine(side, r):
        m_all = [m_st[side * 4 + i, r] for i in range(4)]
        top_m = jnp.maximum(jnp.maximum(m_all[0], m_all[1]), jnp.maximum(m_all[2], m_all[3]))
        total = jnp.zeros((HEADS, T), F32)
        weighted = jnp.zeros((C, T), F32)
        for i in range(4):
            f = jnp.exp(m_all[i] - top_m)
            total = total + f * l_st[side * 4 + i, r]
            weighted = weighted + per_head(f) * a_st[side * 4 + i, r]
        st_loc[side * ROWS + r, 0:4, :] = top_m
        st_loc[side * ROWS + r, 4:8, :] = total
        return weighted

    def forward(u, carry):
        phase, second = u // 2, lax.rem(u, 2)
        side = lax.rem(jnp.where(phase == 3, 1 - yh, yh) + second, 2)
        xb = lax.rem(
            jnp.where(phase == 0, zb, jnp.where(phase == 1, near, jnp.where(phase == 2, far, zb + 2))), NX
        )
        sx = side * 4 + xb

        for i in range(4):
            @pl.when(u == 2 * i)
            def _():
                arrive(i)

        @pl.when(jnp.logical_and(second == 0, xb == xs[2]))
        def _():
            bias_fp.wait_recv()
            bias_fm.wait_recv()
            prep(bias_g.at[2], xs[2])

        for i in range(1, 4):
            @pl.when(u == 2 * i - 1)
            def _():
                ring_step(i)

        @pl.when(u == 1)
        def _():
            rc(set_of(qt, yh), set_of(qt, 1 - yh), pq_s.at[0], pq_r.at[0], hpart).wait_recv()
            d_send.start()
            for r in range(ROWS):
                spread(qbd, qt, (1 - yh) * ROWS + r)

        for r in range(ROWS):
            row = side * ROWS + r
            n = kn[row, pl.ds(pl.multiple_of(xb * KB, KB), KB), :]
            kv = nn(n, w[:, 128:384]).astype(BF)
            kvt = nt(wt[128:384, :], n).astype(BF)
            k_ref[r] = kv[:, 0:128]
            vals[sx, r] = kv[:, 128:256]
            keys_t[sx, r] = kvt[0:128, :]
            vt_ref[r, 0:64, :] = kvt[128:192, :]
            vt_ref[r, 80:144, :] = kvt[192:256, :]

        items = [(r, hp) for r in range(ROWS) for hp in range(2)]
        tops = {}

        def score(t):
            r, hp = items[t]
            cols = slice(hp * 256, hp * 256 + 256)
            q2 = qbd[side * ROWS + r, :, cols]
            top = None
            for i in range(4):
                rows = slice(i * 128, (i + 1) * 128)
                s = nn(k_ref[r, rows, :], q2) + bias_t[xb, rows, cols]
                s_ref[t % 3, rows, :] = s
                part = jnp.max(s.reshape(16, 8, 256), axis=0)
                top = part if top is None else jnp.maximum(top, part)
            tops[t] = jnp.max(top, axis=0, keepdims=True)

        def weigh(t):
            r, hp = items[t]
            cols = slice(hp * 256, hp * 256 + 256)
            for i in range(4):
                rows = slice(i * 128, (i + 1) * 128)
                probs[sx, r, rows, cols] = jnp.exp(s_ref[t % 3, rows, :] - tops[t]).astype(BF)

        def attend(t):
            r, hp = items[t]
            cols = slice(hp * 256, hp * 256 + 256)
            a = nn(vt_ref[r, hp * 80 : hp * 80 + 80, :], probs[sx, r, :, cols])
            for j in range(2):
                h = hp * 2 + j
                lanes = slice(j * 128, (j + 1) * 128)
                m_st[sx, r, h : h + 1, :] = tops[t][:, lanes]
                l_st[sx, r, h : h + 1, :] = a[64:65, lanes]
                a_st[sx, r, h * 32 : (h + 1) * 32, :] = a[j * 32 : (j + 1) * 32, lanes]

        for t in range(8):
            if t < 6:
                score(t)
            if 1 <= t < 7:
                weigh(t - 1)
            if t >= 2:
                attend(t - 2)

        @pl.when(u == 6)
        def _():
            for r in range(ROWS):
                att_tx[r] = combine(1 - yh, r).astype(BF)
            att_copy.start()
            st_copy.start()

        return carry

    lax.fori_loop(0, 8, forward, 0)

    for r in range(ROWS):
        att_loc[yh * ROWS + r] = combine(yh, r)
    att_copy.wait_recv()
    st_copy.wait_recv()
    for r in range(ROWS):
        mine = yh * ROWS + r
        ma, la = st_loc[mine, 0:4, :], st_loc[mine, 4:8, :]
        mb, lb = st_rx[r, 0:4, :], st_rx[r, 4:8, :]
        top_m = jnp.maximum(ma, mb)
        fa, fb = jnp.exp(ma - top_m), jnp.exp(mb - top_m)
        total = fa * la + fb * lb
        attended = (per_head(fa) * att_loc[mine] + per_head(fb) * att_rx[r].astype(F32)) / per_head(total)
        gate = gates[r]
        product = dot[mine].astype(F32) * attended
        lse = top_m + jnp.log(total)
        stats[mine, 0:4, :] = lse
        back_tx[r, 0:4, :] = lse
        for h in range(HEADS):
            delta = jnp.sum(product[h * 32 : (h + 1) * 32, :], axis=0, keepdims=True)
            stats[mine, 4 + h : 5 + h, :] = delta
            back_tx[r, 4 + h : 5 + h, :] = delta
        att_loc[mine] = attended
    back_copy.start()
    for r in range(ROWS):
        attended = att_loc[yh * ROWS + r]
        gate = gates[r]
        dgp[r] = dgated[r] * attended * gate * (1.0 - gate)
        update[r] = nn(wot[...], (gate * attended).astype(BF)).T.astype(BF)
    update_out = pltpu.make_async_copy(update, update_hbm, o_s.at[0])
    update_out.start()
    rc(set_of(dot, yh), set_of(dot, 1 - yh), pq_s.at[1], pq_r.at[1], hpart).wait_recv()
    for r in range(ROWS):
        spread(dos, dot, (1 - yh) * ROWS + r)
        key_factors((1 - yh) * ROWS + r)
    back_copy.wait_recv()
    for r in range(ROWS):
        stats[(1 - yh) * ROWS + r] = back_rx[r]
    dq[...] = jnp.zeros_like(dq)

    def core_half(xb, cc):
        return pl.ds(pl.multiple_of(xb * KB + cc * 256, 256), 256)

    def z_part(zz):
        return pl.ds(pl.multiple_of(zz * 32, 32), 32)

    def core_copy(xb):
        return rc(kt.at[:, core_half(xb, 1 - c)], rxc.at[xb], kc_s.at[xb], kc_r.at[xb], sib)

    def y_copy(xb):
        return rc(ytx.at[xb], rxy.at[xb], ky_s.at[xb], ky_r.at[xb], ypart)

    def z_copy(xb, i):
        return rc(
            ztx.at[xb, :, z_part(zs[i])], zrx.at[xb, i], zq_s.at[xb, i], zq_r.at[xb, i], dev(z_=zs[i])
        )

    def own_copy(xb):
        part = lax.rem(z, 4)
        return rc(
            htx.at[xb], frx.at[:, z_part(part)], f_s.at[xb], f_r.at[part],
            dev(yh_=yl, yl_=yh, z_=2 * xb + c, c_=z // 4),
        )

    def y_stage(xb):
        core_copy(xb).wait_recv()
        for r in range(ROWS):
            theirs = (1 - yl) * ROWS + r
            ytx[xb, r] = (kt[theirs, core_half(xb, c), :].astype(F32) + rxc[xb, theirs].astype(F32)).astype(BF)
        y_copy(xb).start()

    def z_stage(xb):
        y_copy(xb).wait_recv()
        for r in range(ROWS):
            ours = yl * ROWS + r
            total = kt[ours, core_half(xb, c), :].astype(F32) + rxc[xb, ours].astype(F32)
            total = total + rxy[xb, r].astype(F32)
            rsum[xb, r] = total
            ztx[xb, r] = total.astype(BF)
        for i in (4, 3, 5, 2, 6, 1, 7):
            z_copy(xb, i).start()

    def home_stage(xb):
        total = rsum[xb, :, z_part(z), :]
        for i in range(1, 8):
            z_copy(xb, i).wait_recv()
            total = total + zrx[xb, i].astype(F32)
        htx[xb] = total.astype(BF)
        stays = jnp.logical_and(self_home, z // 2 == xb)

        @pl.when(stays)
        def _():
            frx[:, z_part(lax.rem(z, 4)), :] = htx[xb]

        @pl.when(jnp.logical_not(stays))
        def _():
            own_copy(xb).start()

    g_half_p = rc(gtx.at[0, pl.ds(0, 2)], grx.at[0, pl.ds(0, 2)], g_s.at[0], g_r.at[0], xp)
    g_half_m = rc(gtx.at[0, pl.ds(2, 2)], grx.at[0, pl.ds(2, 2)], g_s.at[1], g_r.at[1], xm)
    g_p = rc(gtx.at[1], grx.at[1], g_s.at[2], g_r.at[2], xp)
    g_m = rc(gtx.at[2], grx.at[2], g_s.at[3], g_r.at[3], xm)

    def bias_stage(step):
        if step == 1:
            g_half_p.wait_recv()
        if step == 2:
            g_half_m.wait_recv()
        if step == 3:
            g_p.wait_recv()
            g_m.wait_recv()
        for h in range(HEADS):
            for k in range(4):
                lanes = slice(k * 128, (k + 1) * 128)
                tile = turned[h, :, lanes]
                if (step == 1 and h < 2) or (step == 2 and h >= 2):
                    tile = tile + grx[0, h, :, lanes].astype(F32)
                if step == 3:
                    tile = tile + grx[1, h, :, lanes].astype(F32) + grx[2, h, :, lanes].astype(F32)
                    bias_grad[h, :, lanes] = tile.astype(BF)
                else:
                    gtx[step, h, :, lanes] = tile.astype(BF)
        if step == 0:
            g_half_p.start()
            g_half_m.start()
        if step == 1:
            g_p.start()
        if step == 2:
            g_m.start()

    def backward(step, carry):
        xb = lax.rem(x + jnp.where(step == 0, 2, jnp.where(step == 1, 1, jnp.where(step == 2, 3, 0))), NX)
        places, factors, deltas = [], [], []
        for q in range(2 * ROWS):
            side = yh if q < ROWS else 1 - yh
            sx, r, row = side * 4 + xb, q % ROWS, side * ROWS + q % ROWS
            places.append((q, sx, r, row))
            st = stats[row]
            f, delta = jnp.exp(m_st[sx, r] - st[0:4, :]), st[4:8, :]
            factors.append([jnp.concatenate([f[h : h + 1, :], f[h + 1 : h + 2, :]], axis=1) for h in (0, 2)])
            deltas.append([jnp.concatenate([delta[h : h + 1, :], delta[h + 1 : h + 2, :]], axis=1) for h in (0, 2)])
        for hp in range(2):
            cols = slice(hp * 256, hp * 256 + 256)
            p_cols = slice(512 + hp * 256, 768 + hp * 256)
            for i in range(4):
                rows = slice(i * 128, (i + 1) * 128)
                total = None
                for q, sx, r, row in places:
                    d_prob = nn(vals[sx, r, rows, :], dos[row, :, cols]) - deltas[q][hp]
                    prob = probs[sx, r, rows, cols].astype(F32) * factors[q][hp]
                    d_score = prob * d_prob
                    total = d_score if total is None else total + d_score
                    ds_ref[q, rows, cols] = d_score.astype(BF)
                    ds_ref[q, rows, p_cols] = prob.astype(BF)
                for j in range(2):
                    turned[hp * 2 + j, :, rows] = total[:, j * 128 : (j + 1) * 128].T
            for q, sx, r, row in places:
                d_query = nn(keys_t[sx, r, hp * 64 : hp * 64 + 64, :], ds_ref[q, :, cols])
                for j in range(2):
                    rows = slice((hp * 2 + j) * 32, (hp * 2 + j + 1) * 32)
                    dq[q, rows, :] = dq[q, rows, :] + d_query[j * 32 : (j + 1) * 32, j * 128 : (j + 1) * 128]
        for q, sx, r, row in places:
            for i in range(2):
                rows = slice(i * 256, (i + 1) * 256)
                kt[row, pl.ds(pl.multiple_of(xb * KB + i * 256, 256), 256), :] = nn(
                    ds_ref[q, rows, :], g_n[row]
                ).astype(BF)

        def block_at(back):
            return lax.rem(x + jnp.where(step == back, 2, jnp.where(step == back + 1, 1, 3)), NX)

        core_copy(xb).start()
        for s in range(3):
            @pl.when(step == s)
            def _():
                bias_stage(s)

        @pl.when(step >= 1)
        def _():
            z_stage(block_at(1))

        @pl.when(step >= 2)
        def _():
            home_stage(block_at(2))

        y_stage(xb)
        return carry

    lax.fori_loop(0, 4, backward, 0)

    for r in range(ROWS):
        dqtx[r] = dq[ROWS + r].astype(BF)
    dq_copy = rc(dqtx, dqrx, f_s.at[4], f_r.at[4], hpart)
    dq_copy.start()
    dq_copy.wait_recv()
    for r in range(ROWS):
        d_query = (dq[r] + dqrx[r].astype(F32)) * (DH ** -0.5)
        unit_t = split_nn(w[:, 0:128], d_query) + split_nn(w[:, 384:512], dgp[r])
        dgated[r] = unit_t.T
    z_stage(x)
    home_stage(xs[3])
    home_stage(x)
    bias_stage(3)
    bias_out = pltpu.make_async_copy(bias_grad, bias_hbm, o_s.at[1])
    bias_out.start()
    for j in range(4):
        @pl.when(jnp.logical_not(jnp.logical_and(self_home, lax.rem(z, 4) == j)))
        def _():
            rc(htx.at[0], frx.at[:, pl.ds(j * 32, 32)], f_s.at[0], f_r.at[j], sib).wait_recv()
    for r in range(ROWS):
        dgated[r] = dgated[r] + frx[r].astype(F32)
    normed_out = pltpu.make_async_copy(dgated, normed_hbm, o_s.at[2])
    normed_out.start()

    for copy in (bias_p, bias_m, bias_fp, bias_fm, q_send, d_send, att_copy, st_copy, back_copy, dq_copy,
                 g_half_p, g_half_m, g_p, g_m):
        copy.wait_send()
    for t in range(2):
        @pl.when(jnp.logical_not(jnp.logical_and(is_home, yl == t)))
        def _():
            key_send[t].wait_send()
    for i in range(4):
        for p in range(2):
            if goes_up(i, p):
                up(i, p).wait_send()
            if goes_down(i, p):
                down(i, p).wait_send()
        core_copy(i).wait_send()
        y_copy(i).wait_send()
        for j in range(1, 8):
            z_copy(i, j).wait_send()

        @pl.when(jnp.logical_not(jnp.logical_and(self_home, z // 2 == i)))
        def _():
            own_copy(i).wait_send()

    for i in range(8):
        to_sib(i).wait_send()

    update_out.wait()
    bias_out.wait()
    normed_out.wait()


def shards(codes, expo, tok, gain, w, wo, bias, ug):
    vm = pltpu.VMEM
    dma = pltpu.SemaphoreType.DMA
    blk = (ROWS, T, C)
    scratch = [
        vm(blk, BF), vm((HEADS, T, KB), BF),
        vm((512, C), BF), vm((C, C), BF), vm(blk, BF), vm(blk, F32), vm(blk, F32),
        vm((6, 2048, C), BF), vm((6, C, T), BF), vm((6, C, T), BF), vm((3, HEADS, T, KB), BF),
        vm((4, KB, 512), F32), vm((8, 3, KB, 512), BF), vm((3, KB, 256), F32), vm((6, C, 512), BF),
        vm((6, C, 512), BF),
        vm((8, 3, HEADS, T), F32), vm((8, 3, HEADS, T), F32), vm((8, 3, C, T), F32),
        vm((8, 3, KB, C), BF), vm((8, 3, C, KB), BF), vm((6, 1024, C), BF), vm((6, C, T), F32), vm((6, 8, T), F32),
        vm(blk, BF), vm(blk, BF), vm((ROWS, 8, T), F32), vm((ROWS, 8, T), F32), vm((ROWS, 8, T), F32),
        vm((6, 8, T), F32), vm(blk, F32),
        vm((6, KB, 1024), BF), vm((3, KB, C), BF), vm((3, 160, KB), BF),
        vm((HEADS, T, KB), F32),
        vm((6, C, T), F32), vm((6, 2048, C), BF),
        vm((4, 6, 256, C), BF), vm((4, 3, 256, C), BF), vm((4, 3, 256, C), BF), vm((4, 3, 256, C), F32),
        vm((4, 3, 256, C), BF), vm((4, 8, 3, 32, C), BF), vm((4, 3, 32, C), BF), vm(blk, BF), vm(blk, BF), vm(blk, BF),
        vm((3, HEADS, T, KB), BF), vm((3, HEADS, T, KB), BF),
        dma((4,)), dma((4,)), dma((2,)), dma((2,)), dma((2, 4, 2)), dma((2, 4, 2)), dma((8,)), dma((8,)),
        dma((2,)), dma((2,)), dma((3,)), dma((3,)), dma((4,)), dma((4,)), dma((4,)), dma((4,)),
        dma((4, 8)), dma((4, 8)), dma((5,)), dma((5,)), dma((4,)), dma((4,)), dma((3,)),
    ]
    v = pl.BlockSpec(memory_space=pltpu.VMEM)
    hbm = pl.BlockSpec(memory_space=pl.ANY)
    shapes = (
        jax.ShapeDtypeStruct(blk, BF),
        jax.ShapeDtypeStruct(blk, F32),
        jax.ShapeDtypeStruct((HEADS, T, KB), BF),
    )
    gain, expo = gain.reshape(1, C), expo.reshape(1, ROWS)
    update, d_normed, bias_grad = pl.pallas_call(
        kernel,
        out_shape=shapes,
        in_specs=[v] * 8,
        out_specs=(hbm, hbm, hbm),
        scratch_shapes=scratch,
        compiler_params=pltpu.CompilerParams(
            collective_id=0, has_side_effects=True, vmem_limit_bytes=60 * 1024 * 1024
        ),
        cost_estimate=pl.CostEstimate(flops=8_000_000_000, bytes_accessed=4_000_000, transcendentals=6_300_000),
    )(tok, codes, expo, gain, w, wo, bias, ug)
    return pl.pallas_call(
        norm_back,
        out_shape=(shapes[0], shapes[0], shapes[2]),
        in_specs=[v] * 6,
        out_specs=(v, v, v),
        compiler_params=pltpu.CompilerParams(vmem_limit_bytes=58 * 1024 * 1024),
    )(codes, expo, gain, d_normed, update, bias_grad)


def solution(mesh):
    in_specs = (
        P("row", "col", None), P("row", "col"), P(), P(), P(), P(), P(None, "col", "row"), P("row", "col", None),
    )
    out_specs = (P("row", "col", None), P("row", "col", None), P(None, "col", "row"))
    return jax.shard_map(shards, mesh=mesh, in_specs=in_specs, out_specs=out_specs, check_vma=False)
```

```python
import jax
import jax.numpy as jnp
from jax import lax
from jax.experimental import pallas as pl
from jax.experimental.pallas import tpu as pltpu
from jax.sharding import PartitionSpec as P

MASKED = -1e30
EPSILON = 1e-05
F32 = jnp.float32
BF = jnp.bfloat16
NX, NZ = 4, 8
HEADS, DH, C, T = 4, 32, 128, 128
KB = 512
ROWS = 3


def nn(a, b):
    return lax.dot_general(a, b, (((1,), (0,)), ((), ())), preferred_element_type=F32)


def nt(a, b):
    return lax.dot_general(a, b, (((1,), (1,)), ((), ())), preferred_element_type=F32)


def split_nn(w, a):
    high = a.astype(BF)
    low = (a - high.astype(F32)).astype(BF)
    return nn(w, high) + nn(w, low)


def per_head(stat):
    return jnp.concatenate(
        [jnp.broadcast_to(stat[h : h + 1, :], (DH, T)) for h in range(HEADS)], axis=0
    )


def normalised(codes, expo, r):
    value = codes[r].astype(F32) * jnp.exp2(expo[0:1, r : r + 1].astype(F32))
    centered = value - jnp.mean(value, axis=-1, keepdims=True)
    inv_std = lax.rsqrt(jnp.mean(centered * centered, axis=-1, keepdims=True) + EPSILON)
    return centered * inv_std, inv_std


def norm_back(codes, expo, gain, d_normed, update_in, bias_in, update, pair_grad, bias_grad):
    update[...] = update_in[...]
    bias_grad[...] = bias_in[...]
    for r in range(ROWS):
        unit, inv_std = normalised(codes, expo, r)
        e = d_normed[r] * gain[...]
        pair_grad[r] = (
            inv_std
            * (e - jnp.mean(e, axis=-1, keepdims=True) - unit * jnp.mean(e * unit, axis=-1, keepdims=True))
        ).astype(BF)


def kernel(
    tok, codes, expo, gain, w, wo, bias, ug,
    update_hbm, normed_hbm, bias_hbm,
    update, bias_grad,
    wt, wot, nb, gates, dgated, kn, qt, dot, bias_g, bias_t, probs, s_ref, qbd, dos,
    m_st, l_st, a_st, vals, keys_t, g_n, att_loc, st_loc, att_tx, att_rx, st_rx, back_tx, back_rx, stats, dgp,
    ds_ref, k_ref, vt_ref, turned, dq, kt, rxc, ytx, rxy, rsum, ztx, zrx, htx, frx, dqtx, dqrx, gtx, grx,
    bx_s, bx_r, ks_s, ks_r, zr_s, zr_r, sb_s, sb_r, pq_s, pq_r, ex_s, ex_r, kc_s, kc_r,
    ky_s, ky_r, zq_s, zq_r, f_s, f_r, g_s, g_r, o_s,
):
    row_id = lax.axis_index("row")
    col_id = lax.axis_index("col")
    yh, x = row_id // NX, lax.rem(row_id, NX)
    yl, z, c = col_id // 16, lax.rem(col_id, 16) // 2, lax.rem(col_id, 2)
    xs = [lax.rem(x + i, NX) for i in range(NX)]
    zs = [lax.rem(z + i, NZ) for i in range(NZ)]

    def dev(x_=x, yh_=yh, yl_=yl, z_=z, c_=c):
        return (yh_ * NX + x_, yl_ * 16 + z_ * 2 + c_)

    def rc(src, dst, send, recv, to):
        return pltpu.make_async_remote_copy(
            src_ref=src, dst_ref=dst, send_sem=send, recv_sem=recv,
            device_id=to, device_id_type=pl.DeviceIdType.MESH,
        )

    xp, xm, zp, zm = dev(x_=xs[1]), dev(x_=xs[3]), dev(z_=zs[1]), dev(z_=zs[7])
    sib = dev(c_=1 - c)
    ypart = dev(yl_=1 - yl)
    hpart = dev(yh_=1 - yh)
    cross = dev(yh_=1 - yh, yl_=1 - yl)
    is_home = yh == yl
    self_home = jnp.logical_and(is_home, jnp.logical_and(z // 4 == c, lax.rem(z, 2) == c))

    barrier = pltpu.get_barrier_semaphore()
    def greet(to):
        pl.semaphore_signal(barrier, inc=1, device_id=to, device_id_type=pl.DeviceIdType.MESH)

    for to in (xp, xm, sib, ypart, hpart, cross):
        greet(to)
    for i in range(1, 8):
        greet(dev(z_=zs[i]))
    for i in range(4):
        @pl.when(jnp.logical_not(jnp.logical_and(self_home, z // 2 == i)))
        def _():
            greet(dev(yh_=yl, yl_=yh, z_=2 * i + c, c_=z // 4))

        @pl.when(jnp.logical_not(jnp.logical_and(self_home, lax.rem(z, 4) == i)))
        def _():
            greet(dev(yh_=yl, yl_=yh, z_=4 * c + i, c_=lax.rem(z, 2)))


    gain_row = gain[...]
    for r in range(ROWS):
        nb[r] = (normalised(codes, expo, r)[0] * gain_row).astype(BF)

    pl.semaphore_wait(barrier, jnp.where(self_home, 19, 21))

    bias_p = rc(bias, bias_g.at[0], bx_s.at[0], bx_r.at[0], xp)
    bias_m = rc(bias, bias_g.at[1], bx_s.at[1], bx_r.at[1], xm)
    bias_fp = rc(bias_g.at[0, pl.ds(0, 2)], bias_g.at[2, pl.ds(0, 2)], bx_s.at[2], bx_r.at[2], xp)
    bias_fm = rc(bias_g.at[1, pl.ds(2, 2)], bias_g.at[2, pl.ds(2, 2)], bx_s.at[3], bx_r.at[3], xm)
    bias_p.start()
    bias_m.start()

    def key_at(zz, cc):
        return pl.ds(pl.multiple_of(zz * 256 + cc * 128, 128), 128)

    my_set = pl.ds(pl.multiple_of(yh * ROWS, ROWS), ROWS)
    key_send = [
        rc(nb, kn.at[pl.ds(yh * ROWS, ROWS), key_at(z, c)], ks_s.at[t], ks_r.at[yh], dev(yh_=yl, yl_=t))
        for t in range(2)
    ]
    for t in range(2):
        @pl.when(jnp.logical_not(jnp.logical_and(is_home, yl == t)))
        def _():
            key_send[t].start()

    @pl.when(is_home)
    def _():
        kn[pl.ds(yh * ROWS, ROWS), key_at(z, c), :] = nb[...]

    for q in range(4):
        wt[q * 128 : (q + 1) * 128, :] = w[:, q * 128 : (q + 1) * 128].astype(F32).T.astype(BF)
    wot[...] = wo[...].astype(F32).T.astype(BF)

    def set_of(ref, s):
        return ref.at[pl.ds(s * ROWS, ROWS)]

    for r in range(ROWS):
        n = nb[r]
        qt[yh * ROWS + r] = (nt(wt[0:128, :], n) * (DH ** -0.5)).astype(BF)
        gate = jax.nn.sigmoid(nt(wt[384:512, :], n))
        gates[r] = gate
        dg = nt(wo[...], ug[r])
        dgated[r] = dg
        dot[yh * ROWS + r] = (dg * gate).astype(BF)
    q_send = rc(set_of(qt, yh), set_of(qt, yh), pq_s.at[0], pq_r.at[0], hpart)
    d_send = rc(set_of(dot, yh), set_of(dot, yh), pq_s.at[1], pq_r.at[1], hpart)
    q_send.start()

    live = tok[...].reshape(1, 1)

    def prep(src, xb):
        for k in range(4):
            first = (yh * NX + xb) * KB + k * 128
            valid = first + lax.broadcasted_iota(jnp.int32, (128, 128), 0) < live
            for h in range(HEADS):
                tile = src[h, :, k * 128 : (k + 1) * 128].astype(F32).T
                bias_t[xb, k * 128 : (k + 1) * 128, h * 128 : (h + 1) * 128] = jnp.where(valid, tile, MASKED)

    qbd[...] = jnp.zeros_like(qbd)
    dos[...] = jnp.zeros_like(dos)

    def spread(dst, src, row):
        for h in range(HEADS):
            rows = slice(h * 32, (h + 1) * 32)
            dst[row, rows, h * 128 : (h + 1) * 128] = src[row, rows, :]

    def key_factors(row):
        for part, src in enumerate((qbd, dos)):
            g = nn(w[:, 128 + part * 128 : 256 + part * 128], src[row])
            for h in range(HEADS):
                rows = slice(part * 512 + h * 128, part * 512 + (h + 1) * 128)
                g_n[row, rows, :] = g[:, h * 128 : (h + 1) * 128].T.astype(BF)

    for r in range(ROWS):
        spread(qbd, qt, yh * ROWS + r)
        spread(dos, dot, yh * ROWS + r)
        key_factors(yh * ROWS + r)
    prep(bias, x)

    def block(zz, cc=c):
        return kn.at[:, key_at(zz, cc)]

    def half(zz, s):
        return kn.at[pl.ds(s * ROWS, ROWS), key_at(zz, c)]

    sides = [yh, 1 - yh]

    def up(i, p):
        src = half(zs[(8 - i) % 8], sides[p])
        return rc(src, src, zr_s.at[0, i, p], zr_r.at[0, i, p], zp)

    def down(i, p):
        src = half(zs[i], sides[p])
        return rc(src, src, zr_s.at[1, i, p], zr_r.at[1, i, p], zm)

    def to_sib(i):
        return rc(block(zs[i]), block(zs[i]), sb_s.at[i], sb_r.at[i], sib)

    def from_sib(i):
        return rc(block(zs[i], 1 - c), block(zs[i], 1 - c), sb_s.at[i], sb_r.at[i], sib)

    def up_in(i, p):
        dst = half(zs[7 - i], sides[p])
        return rc(dst, dst, zr_s.at[0, i, p], zr_r.at[0, i, p], zp)

    def down_in(i, p):
        dst = half(zs[i + 1], sides[p])
        return rc(dst, dst, zr_s.at[1, i, p], zr_r.at[1, i, p], zm)

    def goes_up(i, p):
        return i < 3 or (i == 3 and p == 0)

    def goes_down(i, p):
        return i < 3 or (i == 3 and p == 1)

    def ring_step(i):
        for p in range(2):
            if goes_up(i, p):
                up_in(i, p).wait_recv()
                if goes_up(i + 1, p):
                    up(i + 1, p).start()
            if goes_down(i, p):
                down_in(i, p).wait_recv()
                if goes_down(i + 1, p):
                    down(i + 1, p).start()
        if i < 3:
            to_sib(7 - i).start()
            to_sib(i + 1).start()
        else:
            to_sib(4).start()

    for p in range(2):
        @pl.when(jnp.logical_not(jnp.logical_and(is_home, p == 0)))
        def _():
            rc(nb, half(z, sides[p]), ks_s.at[0], ks_r.at[sides[p]], sib).wait_recv()

        up(0, p).start()
        down(0, p).start()
    to_sib(0).start()
    bias_p.wait_recv()
    bias_fp.start()
    bias_m.wait_recv()
    bias_fm.start()
    prep(bias_g.at[0], xs[3])
    prep(bias_g.at[1], xs[1])
    ring_step(0)

    zb = z // 2
    even = lax.rem(z, 2) == 0
    near = jnp.where(even, zb + 3, zb + 1)
    far = jnp.where(even, zb + 1, zb + 3)

    turned_round = zb == xs[2]
    order = [jnp.where(turned_round, near, zb), jnp.where(turned_round, zb, near), far, zb + 2]

    @pl.when(turned_round)
    def _():
        ring_step(1)

    def arrive(phase):
        for i in ((0, 1, 7), (2, 6), (3, 5), (4,))[phase]:
            from_sib(i).wait_recv()

    for r in range(ROWS):
        vt_ref[r, 64:80, :] = jnp.ones((16, KB), BF)
        vt_ref[r, 144:160, :] = jnp.ones((16, KB), BF)

    att_copy = rc(att_tx, att_rx, ex_s.at[0], ex_r.at[0], hpart)
    st_copy = rc(set_of(st_loc, 1 - yh), st_rx, ex_s.at[1], ex_r.at[1], hpart)
    back_copy = rc(back_tx, back_rx, ex_s.at[2], ex_r.at[2], hpart)

    def combine(side, r):
        m_all = [m_st[side * 4 + i, r] for i in range(4)]
        top_m = jnp.maximum(jnp.maximum(m_all[0], m_all[1]), jnp.maximum(m_all[2], m_all[3]))
        total = jnp.zeros((HEADS, T), F32)
        weighted = jnp.zeros((C, T), F32)
        for i in range(4):
            f = jnp.exp(m_all[i] - top_m)
            total = total + f * l_st[side * 4 + i, r]
            weighted = weighted + per_head(f) * a_st[side * 4 + i, r]
        st_loc[side * ROWS + r, 0:4, :] = top_m
        st_loc[side * ROWS + r, 4:8, :] = total
        return weighted

    def forward(u, carry):
        phase, second = u // 2, lax.rem(u, 2)
        side = lax.rem(jnp.where(phase == 3, 1 - yh, yh) + second, 2)
        xb = lax.rem(
            jnp.where(phase == 0, order[0], jnp.where(phase == 1, order[1], jnp.where(phase == 2, far, zb + 2))), NX
        )
        sx = side * 4 + xb

        for i in range(4):
            @pl.when(u == (jnp.where(turned_round, 0, 2) if i == 1 else 2 * i))
            def _():
                arrive(i)

        @pl.when(jnp.logical_and(second == 0, xb == xs[2]))
        def _():
            bias_fp.wait_recv()
            bias_fm.wait_recv()
            prep(bias_g.at[2], xs[2])

        for i in range(1, 4):
            @pl.when(u == (jnp.where(turned_round, -1, 1) if i == 1 else 2 * i - 1))
            def _():
                ring_step(i)

        @pl.when(u == 1)
        def _():
            rc(set_of(qt, yh), set_of(qt, 1 - yh), pq_s.at[0], pq_r.at[0], hpart).wait_recv()
            d_send.start()
            for r in range(ROWS):
                spread(qbd, qt, (1 - yh) * ROWS + r)

        for r in range(ROWS):
            row = side * ROWS + r
            n = kn[row, pl.ds(pl.multiple_of(xb * KB, KB), KB), :]
            kv = nn(n, w[:, 128:384]).astype(BF)
            kvt = nt(wt[128:384, :], n).astype(BF)
            k_ref[r] = kv[:, 0:128]
            vals[sx, r] = kv[:, 128:256]
            keys_t[sx, r] = kvt[0:128, :]
            vt_ref[r, 0:64, :] = kvt[128:192, :]
            vt_ref[r, 80:144, :] = kvt[192:256, :]

        items = [(r, hp) for r in range(ROWS) for hp in range(2)]
        tops = {}

        def score(t):
            r, hp = items[t]
            cols = slice(hp * 256, hp * 256 + 256)
            q2 = qbd[side * ROWS + r, :, cols]
            top = None
            for i in range(4):
                rows = slice(i * 128, (i + 1) * 128)
                s = nn(k_ref[r, rows, :], q2) + bias_t[xb, rows, cols]
                s_ref[t % 3, rows, :] = s
                part = jnp.max(s.reshape(16, 8, 256), axis=0)
                top = part if top is None else jnp.maximum(top, part)
            tops[t] = jnp.max(top, axis=0, keepdims=True)

        def weigh(t):
            r, hp = items[t]
            cols = slice(hp * 256, hp * 256 + 256)
            for i in range(4):
                rows = slice(i * 128, (i + 1) * 128)
                probs[sx, r, rows, cols] = jnp.exp(s_ref[t % 3, rows, :] - tops[t]).astype(BF)

        def attend(t):
            r, hp = items[t]
            cols = slice(hp * 256, hp * 256 + 256)
            a = nn(vt_ref[r, hp * 80 : hp * 80 + 80, :], probs[sx, r, :, cols])
            for j in range(2):
                h = hp * 2 + j
                lanes = slice(j * 128, (j + 1) * 128)
                m_st[sx, r, h : h + 1, :] = tops[t][:, lanes]
                l_st[sx, r, h : h + 1, :] = a[64:65, lanes]
                a_st[sx, r, h * 32 : (h + 1) * 32, :] = a[j * 32 : (j + 1) * 32, lanes]

        for t in range(8):
            if t < 6:
                score(t)
            if 1 <= t < 7:
                weigh(t - 1)
            if t >= 2:
                attend(t - 2)

        @pl.when(u == 6)
        def _():
            for r in range(ROWS):
                att_tx[r] = combine(1 - yh, r).astype(BF)
            att_copy.start()
            st_copy.start()

        return carry

    lax.fori_loop(0, 8, forward, 0)

    for r in range(ROWS):
        att_loc[yh * ROWS + r] = combine(yh, r)
    att_copy.wait_recv()
    st_copy.wait_recv()
    for r in range(ROWS):
        mine = yh * ROWS + r
        ma, la = st_loc[mine, 0:4, :], st_loc[mine, 4:8, :]
        mb, lb = st_rx[r, 0:4, :], st_rx[r, 4:8, :]
        top_m = jnp.maximum(ma, mb)
        fa, fb = jnp.exp(ma - top_m), jnp.exp(mb - top_m)
        total = fa * la + fb * lb
        attended = (per_head(fa) * att_loc[mine] + per_head(fb) * att_rx[r].astype(F32)) / per_head(total)
        gate = gates[r]
        product = dot[mine].astype(F32) * attended
        lse = top_m + jnp.log(total)
        stats[mine, 0:4, :] = lse
        back_tx[r, 0:4, :] = lse
        for h in range(HEADS):
            delta = jnp.sum(product[h * 32 : (h + 1) * 32, :], axis=0, keepdims=True)
            stats[mine, 4 + h : 5 + h, :] = delta
            back_tx[r, 4 + h : 5 + h, :] = delta
        att_loc[mine] = attended
    back_copy.start()
    for r in range(ROWS):
        attended = att_loc[yh * ROWS + r]
        gate = gates[r]
        dgp[r] = dgated[r] * attended * gate * (1.0 - gate)
        update[r] = nn(wot[...], (gate * attended).astype(BF)).T.astype(BF)
    update_out = pltpu.make_async_copy(update, update_hbm, o_s.at[0])
    update_out.start()
    rc(set_of(dot, yh), set_of(dot, 1 - yh), pq_s.at[1], pq_r.at[1], hpart).wait_recv()
    for r in range(ROWS):
        spread(dos, dot, (1 - yh) * ROWS + r)
        key_factors((1 - yh) * ROWS + r)
    back_copy.wait_recv()
    for r in range(ROWS):
        stats[(1 - yh) * ROWS + r] = back_rx[r]
    dq[...] = jnp.zeros_like(dq)

    def core_half(xb, cc):
        return pl.ds(pl.multiple_of(xb * KB + cc * 256, 256), 256)

    def z_part(zz):
        return pl.ds(pl.multiple_of(zz * 32, 32), 32)

    def core_copy(xb):
        return rc(kt.at[:, core_half(xb, 1 - c)], rxc.at[xb], kc_s.at[xb], kc_r.at[xb], sib)

    def y_copy(xb, p):
        part = pl.ds(p * 128, 128)
        return rc(ytx.at[xb, :, part], rxy.at[xb, :, part], ky_s.at[xb, p], ky_r.at[xb, p], ypart)

    def z_copy(xb, i):
        return rc(
            ztx.at[xb, :, z_part(zs[i])], zrx.at[xb, i], zq_s.at[xb, i], zq_r.at[xb, i], dev(z_=zs[i])
        )

    def own_copy(xb):
        part = lax.rem(z, 4)
        return rc(
            htx.at[xb], frx.at[:, z_part(part)], f_s.at[xb], f_r.at[part],
            dev(yh_=yl, yl_=yh, z_=2 * xb + c, c_=z // 4),
        )

    def key_part(xb, p):
        return pl.ds(pl.multiple_of(xb * KB + c * 256 + p * 128, 128), 128)

    def y_stage(xb):
        core_copy(xb).wait_recv()
        for p in range(2):
            part = slice(p * 128, (p + 1) * 128)
            for r in range(ROWS):
                theirs = (1 - yl) * ROWS + r
                ytx[xb, r, part, :] = (
                    kt[theirs, key_part(xb, p), :].astype(F32) + rxc[xb, theirs, part, :].astype(F32)
                ).astype(BF)
            y_copy(xb, p).start()

    def z_stage(xb):
        for p in range(2):
            part = slice(p * 128, (p + 1) * 128)
            y_copy(xb, p).wait_recv()
            for r in range(ROWS):
                ours = yl * ROWS + r
                total = kt[ours, key_part(xb, p), :].astype(F32) + rxc[xb, ours, part, :].astype(F32)
                total = total + rxy[xb, r, part, :].astype(F32)
                rsum[xb, r, part, :] = total
                ztx[xb, r, part, :] = total.astype(BF)
            for i in (4, 3, 5, 2, 6, 1, 7):
                @pl.when(zs[i] // 4 == p)
                def _():
                    z_copy(xb, i).start()

    def home_stage(xb):
        total = rsum[xb, :, z_part(z), :]
        for i in range(1, 8):
            z_copy(xb, i).wait_recv()
            total = total + zrx[xb, i].astype(F32)
        htx[xb] = total.astype(BF)
        stays = jnp.logical_and(self_home, z // 2 == xb)

        @pl.when(stays)
        def _():
            frx[:, z_part(lax.rem(z, 4)), :] = htx[xb]

        @pl.when(jnp.logical_not(stays))
        def _():
            own_copy(xb).start()

    g_half_p = rc(gtx.at[0, pl.ds(0, 2)], grx.at[0, pl.ds(0, 2)], g_s.at[0], g_r.at[0], xp)
    g_half_m = rc(gtx.at[0, pl.ds(2, 2)], grx.at[0, pl.ds(2, 2)], g_s.at[1], g_r.at[1], xm)
    g_p = rc(gtx.at[1], grx.at[1], g_s.at[2], g_r.at[2], xp)
    g_m = rc(gtx.at[2], grx.at[2], g_s.at[3], g_r.at[3], xm)

    def bias_stage(step):
        if step == 1:
            g_half_p.wait_recv()
        if step == 2:
            g_half_m.wait_recv()
        if step == 3:
            g_p.wait_recv()
            g_m.wait_recv()
        for h in range(HEADS):
            for k in range(4):
                lanes = slice(k * 128, (k + 1) * 128)
                tile = turned[h, :, lanes]
                if (step == 1 and h < 2) or (step == 2 and h >= 2):
                    tile = tile + grx[0, h, :, lanes].astype(F32)
                if step == 3:
                    tile = tile + grx[1, h, :, lanes].astype(F32) + grx[2, h, :, lanes].astype(F32)
                    bias_grad[h, :, lanes] = tile.astype(BF)
                else:
                    gtx[step, h, :, lanes] = tile.astype(BF)
        if step == 0:
            g_half_p.start()
            g_half_m.start()
        if step == 1:
            g_p.start()
        if step == 2:
            g_m.start()

    def backward(step, carry):
        xb = lax.rem(x + jnp.where(step == 0, 2, jnp.where(step == 1, 1, jnp.where(step == 2, 3, 0))), NX)
        places, factors, deltas = [], [], []
        for q in range(2 * ROWS):
            side = yh if q < ROWS else 1 - yh
            sx, r, row = side * 4 + xb, q % ROWS, side * ROWS + q % ROWS
            places.append((q, sx, r, row))
            st = stats[row]
            f, delta = jnp.exp(m_st[sx, r] - st[0:4, :]), st[4:8, :]
            factors.append([jnp.concatenate([f[h : h + 1, :], f[h + 1 : h + 2, :]], axis=1) for h in (0, 2)])
            deltas.append([jnp.concatenate([delta[h : h + 1, :], delta[h + 1 : h + 2, :]], axis=1) for h in (0, 2)])
        for hp in range(2):
            cols = slice(hp * 256, hp * 256 + 256)
            p_cols = slice(512 + hp * 256, 768 + hp * 256)
            for i in range(4):
                rows = slice(i * 128, (i + 1) * 128)
                total = None
                for q, sx, r, row in places:
                    d_prob = nn(vals[sx, r, rows, :], dos[row, :, cols]) - deltas[q][hp]
                    prob = probs[sx, r, rows, cols].astype(F32) * factors[q][hp]
                    d_score = prob * d_prob
                    total = d_score if total is None else total + d_score
                    ds_ref[q, rows, cols] = d_score.astype(BF)
                    ds_ref[q, rows, p_cols] = prob.astype(BF)
                for j in range(2):
                    turned[hp * 2 + j, :, rows] = total[:, j * 128 : (j + 1) * 128].T
            for q, sx, r, row in places:
                d_query = nn(keys_t[sx, r, hp * 64 : hp * 64 + 64, :], ds_ref[q, :, cols])
                for j in range(2):
                    rows = slice((hp * 2 + j) * 32, (hp * 2 + j + 1) * 32)
                    dq[q, rows, :] = dq[q, rows, :] + d_query[j * 32 : (j + 1) * 32, j * 128 : (j + 1) * 128]
        for q, sx, r, row in places:
            for i in range(2):
                rows = slice(i * 256, (i + 1) * 256)
                kt[row, pl.ds(pl.multiple_of(xb * KB + i * 256, 256), 256), :] = nn(
                    ds_ref[q, rows, :], g_n[row]
                ).astype(BF)

        def block_at(back):
            return lax.rem(x + jnp.where(step == back, 2, jnp.where(step == back + 1, 1, 3)), NX)

        core_copy(xb).start()
        for s in range(3):
            @pl.when(step == s)
            def _():
                bias_stage(s)

        @pl.when(step >= 1)
        def _():
            z_stage(block_at(1))

        @pl.when(step >= 2)
        def _():
            home_stage(block_at(2))

        y_stage(xb)
        return carry

    lax.fori_loop(0, 4, backward, 0)

    for r in range(ROWS):
        dqtx[r] = dq[ROWS + r].astype(BF)
    dq_copy = rc(dqtx, dqrx, f_s.at[4], f_r.at[4], hpart)
    dq_copy.start()
    z_stage(x)
    home_stage(xs[3])
    dq_copy.wait_recv()
    for r in range(ROWS):
        d_query = (dq[r] + dqrx[r].astype(F32)) * (DH ** -0.5)
        unit_t = split_nn(w[:, 0:128], d_query) + split_nn(w[:, 384:512], dgp[r])
        dgated[r] = unit_t.T
    home_stage(x)
    bias_stage(3)
    bias_out = pltpu.make_async_copy(bias_grad, bias_hbm, o_s.at[1])
    bias_out.start()
    for j in range(4):
        @pl.when(jnp.logical_not(jnp.logical_and(self_home, lax.rem(z, 4) == j)))
        def _():
            rc(htx.at[0], frx.at[:, pl.ds(j * 32, 32)], f_s.at[0], f_r.at[j], sib).wait_recv()
    for r in range(ROWS):
        dgated[r] = dgated[r] + frx[r].astype(F32)
    normed_out = pltpu.make_async_copy(dgated, normed_hbm, o_s.at[2])
    normed_out.start()

    for copy in (bias_p, bias_m, bias_fp, bias_fm, q_send, d_send, att_copy, st_copy, back_copy, dq_copy,
                 g_half_p, g_half_m, g_p, g_m):
        copy.wait_send()
    for t in range(2):
        @pl.when(jnp.logical_not(jnp.logical_and(is_home, yl == t)))
        def _():
            key_send[t].wait_send()
    for i in range(4):
        for p in range(2):
            if goes_up(i, p):
                up(i, p).wait_send()
            if goes_down(i, p):
                down(i, p).wait_send()
        core_copy(i).wait_send()
        y_copy(i, 0).wait_send()
        y_copy(i, 1).wait_send()
        for j in range(1, 8):
            z_copy(i, j).wait_send()

        @pl.when(jnp.logical_not(jnp.logical_and(self_home, z // 2 == i)))
        def _():
            own_copy(i).wait_send()

    for i in range(8):
        to_sib(i).wait_send()

    update_out.wait()
    bias_out.wait()
    normed_out.wait()


def shards(codes, expo, tok, gain, w, wo, bias, ug):
    vm = pltpu.VMEM
    dma = pltpu.SemaphoreType.DMA
    blk = (ROWS, T, C)
    scratch = [
        vm(blk, BF), vm((HEADS, T, KB), BF),
        vm((512, C), BF), vm((C, C), BF), vm(blk, BF), vm(blk, F32), vm(blk, F32),
        vm((6, 2048, C), BF), vm((6, C, T), BF), vm((6, C, T), BF), vm((3, HEADS, T, KB), BF),
        vm((4, KB, 512), F32), vm((8, 3, KB, 512), BF), vm((3, KB, 256), F32), vm((6, C, 512), BF),
        vm((6, C, 512), BF),
        vm((8, 3, HEADS, T), F32), vm((8, 3, HEADS, T), F32), vm((8, 3, C, T), F32),
        vm((8, 3, KB, C), BF), vm((8, 3, C, KB), BF), vm((6, 1024, C), BF), vm((6, C, T), F32), vm((6, 8, T), F32),
        vm(blk, BF), vm(blk, BF), vm((ROWS, 8, T), F32), vm((ROWS, 8, T), F32), vm((ROWS, 8, T), F32),
        vm((6, 8, T), F32), vm(blk, F32),
        vm((6, KB, 1024), BF), vm((3, KB, C), BF), vm((3, 160, KB), BF),
        vm((HEADS, T, KB), F32),
        vm((6, C, T), F32), vm((6, 2048, C), BF),
        vm((4, 6, 256, C), BF), vm((4, 3, 256, C), BF), vm((4, 3, 256, C), BF), vm((4, 3, 256, C), F32),
        vm((4, 3, 256, C), BF), vm((4, 8, 3, 32, C), BF), vm((4, 3, 32, C), BF), vm(blk, BF), vm(blk, BF), vm(blk, BF),
        vm((3, HEADS, T, KB), BF), vm((3, HEADS, T, KB), BF),
        dma((4,)), dma((4,)), dma((2,)), dma((2,)), dma((2, 4, 2)), dma((2, 4, 2)), dma((8,)), dma((8,)),
        dma((2,)), dma((2,)), dma((3,)), dma((3,)), dma((4,)), dma((4,)), dma((4, 2)), dma((4, 2)),
        dma((4, 8)), dma((4, 8)), dma((5,)), dma((5,)), dma((4,)), dma((4,)), dma((3,)),
    ]
    v = pl.BlockSpec(memory_space=pltpu.VMEM)
    hbm = pl.BlockSpec(memory_space=pl.ANY)
    shapes = (
        jax.ShapeDtypeStruct(blk, BF),
        jax.ShapeDtypeStruct(blk, F32),
        jax.ShapeDtypeStruct((HEADS, T, KB), BF),
    )
    gain, expo = gain.reshape(1, C), expo.reshape(1, ROWS)
    update, d_normed, bias_grad = pl.pallas_call(
        kernel,
        out_shape=shapes,
        in_specs=[v] * 8,
        out_specs=(hbm, hbm, hbm),
        scratch_shapes=scratch,
        compiler_params=pltpu.CompilerParams(
            collective_id=0, has_side_effects=True, vmem_limit_bytes=60 * 1024 * 1024
        ),
        cost_estimate=pl.CostEstimate(flops=8_000_000_000, bytes_accessed=4_000_000, transcendentals=6_300_000),
    )(tok, codes, expo, gain, w, wo, bias, ug)
    return pl.pallas_call(
        norm_back,
        out_shape=(shapes[0], shapes[0], shapes[2]),
        in_specs=[v] * 6,
        out_specs=(v, v, v),
        compiler_params=pltpu.CompilerParams(vmem_limit_bytes=58 * 1024 * 1024),
    )(codes, expo, gain, d_normed, update, bias_grad)


def solution(mesh):
    in_specs = (
        P("row", "col", None), P("row", "col"), P(), P(), P(), P(), P(None, "col", "row"), P("row", "col", None),
    )
    out_specs = (P("row", "col", None), P("row", "col", None), P(None, "col", "row"))
    return jax.shard_map(shards, mesh=mesh, in_specs=in_specs, out_specs=out_specs, check_vma=False)
```

```python
import jax
import jax.numpy as jnp
from jax import lax
from jax.experimental import pallas as pl
from jax.experimental.pallas import tpu as pltpu
from jax.sharding import PartitionSpec as P

MASKED = -1e30
EPSILON = 1e-05
F32 = jnp.float32
BF = jnp.bfloat16
NX, NZ = 4, 8
HEADS, DH, C, T = 4, 32, 128, 128
KB = 512
ROWS = 3


def nn(a, b):
    return lax.dot_general(a, b, (((1,), (0,)), ((), ())), preferred_element_type=F32)


def nt(a, b):
    return lax.dot_general(a, b, (((1,), (1,)), ((), ())), preferred_element_type=F32)


def split_nn(w, a):
    high = a.astype(BF)
    low = (a - high.astype(F32)).astype(BF)
    return nn(w, high) + nn(w, low)


def per_head(stat):
    return jnp.concatenate(
        [jnp.broadcast_to(stat[h : h + 1, :], (DH, T)) for h in range(HEADS)], axis=0
    )


def normalised(codes, expo, r):
    value = codes[r].astype(F32) * jnp.exp2(expo[0:1, r : r + 1].astype(F32))
    centered = value - jnp.mean(value, axis=-1, keepdims=True)
    inv_std = lax.rsqrt(jnp.mean(centered * centered, axis=-1, keepdims=True) + EPSILON)
    return centered * inv_std, inv_std


def norm_back(codes, expo, gain, d_normed, update_in, bias_in, update, pair_grad, bias_grad):
    update[...] = update_in[...]
    bias_grad[...] = bias_in[...]
    for r in range(ROWS):
        unit, inv_std = normalised(codes, expo, r)
        e = d_normed[r] * gain[...]
        pair_grad[r] = (
            inv_std
            * (e - jnp.mean(e, axis=-1, keepdims=True) - unit * jnp.mean(e * unit, axis=-1, keepdims=True))
        ).astype(BF)


def kernel(
    tok, codes, expo, gain, w, wo, bias, ug,
    update_hbm, normed_hbm, bias_hbm,
    update, bias_grad,
    wt, wot, nb, gates, dgated, kn, qt, dot, bias_g, bias_t, probs, s_ref, qbd, dos,
    m_st, l_st, a_st, vals, keys_t, g_n, att_loc, st_loc, att_tx, att_rx, st_rx, back_tx, back_rx, stats, dgp,
    ds_ref, k_ref, vt_ref, turned, dq, kt, rxc, ytx, rxy, rsum, ztx, zrx, htx, frx, dqtx, dqrx, gtx, grx,
    bx_s, bx_r, ks_s, ks_r, zr_s, zr_r, sb_s, sb_r, pq_s, pq_r, ex_s, ex_r, kc_s, kc_r,
    ky_s, ky_r, zq_s, zq_r, f_s, f_r, g_s, g_r, o_s,
):
    row_id = lax.axis_index("row")
    col_id = lax.axis_index("col")
    yh, x = row_id // NX, lax.rem(row_id, NX)
    yl, z, c = col_id // 16, lax.rem(col_id, 16) // 2, lax.rem(col_id, 2)
    xs = [lax.rem(x + i, NX) for i in range(NX)]
    zs = [lax.rem(z + i, NZ) for i in range(NZ)]

    def dev(x_=x, yh_=yh, yl_=yl, z_=z, c_=c):
        return (yh_ * NX + x_, yl_ * 16 + z_ * 2 + c_)

    def rc(src, dst, send, recv, to):
        return pltpu.make_async_remote_copy(
            src_ref=src, dst_ref=dst, send_sem=send, recv_sem=recv,
            device_id=to, device_id_type=pl.DeviceIdType.MESH,
        )

    xp, xm, zp, zm = dev(x_=xs[1]), dev(x_=xs[3]), dev(z_=zs[1]), dev(z_=zs[7])
    sib = dev(c_=1 - c)
    ypart = dev(yl_=1 - yl)
    hpart = dev(yh_=1 - yh)
    cross = dev(yh_=1 - yh, yl_=1 - yl)
    is_home = yh == yl
    self_home = jnp.logical_and(is_home, jnp.logical_and(z // 4 == c, lax.rem(z, 2) == c))

    barrier = pltpu.get_barrier_semaphore()
    def greet(to):
        pl.semaphore_signal(barrier, inc=1, device_id=to, device_id_type=pl.DeviceIdType.MESH)

    for to in (xp, xm, sib, ypart, hpart, cross):
        greet(to)
    for i in range(1, 8):
        greet(dev(z_=zs[i]))
    for i in range(4):
        @pl.when(jnp.logical_not(jnp.logical_and(self_home, z // 2 == i)))
        def _():
            greet(dev(yh_=yl, yl_=yh, z_=2 * i + c, c_=z // 4))

        @pl.when(jnp.logical_not(jnp.logical_and(self_home, lax.rem(z, 4) == i)))
        def _():
            greet(dev(yh_=yl, yl_=yh, z_=4 * c + i, c_=lax.rem(z, 2)))


    gain_row = gain[...]
    for r in range(ROWS):
        nb[r] = (normalised(codes, expo, r)[0] * gain_row).astype(BF)

    pl.semaphore_wait(barrier, jnp.where(self_home, 19, 21))

    bias_p = rc(bias, bias_g.at[0], bx_s.at[0], bx_r.at[0], xp)
    bias_m = rc(bias, bias_g.at[1], bx_s.at[1], bx_r.at[1], xm)
    bias_fp = rc(bias_g.at[0, pl.ds(0, 2)], bias_g.at[2, pl.ds(0, 2)], bx_s.at[2], bx_r.at[2], xp)
    bias_fm = rc(bias_g.at[1, pl.ds(2, 2)], bias_g.at[2, pl.ds(2, 2)], bx_s.at[3], bx_r.at[3], xm)
    bias_p.start()
    bias_m.start()

    def key_at(zz, cc):
        return pl.ds(pl.multiple_of(zz * 256 + cc * 128, 128), 128)

    my_set = pl.ds(pl.multiple_of(yh * ROWS, ROWS), ROWS)
    key_send = [
        rc(nb, kn.at[pl.ds(yh * ROWS, ROWS), key_at(z, c)], ks_s.at[t], ks_r.at[yh], dev(yh_=yl, yl_=t))
        for t in range(2)
    ]
    for t in range(2):
        @pl.when(jnp.logical_not(jnp.logical_and(is_home, yl == t)))
        def _():
            key_send[t].start()

    @pl.when(is_home)
    def _():
        kn[pl.ds(yh * ROWS, ROWS), key_at(z, c), :] = nb[...]

    for q in range(4):
        wt[q * 128 : (q + 1) * 128, :] = w[:, q * 128 : (q + 1) * 128].astype(F32).T.astype(BF)
    wot[...] = wo[...].astype(F32).T.astype(BF)

    def set_of(ref, s):
        return ref.at[pl.ds(s * ROWS, ROWS)]

    for r in range(ROWS):
        n = nb[r]
        qt[yh * ROWS + r] = (nt(wt[0:128, :], n) * (DH ** -0.5)).astype(BF)
        gate = jax.nn.sigmoid(nt(wt[384:512, :], n))
        gates[r] = gate
        dg = nt(wo[...], ug[r])
        dgated[r] = dg
        dot[yh * ROWS + r] = (dg * gate).astype(BF)
    q_send = rc(set_of(qt, yh), set_of(qt, yh), pq_s.at[0], pq_r.at[0], hpart)
    d_send = rc(set_of(dot, yh), set_of(dot, yh), pq_s.at[1], pq_r.at[1], hpart)
    q_send.start()

    live = tok[...].reshape(1, 1)

    def prep(src, xb):
        for k in range(4):
            first = (yh * NX + xb) * KB + k * 128
            valid = first + lax.broadcasted_iota(jnp.int32, (128, 128), 0) < live
            for h in range(HEADS):
                tile = src[h, :, k * 128 : (k + 1) * 128].astype(F32).T
                bias_t[xb, k * 128 : (k + 1) * 128, h * 128 : (h + 1) * 128] = jnp.where(valid, tile, MASKED)

    qbd[...] = jnp.zeros_like(qbd)
    dos[...] = jnp.zeros_like(dos)

    def spread(dst, src, row):
        for h in range(HEADS):
            rows = slice(h * 32, (h + 1) * 32)
            dst[row, rows, h * 128 : (h + 1) * 128] = src[row, rows, :]

    def key_factors(row):
        for part, src in enumerate((qbd, dos)):
            g = nn(w[:, 128 + part * 128 : 256 + part * 128], src[row])
            for h in range(HEADS):
                rows = slice(part * 512 + h * 128, part * 512 + (h + 1) * 128)
                g_n[row, rows, :] = g[:, h * 128 : (h + 1) * 128].T.astype(BF)

    for r in range(ROWS):
        spread(qbd, qt, yh * ROWS + r)
        spread(dos, dot, yh * ROWS + r)

    def block(zz, cc=c):
        return kn.at[:, key_at(zz, cc)]

    def half(zz, s):
        return kn.at[pl.ds(s * ROWS, ROWS), key_at(zz, c)]

    sides = [yh, 1 - yh]

    def up(i, p):
        src = half(zs[(8 - i) % 8], sides[p])
        return rc(src, src, zr_s.at[0, i, p], zr_r.at[0, i, p], zp)

    def down(i, p):
        src = half(zs[i], sides[p])
        return rc(src, src, zr_s.at[1, i, p], zr_r.at[1, i, p], zm)

    def to_sib(i):
        return rc(block(zs[i]), block(zs[i]), sb_s.at[i], sb_r.at[i], sib)

    def from_sib(i):
        return rc(block(zs[i], 1 - c), block(zs[i], 1 - c), sb_s.at[i], sb_r.at[i], sib)

    def up_in(i, p):
        dst = half(zs[7 - i], sides[p])
        return rc(dst, dst, zr_s.at[0, i, p], zr_r.at[0, i, p], zp)

    def down_in(i, p):
        dst = half(zs[i + 1], sides[p])
        return rc(dst, dst, zr_s.at[1, i, p], zr_r.at[1, i, p], zm)

    def goes_up(i, p):
        return i < 3 or (i == 3 and p == 0)

    def goes_down(i, p):
        return i < 3 or (i == 3 and p == 1)

    def ring_step(i):
        for p in range(2):
            if goes_up(i, p):
                up_in(i, p).wait_recv()
                if goes_up(i + 1, p):
                    up(i + 1, p).start()
            if goes_down(i, p):
                down_in(i, p).wait_recv()
                if goes_down(i + 1, p):
                    down(i + 1, p).start()
        if i < 3:
            to_sib(7 - i).start()
            to_sib(i + 1).start()
        else:
            to_sib(4).start()

    for p in range(2):
        @pl.when(jnp.logical_not(jnp.logical_and(is_home, p == 0)))
        def _():
            rc(nb, half(z, sides[p]), ks_s.at[0], ks_r.at[sides[p]], sib).wait_recv()

        up(0, p).start()
        down(0, p).start()
    to_sib(0).start()
    prep(bias, x)
    for r in range(ROWS):
        key_factors(yh * ROWS + r)
    bias_p.wait_recv()
    bias_fp.start()
    bias_m.wait_recv()
    bias_fm.start()
    ring_step(0)
    prep(bias_g.at[0], xs[3])
    prep(bias_g.at[1], xs[1])

    zb = z // 2
    even = lax.rem(z, 2) == 0
    near = jnp.where(even, zb + 3, zb + 1)
    far = jnp.where(even, zb + 1, zb + 3)

    turned_round = zb == xs[2]
    order = [jnp.where(turned_round, near, zb), jnp.where(turned_round, zb, near), far, zb + 2]

    @pl.when(turned_round)
    def _():
        ring_step(1)

    def arrive(phase):
        for i in ((0, 1, 7), (2, 6), (3, 5), (4,))[phase]:
            from_sib(i).wait_recv()

    for r in range(ROWS):
        vt_ref[r, 64:80, :] = jnp.ones((16, KB), BF)
        vt_ref[r, 144:160, :] = jnp.ones((16, KB), BF)

    att_copy = rc(att_tx, att_rx, ex_s.at[0], ex_r.at[0], hpart)
    st_copy = rc(set_of(st_loc, 1 - yh), st_rx, ex_s.at[1], ex_r.at[1], hpart)
    back_copy = rc(back_tx, back_rx, ex_s.at[2], ex_r.at[2], hpart)

    def combine(side, r):
        m_all = [m_st[side * 4 + i, r] for i in range(4)]
        top_m = jnp.maximum(jnp.maximum(m_all[0], m_all[1]), jnp.maximum(m_all[2], m_all[3]))
        total = jnp.zeros((HEADS, T), F32)
        weighted = jnp.zeros((C, T), F32)
        for i in range(4):
            f = jnp.exp(m_all[i] - top_m)
            total = total + f * l_st[side * 4 + i, r]
            weighted = weighted + per_head(f) * a_st[side * 4 + i, r]
        st_loc[side * ROWS + r, 0:4, :] = top_m
        st_loc[side * ROWS + r, 4:8, :] = total
        return weighted

    def forward(u, carry):
        phase, second = u // 2, lax.rem(u, 2)
        side = lax.rem(jnp.where(phase == 3, 1 - yh, yh) + second, 2)
        xb = lax.rem(
            jnp.where(phase == 0, order[0], jnp.where(phase == 1, order[1], jnp.where(phase == 2, far, zb + 2))), NX
        )
        sx = side * 4 + xb

        for i in range(4):
            @pl.when(u == (jnp.where(turned_round, 0, 2) if i == 1 else 2 * i))
            def _():
                arrive(i)

        @pl.when(jnp.logical_and(second == 0, xb == xs[2]))
        def _():
            bias_fp.wait_recv()
            bias_fm.wait_recv()
            prep(bias_g.at[2], xs[2])

        for i in range(1, 4):
            @pl.when(u == (jnp.where(turned_round, -1, 1) if i == 1 else 2 * i - 1))
            def _():
                ring_step(i)

        @pl.when(u == 1)
        def _():
            rc(set_of(qt, yh), set_of(qt, 1 - yh), pq_s.at[0], pq_r.at[0], hpart).wait_recv()
            d_send.start()
            for r in range(ROWS):
                spread(qbd, qt, (1 - yh) * ROWS + r)

        for r in range(ROWS):
            row = side * ROWS + r
            n = kn[row, pl.ds(pl.multiple_of(xb * KB, KB), KB), :]
            kv = nn(n, w[:, 128:384]).astype(BF)
            kvt = nt(wt[128:384, :], n).astype(BF)
            k_ref[r] = kv[:, 0:128]
            vals[sx, r] = kv[:, 128:256]
            keys_t[sx, r] = kvt[0:128, :]
            vt_ref[r, 0:64, :] = kvt[128:192, :]
            vt_ref[r, 80:144, :] = kvt[192:256, :]

        items = [(r, hp) for r in range(ROWS) for hp in range(2)]
        tops = {}

        def score(t):
            r, hp = items[t]
            cols = slice(hp * 256, hp * 256 + 256)
            q2 = qbd[side * ROWS + r, :, cols]
            top = None
            for i in range(4):
                rows = slice(i * 128, (i + 1) * 128)
                s = nn(k_ref[r, rows, :], q2) + bias_t[xb, rows, cols]
                s_ref[t % 3, rows, :] = s
                part = jnp.max(s.reshape(16, 8, 256), axis=0)
                top = part if top is None else jnp.maximum(top, part)
            tops[t] = jnp.max(top, axis=0, keepdims=True)

        def weigh(t):
            r, hp = items[t]
            cols = slice(hp * 256, hp * 256 + 256)
            for i in range(4):
                rows = slice(i * 128, (i + 1) * 128)
                probs[sx, r, rows, cols] = jnp.exp(s_ref[t % 3, rows, :] - tops[t]).astype(BF)

        def attend(t):
            r, hp = items[t]
            cols = slice(hp * 256, hp * 256 + 256)
            a = nn(vt_ref[r, hp * 80 : hp * 80 + 80, :], probs[sx, r, :, cols])
            for j in range(2):
                h = hp * 2 + j
                lanes = slice(j * 128, (j + 1) * 128)
                m_st[sx, r, h : h + 1, :] = tops[t][:, lanes]
                l_st[sx, r, h : h + 1, :] = a[64:65, lanes]
                a_st[sx, r, h * 32 : (h + 1) * 32, :] = a[j * 32 : (j + 1) * 32, lanes]

        for t in range(8):
            if t < 6:
                score(t)
            if 1 <= t < 7:
                weigh(t - 1)
            if t >= 2:
                attend(t - 2)

        @pl.when(u == 6)
        def _():
            for r in range(ROWS):
                att_tx[r] = combine(1 - yh, r).astype(BF)
            att_copy.start()
            st_copy.start()

        return carry

    lax.fori_loop(0, 8, forward, 0)

    for r in range(ROWS):
        att_loc[yh * ROWS + r] = combine(yh, r)
    att_copy.wait_recv()
    st_copy.wait_recv()
    for r in range(ROWS):
        mine = yh * ROWS + r
        ma, la = st_loc[mine, 0:4, :], st_loc[mine, 4:8, :]
        mb, lb = st_rx[r, 0:4, :], st_rx[r, 4:8, :]
        top_m = jnp.maximum(ma, mb)
        fa, fb = jnp.exp(ma - top_m), jnp.exp(mb - top_m)
        total = fa * la + fb * lb
        attended = (per_head(fa) * att_loc[mine] + per_head(fb) * att_rx[r].astype(F32)) / per_head(total)
        gate = gates[r]
        product = dot[mine].astype(F32) * attended
        lse = top_m + jnp.log(total)
        stats[mine, 0:4, :] = lse
        back_tx[r, 0:4, :] = lse
        for h in range(HEADS):
            delta = jnp.sum(product[h * 32 : (h + 1) * 32, :], axis=0, keepdims=True)
            stats[mine, 4 + h : 5 + h, :] = delta
            back_tx[r, 4 + h : 5 + h, :] = delta
        att_loc[mine] = attended
    back_copy.start()
    for r in range(ROWS):
        attended = att_loc[yh * ROWS + r]
        gate = gates[r]
        dgp[r] = dgated[r] * attended * gate * (1.0 - gate)
        update[r] = nn(wot[...], (gate * attended).astype(BF)).T.astype(BF)
    update_out = pltpu.make_async_copy(update, update_hbm, o_s.at[0])
    update_out.start()
    rc(set_of(dot, yh), set_of(dot, 1 - yh), pq_s.at[1], pq_r.at[1], hpart).wait_recv()
    for r in range(ROWS):
        spread(dos, dot, (1 - yh) * ROWS + r)
        key_factors((1 - yh) * ROWS + r)
    back_copy.wait_recv()
    for r in range(ROWS):
        stats[(1 - yh) * ROWS + r] = back_rx[r]
    dq[...] = jnp.zeros_like(dq)

    def core_half(xb, cc):
        return pl.ds(pl.multiple_of(xb * KB + cc * 256, 256), 256)

    def z_part(zz):
        return pl.ds(pl.multiple_of(zz * 32, 32), 32)

    def core_copy(xb):
        return rc(kt.at[:, core_half(xb, 1 - c)], rxc.at[xb], kc_s.at[xb], kc_r.at[xb], sib)

    def y_copy(xb, p):
        part = pl.ds(p * 128, 128)
        return rc(ytx.at[xb, :, part], rxy.at[xb, :, part], ky_s.at[xb, p], ky_r.at[xb, p], ypart)

    def z_copy(xb, i):
        return rc(
            ztx.at[xb, :, z_part(zs[i])], zrx.at[xb, i], zq_s.at[xb, i], zq_r.at[xb, i], dev(z_=zs[i])
        )

    def own_copy(xb):
        part = lax.rem(z, 4)
        return rc(
            htx.at[xb], frx.at[:, z_part(part)], f_s.at[xb], f_r.at[part],
            dev(yh_=yl, yl_=yh, z_=2 * xb + c, c_=z // 4),
        )

    def key_part(xb, p):
        return pl.ds(pl.multiple_of(xb * KB + c * 256 + p * 128, 128), 128)

    def y_stage(xb):
        core_copy(xb).wait_recv()
        for p in range(2):
            part = slice(p * 128, (p + 1) * 128)
            for r in range(ROWS):
                theirs = (1 - yl) * ROWS + r
                ytx[xb, r, part, :] = (
                    kt[theirs, key_part(xb, p), :].astype(F32) + rxc[xb, theirs, part, :].astype(F32)
                ).astype(BF)
            y_copy(xb, p).start()

    def z_stage(xb):
        for p in range(2):
            part = slice(p * 128, (p + 1) * 128)
            y_copy(xb, p).wait_recv()
            for r in range(ROWS):
                ours = yl * ROWS + r
                total = kt[ours, key_part(xb, p), :].astype(F32) + rxc[xb, ours, part, :].astype(F32)
                total = total + rxy[xb, r, part, :].astype(F32)
                rsum[xb, r, part, :] = total
                ztx[xb, r, part, :] = total.astype(BF)
            for i in (4, 3, 5, 2, 6, 1, 7):
                @pl.when(zs[i] // 4 == p)
                def _():
                    z_copy(xb, i).start()

    def home_stage(xb):
        total = rsum[xb, :, z_part(z), :]
        for i in range(1, 8):
            z_copy(xb, i).wait_recv()
            total = total + zrx[xb, i].astype(F32)
        htx[xb] = total.astype(BF)
        stays = jnp.logical_and(self_home, z // 2 == xb)

        @pl.when(stays)
        def _():
            frx[:, z_part(lax.rem(z, 4)), :] = htx[xb]

        @pl.when(jnp.logical_not(stays))
        def _():
            own_copy(xb).start()

    g_half_p = rc(gtx.at[0, pl.ds(0, 2)], grx.at[0, pl.ds(0, 2)], g_s.at[0], g_r.at[0], xp)
    g_half_m = rc(gtx.at[0, pl.ds(2, 2)], grx.at[0, pl.ds(2, 2)], g_s.at[1], g_r.at[1], xm)
    g_p = rc(gtx.at[1], grx.at[1], g_s.at[2], g_r.at[2], xp)
    g_m = rc(gtx.at[2], grx.at[2], g_s.at[3], g_r.at[3], xm)

    def bias_stage(step):
        if step == 1:
            g_half_p.wait_recv()
        if step == 2:
            g_half_m.wait_recv()
        if step == 3:
            g_p.wait_recv()
            g_m.wait_recv()
        for h in range(HEADS):
            for k in range(4):
                lanes = slice(k * 128, (k + 1) * 128)
                tile = turned[h, :, lanes]
                if (step == 1 and h < 2) or (step == 2 and h >= 2):
                    tile = tile + grx[0, h, :, lanes].astype(F32)
                if step == 3:
                    tile = tile + grx[1, h, :, lanes].astype(F32) + grx[2, h, :, lanes].astype(F32)
                    bias_grad[h, :, lanes] = tile.astype(BF)
                else:
                    gtx[step, h, :, lanes] = tile.astype(BF)
        if step == 0:
            g_half_p.start()
            g_half_m.start()
        if step == 1:
            g_p.start()
        if step == 2:
            g_m.start()

    def backward(step, carry):
        xb = lax.rem(x + jnp.where(step == 0, 2, jnp.where(step == 1, 1, jnp.where(step == 2, 3, 0))), NX)
        places, factors, deltas = [], [], []
        for q in range(2 * ROWS):
            side = yh if q < ROWS else 1 - yh
            sx, r, row = side * 4 + xb, q % ROWS, side * ROWS + q % ROWS
            places.append((q, sx, r, row))
            st = stats[row]
            f, delta = jnp.exp(m_st[sx, r] - st[0:4, :]), st[4:8, :]
            factors.append([jnp.concatenate([f[h : h + 1, :], f[h + 1 : h + 2, :]], axis=1) for h in (0, 2)])
            deltas.append([jnp.concatenate([delta[h : h + 1, :], delta[h + 1 : h + 2, :]], axis=1) for h in (0, 2)])
        for hp in range(2):
            cols = slice(hp * 256, hp * 256 + 256)
            p_cols = slice(512 + hp * 256, 768 + hp * 256)
            for i in range(4):
                rows = slice(i * 128, (i + 1) * 128)
                total = None
                for q, sx, r, row in places:
                    d_prob = nn(vals[sx, r, rows, :], dos[row, :, cols]) - deltas[q][hp]
                    prob = probs[sx, r, rows, cols].astype(F32) * factors[q][hp]
                    d_score = prob * d_prob
                    total = d_score if total is None else total + d_score
                    ds_ref[q, rows, cols] = d_score.astype(BF)
                    ds_ref[q, rows, p_cols] = prob.astype(BF)
                for j in range(2):
                    turned[hp * 2 + j, :, rows] = total[:, j * 128 : (j + 1) * 128].T
            for q, sx, r, row in places:
                d_query = nn(keys_t[sx, r, hp * 64 : hp * 64 + 64, :], ds_ref[q, :, cols])
                for j in range(2):
                    rows = slice((hp * 2 + j) * 32, (hp * 2 + j + 1) * 32)
                    dq[q, rows, :] = dq[q, rows, :] + d_query[j * 32 : (j + 1) * 32, j * 128 : (j + 1) * 128]
        for q, sx, r, row in places:
            for i in range(2):
                rows = slice(i * 256, (i + 1) * 256)
                kt[row, pl.ds(pl.multiple_of(xb * KB + i * 256, 256), 256), :] = nn(
                    ds_ref[q, rows, :], g_n[row]
                ).astype(BF)

        def block_at(back):
            return lax.rem(x + jnp.where(step == back, 2, jnp.where(step == back + 1, 1, 3)), NX)

        core_copy(xb).start()
        for s in range(3):
            @pl.when(step == s)
            def _():
                bias_stage(s)

        @pl.when(step >= 1)
        def _():
            z_stage(block_at(1))

        @pl.when(step >= 2)
        def _():
            home_stage(block_at(2))

        y_stage(xb)
        return carry

    lax.fori_loop(0, 4, backward, 0)

    for r in range(ROWS):
        dqtx[r] = dq[ROWS + r].astype(BF)
    dq_copy = rc(dqtx, dqrx, f_s.at[4], f_r.at[4], hpart)
    dq_copy.start()
    z_stage(x)
    home_stage(xs[3])
    dq_copy.wait_recv()
    for r in range(ROWS):
        d_query = (dq[r] + dqrx[r].astype(F32)) * (DH ** -0.5)
        unit_t = split_nn(w[:, 0:128], d_query) + split_nn(w[:, 384:512], dgp[r])
        dgated[r] = unit_t.T
    home_stage(x)
    bias_stage(3)
    bias_out = pltpu.make_async_copy(bias_grad, bias_hbm, o_s.at[1])
    bias_out.start()
    for j in range(4):
        @pl.when(jnp.logical_not(jnp.logical_and(self_home, lax.rem(z, 4) == j)))
        def _():
            rc(htx.at[0], frx.at[:, pl.ds(j * 32, 32)], f_s.at[0], f_r.at[j], sib).wait_recv()
    for r in range(ROWS):
        dgated[r] = dgated[r] + frx[r].astype(F32)
    normed_out = pltpu.make_async_copy(dgated, normed_hbm, o_s.at[2])
    normed_out.start()

    for copy in (bias_p, bias_m, bias_fp, bias_fm, q_send, d_send, att_copy, st_copy, back_copy, dq_copy,
                 g_half_p, g_half_m, g_p, g_m):
        copy.wait_send()
    for t in range(2):
        @pl.when(jnp.logical_not(jnp.logical_and(is_home, yl == t)))
        def _():
            key_send[t].wait_send()
    for i in range(4):
        for p in range(2):
            if goes_up(i, p):
                up(i, p).wait_send()
            if goes_down(i, p):
                down(i, p).wait_send()
        core_copy(i).wait_send()
        y_copy(i, 0).wait_send()
        y_copy(i, 1).wait_send()
        for j in range(1, 8):
            z_copy(i, j).wait_send()

        @pl.when(jnp.logical_not(jnp.logical_and(self_home, z // 2 == i)))
        def _():
            own_copy(i).wait_send()

    for i in range(8):
        to_sib(i).wait_send()

    update_out.wait()
    bias_out.wait()
    normed_out.wait()


def shards(codes, expo, tok, gain, w, wo, bias, ug):
    vm = pltpu.VMEM
    dma = pltpu.SemaphoreType.DMA
    blk = (ROWS, T, C)
    scratch = [
        vm(blk, BF), vm((HEADS, T, KB), BF),
        vm((512, C), BF), vm((C, C), BF), vm(blk, BF), vm(blk, F32), vm(blk, F32),
        vm((6, 2048, C), BF), vm((6, C, T), BF), vm((6, C, T), BF), vm((3, HEADS, T, KB), BF),
        vm((4, KB, 512), F32), vm((8, 3, KB, 512), BF), vm((3, KB, 256), F32), vm((6, C, 512), BF),
        vm((6, C, 512), BF),
        vm((8, 3, HEADS, T), F32), vm((8, 3, HEADS, T), F32), vm((8, 3, C, T), F32),
        vm((8, 3, KB, C), BF), vm((8, 3, C, KB), BF), vm((6, 1024, C), BF), vm((6, C, T), F32), vm((6, 8, T), F32),
        vm(blk, BF), vm(blk, BF), vm((ROWS, 8, T), F32), vm((ROWS, 8, T), F32), vm((ROWS, 8, T), F32),
        vm((6, 8, T), F32), vm(blk, F32),
        vm((6, KB, 1024), BF), vm((3, KB, C), BF), vm((3, 160, KB), BF),
        vm((HEADS, T, KB), F32),
        vm((6, C, T), F32), vm((6, 2048, C), BF),
        vm((4, 6, 256, C), BF), vm((4, 3, 256, C), BF), vm((4, 3, 256, C), BF), vm((4, 3, 256, C), F32),
        vm((4, 3, 256, C), BF), vm((4, 8, 3, 32, C), BF), vm((4, 3, 32, C), BF), vm(blk, BF), vm(blk, BF), vm(blk, BF),
        vm((3, HEADS, T, KB), BF), vm((3, HEADS, T, KB), BF),
        dma((4,)), dma((4,)), dma((2,)), dma((2,)), dma((2, 4, 2)), dma((2, 4, 2)), dma((8,)), dma((8,)),
        dma((2,)), dma((2,)), dma((3,)), dma((3,)), dma((4,)), dma((4,)), dma((4, 2)), dma((4, 2)),
        dma((4, 8)), dma((4, 8)), dma((5,)), dma((5,)), dma((4,)), dma((4,)), dma((3,)),
    ]
    v = pl.BlockSpec(memory_space=pltpu.VMEM)
    hbm = pl.BlockSpec(memory_space=pl.ANY)
    shapes = (
        jax.ShapeDtypeStruct(blk, BF),
        jax.ShapeDtypeStruct(blk, F32),
        jax.ShapeDtypeStruct((HEADS, T, KB), BF),
    )
    gain, expo = gain.reshape(1, C), expo.reshape(1, ROWS)
    update, d_normed, bias_grad = pl.pallas_call(
        kernel,
        out_shape=shapes,
        in_specs=[v] * 8,
        out_specs=(hbm, hbm, hbm),
        scratch_shapes=scratch,
        compiler_params=pltpu.CompilerParams(
            collective_id=0, has_side_effects=True, vmem_limit_bytes=60 * 1024 * 1024
        ),
        cost_estimate=pl.CostEstimate(flops=8_000_000_000, bytes_accessed=4_000_000, transcendentals=6_300_000),
    )(tok, codes, expo, gain, w, wo, bias, ug)
    return pl.pallas_call(
        norm_back,
        out_shape=(shapes[0], shapes[0], shapes[2]),
        in_specs=[v] * 6,
        out_specs=(v, v, v),
        compiler_params=pltpu.CompilerParams(vmem_limit_bytes=58 * 1024 * 1024),
    )(codes, expo, gain, d_normed, update, bias_grad)


def solution(mesh):
    in_specs = (
        P("row", "col", None), P("row", "col"), P(), P(), P(), P(), P(None, "col", "row"), P("row", "col", None),
    )
    out_specs = (P("row", "col", None), P("row", "col", None), P(None, "col", "row"))
    return jax.shard_map(shards, mesh=mesh, in_specs=in_specs, out_specs=out_specs, check_vma=False)
```

```python
import jax
import jax.numpy as jnp
from jax import lax
from jax.experimental import pallas as pl
from jax.experimental.pallas import tpu as pltpu
from jax.sharding import PartitionSpec as P

MASKED = -1e30
EPSILON = 1e-05
F32 = jnp.float32
BF = jnp.bfloat16
NX, NZ = 4, 8
HEADS, DH, C, T = 4, 32, 128, 128
KB = 512
ROWS = 3


def nn(a, b):
    return lax.dot_general(a, b, (((1,), (0,)), ((), ())), preferred_element_type=F32)


def nt(a, b):
    return lax.dot_general(a, b, (((1,), (1,)), ((), ())), preferred_element_type=F32)


def split_nn(w, a):
    high = a.astype(BF)
    low = (a - high.astype(F32)).astype(BF)
    return nn(w, high) + nn(w, low)


def per_head(stat):
    return jnp.concatenate(
        [jnp.broadcast_to(stat[h : h + 1, :], (DH, T)) for h in range(HEADS)], axis=0
    )


def normalised(codes, expo, r):
    value = codes[r].astype(F32) * jnp.exp2(expo[0:1, r : r + 1].astype(F32))
    centered = value - jnp.mean(value, axis=-1, keepdims=True)
    inv_std = lax.rsqrt(jnp.mean(centered * centered, axis=-1, keepdims=True) + EPSILON)
    return centered * inv_std, inv_std


def norm_back(codes, expo, gain, d_normed, update_in, bias_in, update, pair_grad, bias_grad):
    update[...] = update_in[...]
    bias_grad[...] = bias_in[...]
    for r in range(ROWS):
        unit, inv_std = normalised(codes, expo, r)
        e = d_normed[r] * gain[...]
        pair_grad[r] = (
            inv_std
            * (e - jnp.mean(e, axis=-1, keepdims=True) - unit * jnp.mean(e * unit, axis=-1, keepdims=True))
        ).astype(BF)


def kernel(
    tok, codes, expo, gain, w, wo, bias, ug,
    update_hbm, normed_hbm, bias_hbm,
    update, bias_grad,
    wt, wot, nb, gates, dgated, kn, qt, dot, bias_g, bias_t, probs, s_ref, qbd, dos,
    m_st, l_st, a_st, vals, keys_t, g_n, att_loc, st_loc, att_tx, att_rx, st_rx, back_tx, back_rx, stats, dgp,
    ds_ref, k_ref, vt_ref, turned, dq, kt, rxc, ytx, rxy, rsum, ztx, zrx, htx, frx, dqtx, dqrx, gtx, grx,
    bx_s, bx_r, ks_s, ks_r, zr_s, zr_r, sb_s, sb_r, pq_s, pq_r, ex_s, ex_r, kc_s, kc_r,
    ky_s, ky_r, zq_s, zq_r, f_s, f_r, g_s, g_r, o_s,
):
    row_id = lax.axis_index("row")
    col_id = lax.axis_index("col")
    yh, x = row_id // NX, lax.rem(row_id, NX)
    yl, z, c = col_id // 16, lax.rem(col_id, 16) // 2, lax.rem(col_id, 2)
    xs = [lax.rem(x + i, NX) for i in range(NX)]
    zs = [lax.rem(z + i, NZ) for i in range(NZ)]

    def dev(x_=x, yh_=yh, yl_=yl, z_=z, c_=c):
        return (yh_ * NX + x_, yl_ * 16 + z_ * 2 + c_)

    def rc(src, dst, send, recv, to):
        return pltpu.make_async_remote_copy(
            src_ref=src, dst_ref=dst, send_sem=send, recv_sem=recv,
            device_id=to, device_id_type=pl.DeviceIdType.MESH,
        )

    xp, xm, zp, zm = dev(x_=xs[1]), dev(x_=xs[3]), dev(z_=zs[1]), dev(z_=zs[7])
    sib = dev(c_=1 - c)
    ypart = dev(yl_=1 - yl)
    hpart = dev(yh_=1 - yh)
    cross = dev(yh_=1 - yh, yl_=1 - yl)
    is_home = yh == yl
    self_home = jnp.logical_and(is_home, jnp.logical_and(z // 4 == c, lax.rem(z, 2) == c))

    barrier = pltpu.get_barrier_semaphore()
    def greet(to):
        pl.semaphore_signal(barrier, inc=1, device_id=to, device_id_type=pl.DeviceIdType.MESH)

    for to in (xp, xm, sib, ypart, hpart, cross):
        greet(to)
    for i in range(1, 8):
        greet(dev(z_=zs[i]))
    for i in range(4):
        @pl.when(jnp.logical_not(jnp.logical_and(self_home, z // 2 == i)))
        def _():
            greet(dev(yh_=yl, yl_=yh, z_=2 * i + c, c_=z // 4))

        @pl.when(jnp.logical_not(jnp.logical_and(self_home, lax.rem(z, 4) == i)))
        def _():
            greet(dev(yh_=yl, yl_=yh, z_=4 * c + i, c_=lax.rem(z, 2)))


    gain_row = gain[...]
    for r in range(ROWS):
        nb[r] = (normalised(codes, expo, r)[0] * gain_row).astype(BF)

    pl.semaphore_wait(barrier, jnp.where(self_home, 19, 21))

    bias_p = rc(bias, bias_g.at[0], bx_s.at[0], bx_r.at[0], xp)
    bias_m = rc(bias, bias_g.at[1], bx_s.at[1], bx_r.at[1], xm)
    bias_fp = rc(bias_g.at[0, pl.ds(0, 2)], bias_g.at[2, pl.ds(0, 2)], bx_s.at[2], bx_r.at[2], xp)
    bias_fm = rc(bias_g.at[1, pl.ds(2, 2)], bias_g.at[2, pl.ds(2, 2)], bx_s.at[3], bx_r.at[3], xm)
    bias_p.start()
    bias_m.start()

    def key_at(zz, cc):
        return pl.ds(pl.multiple_of(zz * 256 + cc * 128, 128), 128)

    my_set = pl.ds(pl.multiple_of(yh * ROWS, ROWS), ROWS)
    key_send = [
        rc(nb, kn.at[pl.ds(yh * ROWS, ROWS), key_at(z, c)], ks_s.at[t], ks_r.at[yh], dev(yh_=yl, yl_=t))
        for t in range(2)
    ]
    for t in range(2):
        @pl.when(jnp.logical_not(jnp.logical_and(is_home, yl == t)))
        def _():
            key_send[t].start()

    @pl.when(is_home)
    def _():
        kn[pl.ds(yh * ROWS, ROWS), key_at(z, c), :] = nb[...]

    for q in range(4):
        wt[q * 128 : (q + 1) * 128, :] = w[:, q * 128 : (q + 1) * 128].astype(F32).T.astype(BF)
    wot[...] = wo[...].astype(F32).T.astype(BF)

    def set_of(ref, s):
        return ref.at[pl.ds(s * ROWS, ROWS)]

    for r in range(ROWS):
        n = nb[r]
        qt[yh * ROWS + r] = (nt(wt[0:128, :], n) * (DH ** -0.5)).astype(BF)
        gate = jax.nn.sigmoid(nt(wt[384:512, :], n))
        gates[r] = gate
        dg = nt(wo[...], ug[r])
        dgated[r] = dg
        dot[yh * ROWS + r] = (dg * gate).astype(BF)
    q_send = rc(set_of(qt, yh), set_of(qt, yh), pq_s.at[0], pq_r.at[0], hpart)
    d_send = rc(set_of(dot, yh), set_of(dot, yh), pq_s.at[1], pq_r.at[1], hpart)
    q_send.start()

    live = tok[...].reshape(1, 1)

    def prep(src, xb):
        for k in range(4):
            first = (yh * NX + xb) * KB + k * 128
            valid = first + lax.broadcasted_iota(jnp.int32, (128, 128), 0) < live
            for h in range(HEADS):
                tile = src[h, :, k * 128 : (k + 1) * 128].astype(F32).T
                bias_t[xb, k * 128 : (k + 1) * 128, h * 128 : (h + 1) * 128] = jnp.where(valid, tile, MASKED)

    qbd[...] = jnp.zeros_like(qbd)
    dos[...] = jnp.zeros_like(dos)

    def spread(dst, src, row):
        for h in range(HEADS):
            rows = slice(h * 32, (h + 1) * 32)
            dst[row, rows, h * 128 : (h + 1) * 128] = src[row, rows, :]

    def key_factors(row):
        for part, src in enumerate((qbd, dos)):
            g = nn(w[:, 128 + part * 128 : 256 + part * 128], src[row])
            for h in range(HEADS):
                rows = slice(part * 512 + h * 128, part * 512 + (h + 1) * 128)
                g_n[row, rows, :] = g[:, h * 128 : (h + 1) * 128].T.astype(BF)

    for r in range(ROWS):
        spread(qbd, qt, yh * ROWS + r)
        spread(dos, dot, yh * ROWS + r)

    def block(zz, cc=c):
        return kn.at[:, key_at(zz, cc)]

    def half(zz, s):
        return kn.at[pl.ds(s * ROWS, ROWS), key_at(zz, c)]

    sides = [yh, 1 - yh]

    def up(i, p):
        src = half(zs[(8 - i) % 8], sides[p])
        return rc(src, src, zr_s.at[0, i, p], zr_r.at[0, i, p], zp)

    def down(i, p):
        src = half(zs[i], sides[p])
        return rc(src, src, zr_s.at[1, i, p], zr_r.at[1, i, p], zm)

    def to_sib(i):
        return rc(block(zs[i]), block(zs[i]), sb_s.at[i], sb_r.at[i], sib)

    def from_sib(i):
        return rc(block(zs[i], 1 - c), block(zs[i], 1 - c), sb_s.at[i], sb_r.at[i], sib)

    def up_in(i, p):
        dst = half(zs[7 - i], sides[p])
        return rc(dst, dst, zr_s.at[0, i, p], zr_r.at[0, i, p], zp)

    def down_in(i, p):
        dst = half(zs[i + 1], sides[p])
        return rc(dst, dst, zr_s.at[1, i, p], zr_r.at[1, i, p], zm)

    def goes_up(i, p):
        return i < 3 or (i == 3 and p == 0)

    def goes_down(i, p):
        return i < 3 or (i == 3 and p == 1)

    def ring_step(i):
        for p in range(2):
            if goes_up(i, p):
                up_in(i, p).wait_recv()
                if goes_up(i + 1, p):
                    up(i + 1, p).start()
            if goes_down(i, p):
                down_in(i, p).wait_recv()
                if goes_down(i + 1, p):
                    down(i + 1, p).start()
        if i < 3:
            to_sib(7 - i).start()
            to_sib(i + 1).start()
        else:
            to_sib(4).start()

    for p in range(2):
        @pl.when(jnp.logical_not(jnp.logical_and(is_home, p == 0)))
        def _():
            rc(nb, half(z, sides[p]), ks_s.at[0], ks_r.at[sides[p]], sib).wait_recv()

        up(0, p).start()
        down(0, p).start()
    to_sib(0).start()
    prep(bias, x)
    for r in range(ROWS):
        key_factors(yh * ROWS + r)
    bias_p.wait_recv()
    bias_fp.start()
    bias_m.wait_recv()
    bias_fm.start()
    ring_step(0)
    prep(bias_g.at[0], xs[3])
    prep(bias_g.at[1], xs[1])

    zb = z // 2
    even = lax.rem(z, 2) == 0
    near = jnp.where(even, zb + 3, zb + 1)
    far = jnp.where(even, zb + 1, zb + 3)

    turned_round = zb == xs[2]
    order = [jnp.where(turned_round, near, zb), jnp.where(turned_round, zb, near), far, zb + 2]

    @pl.when(turned_round)
    def _():
        ring_step(1)

    def arrive(phase):
        for i in ((0, 1, 7), (2, 6), (3, 5), (4,))[phase]:
            from_sib(i).wait_recv()

    for r in range(ROWS):
        vt_ref[r, 64:80, :] = jnp.ones((16, KB), BF)
        vt_ref[r, 144:160, :] = jnp.ones((16, KB), BF)

    att_copy = rc(att_tx, att_rx, ex_s.at[0], ex_r.at[0], hpart)
    st_copy = rc(set_of(st_loc, 1 - yh), st_rx, ex_s.at[1], ex_r.at[1], hpart)
    back_copy = rc(back_tx, back_rx, ex_s.at[2], ex_r.at[2], hpart)

    def combine(side, r):
        m_all = [m_st[side * 4 + i, r] for i in range(4)]
        top_m = jnp.maximum(jnp.maximum(m_all[0], m_all[1]), jnp.maximum(m_all[2], m_all[3]))
        total = jnp.zeros((HEADS, T), F32)
        weighted = jnp.zeros((C, T), F32)
        for i in range(4):
            f = jnp.exp(m_all[i] - top_m)
            total = total + f * l_st[side * 4 + i, r]
            weighted = weighted + per_head(f) * a_st[side * 4 + i, r]
        st_loc[side * ROWS + r, 0:4, :] = top_m
        st_loc[side * ROWS + r, 4:8, :] = total
        return weighted

    def forward(u, carry):
        phase, second = u // 2, lax.rem(u, 2)
        side = lax.rem(jnp.where(phase == 3, 1 - yh, yh) + second, 2)
        xb = lax.rem(
            jnp.where(phase == 0, order[0], jnp.where(phase == 1, order[1], jnp.where(phase == 2, far, zb + 2))), NX
        )
        sx = side * 4 + xb

        for i in range(4):
            @pl.when(u == (jnp.where(turned_round, 0, 2) if i == 1 else 2 * i))
            def _():
                arrive(i)

        @pl.when(jnp.logical_and(second == 0, xb == xs[2]))
        def _():
            bias_fp.wait_recv()
            bias_fm.wait_recv()
            prep(bias_g.at[2], xs[2])

        for i in range(1, 4):
            @pl.when(u == (jnp.where(turned_round, -1, 1) if i == 1 else 2 * i - 1))
            def _():
                ring_step(i)

        @pl.when(u == 1)
        def _():
            rc(set_of(qt, yh), set_of(qt, 1 - yh), pq_s.at[0], pq_r.at[0], hpart).wait_recv()
            d_send.start()
            for r in range(ROWS):
                spread(qbd, qt, (1 - yh) * ROWS + r)

        for r in range(ROWS):
            row = side * ROWS + r
            n = kn[row, pl.ds(pl.multiple_of(xb * KB, KB), KB), :]
            kv = nn(n, w[:, 128:384]).astype(BF)
            kvt = nt(wt[128:384, :], n).astype(BF)
            k_ref[r] = kv[:, 0:128]
            vals[sx, r] = kv[:, 128:256]
            keys_t[sx, r] = kvt[0:128, :]
            vt_ref[r, 0:64, :] = kvt[128:192, :]
            vt_ref[r, 80:144, :] = kvt[192:256, :]

        items = [(r, hp) for r in range(ROWS) for hp in range(2)]
        tops = {}

        def score(t):
            r, hp = items[t]
            cols = slice(hp * 256, hp * 256 + 256)
            q2 = qbd[side * ROWS + r, :, cols]
            top = None
            for i in range(4):
                rows = slice(i * 128, (i + 1) * 128)
                s = nn(k_ref[r, rows, :], q2) + bias_t[xb, rows, cols]
                s_ref[t % 3, rows, :] = s
                part = jnp.max(s.reshape(16, 8, 256), axis=0)
                top = part if top is None else jnp.maximum(top, part)
            tops[t] = jnp.max(top, axis=0, keepdims=True)

        def weigh(t):
            r, hp = items[t]
            cols = slice(hp * 256, hp * 256 + 256)
            for i in range(4):
                rows = slice(i * 128, (i + 1) * 128)
                probs[sx, r, rows, cols] = jnp.exp(s_ref[t % 3, rows, :] - tops[t]).astype(BF)

        def attend(t):
            r, hp = items[t]
            cols = slice(hp * 256, hp * 256 + 256)
            a = nn(vt_ref[r, hp * 80 : hp * 80 + 80, :], probs[sx, r, :, cols])
            for j in range(2):
                h = hp * 2 + j
                lanes = slice(j * 128, (j + 1) * 128)
                m_st[sx, r, h : h + 1, :] = tops[t][:, lanes]
                l_st[sx, r, h : h + 1, :] = a[64:65, lanes]
                a_st[sx, r, h * 32 : (h + 1) * 32, :] = a[j * 32 : (j + 1) * 32, lanes]

        for t in range(8):
            if t < 6:
                score(t)
            if 1 <= t < 7:
                weigh(t - 1)
            if t >= 2:
                attend(t - 2)

        @pl.when(u == 6)
        def _():
            for r in range(ROWS):
                att_tx[r] = combine(1 - yh, r).astype(BF)
            att_copy.start()
            st_copy.start()

        return carry

    lax.fori_loop(0, 8, forward, 0)

    for r in range(ROWS):
        att_loc[yh * ROWS + r] = combine(yh, r)
    att_copy.wait_recv()
    st_copy.wait_recv()
    for r in range(ROWS):
        mine = yh * ROWS + r
        ma, la = st_loc[mine, 0:4, :], st_loc[mine, 4:8, :]
        mb, lb = st_rx[r, 0:4, :], st_rx[r, 4:8, :]
        top_m = jnp.maximum(ma, mb)
        fa, fb = jnp.exp(ma - top_m), jnp.exp(mb - top_m)
        total = fa * la + fb * lb
        attended = (per_head(fa) * att_loc[mine] + per_head(fb) * att_rx[r].astype(F32)) / per_head(total)
        gate = gates[r]
        product = dot[mine].astype(F32) * attended
        lse = top_m + jnp.log(total)
        stats[mine, 0:4, :] = lse
        back_tx[r, 0:4, :] = lse
        for h in range(HEADS):
            delta = jnp.sum(product[h * 32 : (h + 1) * 32, :], axis=0, keepdims=True)
            stats[mine, 4 + h : 5 + h, :] = delta
            back_tx[r, 4 + h : 5 + h, :] = delta
        att_loc[mine] = attended
    back_copy.start()
    rc(set_of(dot, yh), set_of(dot, 1 - yh), pq_s.at[1], pq_r.at[1], hpart).wait_recv()
    for r in range(ROWS):
        spread(dos, dot, (1 - yh) * ROWS + r)
        key_factors((1 - yh) * ROWS + r)
    back_copy.wait_recv()
    for r in range(ROWS):
        stats[(1 - yh) * ROWS + r] = back_rx[r]
    dq[...] = jnp.zeros_like(dq)

    def core_half(xb, cc):
        return pl.ds(pl.multiple_of(xb * KB + cc * 256, 256), 256)

    def z_part(zz):
        return pl.ds(pl.multiple_of(zz * 32, 32), 32)

    def core_copy(xb, p):
        rows = pl.ds(sides[p] * ROWS, ROWS)
        return rc(
            kt.at[rows, core_half(xb, 1 - c)], rxc.at[xb, rows], kc_s.at[xb, p], kc_r.at[xb, p], sib
        )

    def y_copy(xb, p):
        part = pl.ds(p * 128, 128)
        return rc(ytx.at[xb, :, part], rxy.at[xb, :, part], ky_s.at[xb, p], ky_r.at[xb, p], ypart)

    def z_copy(xb, i):
        return rc(
            ztx.at[xb, :, z_part(zs[i])], zrx.at[xb, i], zq_s.at[xb, i], zq_r.at[xb, i], dev(z_=zs[i])
        )

    def own_copy(xb):
        part = lax.rem(z, 4)
        return rc(
            htx.at[xb], frx.at[:, z_part(part)], f_s.at[xb], f_r.at[part],
            dev(yh_=yl, yl_=yh, z_=2 * xb + c, c_=z // 4),
        )

    def key_part(xb, p):
        return pl.ds(pl.multiple_of(xb * KB + c * 256 + p * 128, 128), 128)

    def y_stage(xb):
        core_copy(xb, 0).wait_recv()
        core_copy(xb, 1).wait_recv()
        for p in range(2):
            part = slice(p * 128, (p + 1) * 128)
            for r in range(ROWS):
                theirs = (1 - yl) * ROWS + r
                ytx[xb, r, part, :] = (
                    kt[theirs, key_part(xb, p), :].astype(F32) + rxc[xb, theirs, part, :].astype(F32)
                ).astype(BF)
            y_copy(xb, p).start()

    def z_stage(xb):
        for p in range(2):
            part = slice(p * 128, (p + 1) * 128)
            y_copy(xb, p).wait_recv()
            for r in range(ROWS):
                ours = yl * ROWS + r
                total = kt[ours, key_part(xb, p), :].astype(F32) + rxc[xb, ours, part, :].astype(F32)
                total = total + rxy[xb, r, part, :].astype(F32)
                rsum[xb, r, part, :] = total
                ztx[xb, r, part, :] = total.astype(BF)
            for i in (4, 3, 5, 2, 6, 1, 7):
                @pl.when(zs[i] // 4 == p)
                def _():
                    z_copy(xb, i).start()

    def home_stage(xb):
        total = rsum[xb, :, z_part(z), :]
        for i in range(1, 8):
            z_copy(xb, i).wait_recv()
            total = total + zrx[xb, i].astype(F32)
        htx[xb] = total.astype(BF)
        stays = jnp.logical_and(self_home, z // 2 == xb)

        @pl.when(stays)
        def _():
            frx[:, z_part(lax.rem(z, 4)), :] = htx[xb]

        @pl.when(jnp.logical_not(stays))
        def _():
            own_copy(xb).start()

    g_half_p = rc(gtx.at[0, pl.ds(0, 2)], grx.at[0, pl.ds(0, 2)], g_s.at[0], g_r.at[0], xp)
    g_half_m = rc(gtx.at[0, pl.ds(2, 2)], grx.at[0, pl.ds(2, 2)], g_s.at[1], g_r.at[1], xm)
    g_p = rc(gtx.at[1], grx.at[1], g_s.at[2], g_r.at[2], xp)
    g_m = rc(gtx.at[2], grx.at[2], g_s.at[3], g_r.at[3], xm)

    def bias_stage(step):
        if step == 1:
            g_half_p.wait_recv()
        if step == 2:
            g_half_m.wait_recv()
        if step == 3:
            g_p.wait_recv()
            g_m.wait_recv()
        for h in range(HEADS):
            for k in range(4):
                lanes = slice(k * 128, (k + 1) * 128)
                tile = turned[h, :, lanes]
                if (step == 1 and h < 2) or (step == 2 and h >= 2):
                    tile = tile + grx[0, h, :, lanes].astype(F32)
                if step == 3:
                    tile = tile + grx[1, h, :, lanes].astype(F32) + grx[2, h, :, lanes].astype(F32)
                    bias_grad[h, :, lanes] = tile.astype(BF)
                else:
                    gtx[step, h, :, lanes] = tile.astype(BF)
        if step == 0:
            g_half_p.start()
            g_half_m.start()
        if step == 1:
            g_p.start()
        if step == 2:
            g_m.start()

    def backward(step, carry):
        xb = lax.rem(x + jnp.where(step == 0, 2, jnp.where(step == 1, 1, jnp.where(step == 2, 3, 0))), NX)
        places, factors, deltas = [], [], []
        for q in range(2 * ROWS):
            side = yh if q < ROWS else 1 - yh
            sx, r, row = side * 4 + xb, q % ROWS, side * ROWS + q % ROWS
            places.append((q, sx, r, row))
            st = stats[row]
            f, delta = jnp.exp(m_st[sx, r] - st[0:4, :]), st[4:8, :]
            factors.append([jnp.concatenate([f[h : h + 1, :], f[h + 1 : h + 2, :]], axis=1) for h in (0, 2)])
            deltas.append([jnp.concatenate([delta[h : h + 1, :], delta[h + 1 : h + 2, :]], axis=1) for h in (0, 2)])
        for hp in range(2):
            cols = slice(hp * 256, hp * 256 + 256)
            p_cols = slice(512 + hp * 256, 768 + hp * 256)
            for i in range(4):
                rows = slice(i * 128, (i + 1) * 128)
                total = None
                for q, sx, r, row in places:
                    d_prob = nn(vals[sx, r, rows, :], dos[row, :, cols]) - deltas[q][hp]
                    prob = probs[sx, r, rows, cols].astype(F32) * factors[q][hp]
                    d_score = prob * d_prob
                    total = d_score if total is None else total + d_score
                    ds_ref[q, rows, cols] = d_score.astype(BF)
                    ds_ref[q, rows, p_cols] = prob.astype(BF)
                for j in range(2):
                    turned[hp * 2 + j, :, rows] = total[:, j * 128 : (j + 1) * 128].T
            for q, sx, r, row in places:
                d_query = nn(keys_t[sx, r, hp * 64 : hp * 64 + 64, :], ds_ref[q, :, cols])
                for j in range(2):
                    rows = slice((hp * 2 + j) * 32, (hp * 2 + j + 1) * 32)
                    dq[q, rows, :] = dq[q, rows, :] + d_query[j * 32 : (j + 1) * 32, j * 128 : (j + 1) * 128]
        for q, sx, r, row in places:
            for i in range(2):
                rows = slice(i * 256, (i + 1) * 256)
                kt[row, pl.ds(pl.multiple_of(xb * KB + i * 256, 256), 256), :] = nn(
                    ds_ref[q, rows, :], g_n[row]
                ).astype(BF)
            if r == ROWS - 1:
                core_copy(xb, q // ROWS).start()

        def block_at(back):
            return lax.rem(x + jnp.where(step == back, 2, jnp.where(step == back + 1, 1, 3)), NX)

        for s in range(3):
            @pl.when(step == s)
            def _():
                bias_stage(s)

        @pl.when(step >= 1)
        def _():
            z_stage(block_at(1))

        @pl.when(step >= 2)
        def _():
            home_stage(block_at(2))

        y_stage(xb)
        return carry

    lax.fori_loop(0, 4, backward, 0)

    for r in range(ROWS):
        dqtx[r] = dq[ROWS + r].astype(BF)
    dq_copy = rc(dqtx, dqrx, f_s.at[4], f_r.at[4], hpart)
    dq_copy.start()
    z_stage(x)
    for r in range(ROWS):
        attended = att_loc[yh * ROWS + r]
        gate = gates[r]
        dgp[r] = dgated[r] * attended * gate * (1.0 - gate)
        update[r] = nn(wot[...], (gate * attended).astype(BF)).T.astype(BF)
    update_out = pltpu.make_async_copy(update, update_hbm, o_s.at[0])
    update_out.start()
    home_stage(xs[3])
    dq_copy.wait_recv()
    for r in range(ROWS):
        d_query = (dq[r] + dqrx[r].astype(F32)) * (DH ** -0.5)
        unit_t = split_nn(w[:, 0:128], d_query) + split_nn(w[:, 384:512], dgp[r])
        dgated[r] = unit_t.T
    home_stage(x)
    bias_stage(3)
    bias_out = pltpu.make_async_copy(bias_grad, bias_hbm, o_s.at[1])
    bias_out.start()
    for j in range(4):
        @pl.when(jnp.logical_not(jnp.logical_and(self_home, lax.rem(z, 4) == j)))
        def _():
            rc(htx.at[0], frx.at[:, pl.ds(j * 32, 32)], f_s.at[0], f_r.at[j], sib).wait_recv()
    for r in range(ROWS):
        dgated[r] = dgated[r] + frx[r].astype(F32)
    normed_out = pltpu.make_async_copy(dgated, normed_hbm, o_s.at[2])
    normed_out.start()

    for copy in (bias_p, bias_m, bias_fp, bias_fm, q_send, d_send, att_copy, st_copy, back_copy, dq_copy,
                 g_half_p, g_half_m, g_p, g_m):
        copy.wait_send()
    for t in range(2):
        @pl.when(jnp.logical_not(jnp.logical_and(is_home, yl == t)))
        def _():
            key_send[t].wait_send()
    for i in range(4):
        for p in range(2):
            if goes_up(i, p):
                up(i, p).wait_send()
            if goes_down(i, p):
                down(i, p).wait_send()
        core_copy(i, 0).wait_send()
        core_copy(i, 1).wait_send()
        y_copy(i, 0).wait_send()
        y_copy(i, 1).wait_send()
        for j in range(1, 8):
            z_copy(i, j).wait_send()

        @pl.when(jnp.logical_not(jnp.logical_and(self_home, z // 2 == i)))
        def _():
            own_copy(i).wait_send()

    for i in range(8):
        to_sib(i).wait_send()

    update_out.wait()
    bias_out.wait()
    normed_out.wait()


def shards(codes, expo, tok, gain, w, wo, bias, ug):
    vm = pltpu.VMEM
    dma = pltpu.SemaphoreType.DMA
    blk = (ROWS, T, C)
    scratch = [
        vm(blk, BF), vm((HEADS, T, KB), BF),
        vm((512, C), BF), vm((C, C), BF), vm(blk, BF), vm(blk, F32), vm(blk, F32),
        vm((6, 2048, C), BF), vm((6, C, T), BF), vm((6, C, T), BF), vm((3, HEADS, T, KB), BF),
        vm((4, KB, 512), F32), vm((8, 3, KB, 512), BF), vm((3, KB, 256), F32), vm((6, C, 512), BF),
        vm((6, C, 512), BF),
        vm((8, 3, HEADS, T), F32), vm((8, 3, HEADS, T), F32), vm((8, 3, C, T), F32),
        vm((8, 3, KB, C), BF), vm((8, 3, C, KB), BF), vm((6, 1024, C), BF), vm((6, C, T), F32), vm((6, 8, T), F32),
        vm(blk, BF), vm(blk, BF), vm((ROWS, 8, T), F32), vm((ROWS, 8, T), F32), vm((ROWS, 8, T), F32),
        vm((6, 8, T), F32), vm(blk, F32),
        vm((6, KB, 1024), BF), vm((3, KB, C), BF), vm((3, 160, KB), BF),
        vm((HEADS, T, KB), F32),
        vm((6, C, T), F32), vm((6, 2048, C), BF),
        vm((4, 6, 256, C), BF), vm((4, 3, 256, C), BF), vm((4, 3, 256, C), BF), vm((4, 3, 256, C), F32),
        vm((4, 3, 256, C), BF), vm((4, 8, 3, 32, C), BF), vm((4, 3, 32, C), BF), vm(blk, BF), vm(blk, BF), vm(blk, BF),
        vm((3, HEADS, T, KB), BF), vm((3, HEADS, T, KB), BF),
        dma((4,)), dma((4,)), dma((2,)), dma((2,)), dma((2, 4, 2)), dma((2, 4, 2)), dma((8,)), dma((8,)),
        dma((2,)), dma((2,)), dma((3,)), dma((3,)), dma((4, 2)), dma((4, 2)), dma((4, 2)), dma((4, 2)),
        dma((4, 8)), dma((4, 8)), dma((5,)), dma((5,)), dma((4,)), dma((4,)), dma((3,)),
    ]
    v = pl.BlockSpec(memory_space=pltpu.VMEM)
    hbm = pl.BlockSpec(memory_space=pl.ANY)
    shapes = (
        jax.ShapeDtypeStruct(blk, BF),
        jax.ShapeDtypeStruct(blk, F32),
        jax.ShapeDtypeStruct((HEADS, T, KB), BF),
    )
    gain, expo = gain.reshape(1, C), expo.reshape(1, ROWS)
    update, d_normed, bias_grad = pl.pallas_call(
        kernel,
        out_shape=shapes,
        in_specs=[v] * 8,
        out_specs=(hbm, hbm, hbm),
        scratch_shapes=scratch,
        compiler_params=pltpu.CompilerParams(
            collective_id=0, has_side_effects=True, vmem_limit_bytes=60 * 1024 * 1024
        ),
        cost_estimate=pl.CostEstimate(flops=8_000_000_000, bytes_accessed=4_000_000, transcendentals=6_300_000),
    )(tok, codes, expo, gain, w, wo, bias, ug)
    return pl.pallas_call(
        norm_back,
        out_shape=(shapes[0], shapes[0], shapes[2]),
        in_specs=[v] * 6,
        out_specs=(v, v, v),
        compiler_params=pltpu.CompilerParams(vmem_limit_bytes=58 * 1024 * 1024),
    )(codes, expo, gain, d_normed, update, bias_grad)


def solution(mesh):
    in_specs = (
        P("row", "col", None), P("row", "col"), P(), P(), P(), P(), P(None, "col", "row"), P("row", "col", None),
    )
    out_specs = (P("row", "col", None), P("row", "col", None), P(None, "col", "row"))
    return jax.shard_map(shards, mesh=mesh, in_specs=in_specs, out_specs=out_specs, check_vma=False)
```
